128 devices in a mesh: bx: 16 (over z, y), by: 8 (over x, core).
Axes of the slice: x: 4, y: 4, z: 4, core: 2. Of those that a mesh axis runs over, the one named last changes fastest.
Arguments:
- vox_feats: bfloat16 [512, 8, 8, 512], P(('bx', 'by')), may hold values from -6 to 6
- block_coords: int32 [3, 512], P(None, ('bx', 'by')), may hold values from 0 to 95, as said below
- neighbors: int32 [27, 512], P(None, ('bx', 'by')), may hold values from -1 to 511, as said below
- conv_w: bfloat16 [3, 3, 3, 64, 64], replicated, may hold values from -0.15625 to 0.15625
- conv_b: float32 [64], replicated, may hold values from -3 to 3
- fold_w: bfloat16 [1024, 128], replicated, may hold values from -0.1875 to 0.1875
- fold_b: float32 [128], replicated, may hold values from -3 to 3
- map_w: bfloat16 [3, 3, 128, 128], replicated, may hold values from -0.1875 to 0.1875
- map_b: float32 [128], replicated, may hold values from -3 to 3
- cotangent: bfloat16 [768, 256, 128], P('bx', 'by'), may hold values from -6 to 6
Outputs:
- bev_map: bfloat16 [768, 256, 128], P('bx', 'by')
- feat_grad: float32 [512, 8, 8, 512], P(('bx', 'by'))
- conv_grads: float32 [3, 3, 3, 64, 64], replicated
- fold_grads: float32 [1024, 128], replicated
- map_grads: float32 [3, 3, 128, 128], replicated
The draws below stay inside these ranges and needn't reach their ends.
Inputs may be any that keep to these rules, and one draw needn't show every extreme that they name: Row 0 of block_coords is a block's row of blocks (0 to 95), row 1 its column of blocks (0 to 31), row 2 its height block (0 or 1: height levels 8 h to 8 h + 7 of 16). The blocks at positions g * 32 to (g + 1) * 32 - 1 all lie in rows of blocks g * 6 to (g + 1) * 6 - 1. No two blocks share coordinates. `neighbors`: entry 9 (dx + 1) + 3 (dy + 1) + dz + 1 of a block's column is the position of the active block at block offset (dx, dy, dz), or -1 where there is none; entry 13 is the block itself. A neighbour of a block of positions g * 32 to (g + 1) * 32 - 1 lies at positions (g - 1) * 32 to (g + 2) * 32 - 1.
All inputs are finite; a program needn't handle non-finite values.
Results may differ from the reference program's by a relative error of at most 0.015.
Values may be sent and summed in bfloat16 or wider, within the bound.
A program may use at most 192 MiB of HBM per device.

```python
import jax
import jax.numpy as jnp
from jax import lax

C = 64
BS = 8
BC = 128
NB_DEV = 4
TR = 6
TC = 4
FOLD = 1024
NB_TOTAL = 512
HB = 96
WB = 32
ROWS = 768
COLS = 256
N_BX = 16
N_BY = 8


def block_layout(key):
    groups = N_BX
    group_size = NB_DEV * N_BY
    squares = group_size // 8
    slot_rows = TR // 2
    slot_cols = TC * N_BY // 2
    inner_slots = (slot_rows - 2) * slot_cols
    border = jax.random.randint(jax.random.fold_in(key, 11), (groups + 1,), 0, slot_cols).astype(jnp.int32)
    within = jnp.arange(8, dtype=jnp.int32)
    step_row = within // 4
    step_col = within // 2 % 2
    step_high = within % 2

    def one_group(group_id):
        group_key = jax.random.fold_in(jax.random.fold_in(key, 12), group_id)
        slot_order = jax.random.permutation(group_key, inner_slots)[:squares].astype(jnp.int32)
        upper_col = jnp.where(group_id == groups - 1, slot_cols - 1, border[group_id + 1]).astype(jnp.int32)
        cand_row = jnp.concatenate([jnp.array([0, slot_rows - 1], jnp.int32), 1 + slot_order // slot_cols])
        cand_col = jnp.concatenate([jnp.stack([border[group_id], upper_col]), slot_order % slot_cols])
        usable = jnp.concatenate([jnp.stack([group_id > 0, group_id >= 0]), jnp.ones((squares,), bool)]).astype(jnp.int32)
        slot_rank = jnp.cumsum(usable) - 1
        picked = ((slot_rank[None, :] == jnp.arange(squares)[:, None]) & (usable[None, :] == 1)).astype(jnp.int32)
        square_row = jnp.sum(picked * cand_row[None, :], 1)
        square_col = jnp.sum(picked * cand_col[None, :], 1)
        row_ids = group_id * TR + 2 * square_row[:, None] + step_row[None, :]
        col_ids = 2 * square_col[:, None] + step_col[None, :]
        height_ids = jnp.zeros_like(row_ids) + step_high[None, :]
        shuffle = jax.random.permutation(jax.random.fold_in(group_key, 1), group_size)
        return (row_ids.reshape(-1)[shuffle], col_ids.reshape(-1)[shuffle], height_ids.reshape(-1)[shuffle])
    row_ids, col_ids, height_ids = jax.vmap(one_group)(jnp.arange(groups, dtype=jnp.int32))
    return (row_ids.reshape(-1).astype(jnp.int32), col_ids.reshape(-1).astype(jnp.int32), height_ids.reshape(-1).astype(jnp.int32))


def draw_block_coords(key, part):
    row_ids, col_ids, height_ids = block_layout(key)
    return jnp.stack([row_ids, col_ids, height_ids]).astype(jnp.int32)


def draw_neighbors(key, part):
    row_ids, col_ids, height_ids = block_layout(key)
    map_width = TC * N_BY
    block_total = row_ids.shape[0]
    keys_flat = (row_ids * map_width + col_ids) * 2 + height_ids
    offsets = jnp.arange(27, dtype=jnp.int32)
    shift_x = offsets // 9 - 1
    shift_y = offsets // 3 % 3 - 1
    shift_z = offsets % 3 - 1
    want_row = row_ids[None, :] + shift_x[:, None]
    want_col = col_ids[None, :] + shift_y[:, None]
    want_high = height_ids[None, :] + shift_z[:, None]
    valid = (want_row >= 0) & (want_row < N_BX * TR) & (want_col >= 0) & (want_col < map_width) & (want_high >= 0) & (want_high < 2)
    wanted = jnp.where(valid, (want_row * map_width + want_col) * 2 + want_high, -7)
    matched = (wanted[:, :, None] == keys_flat[None, None, :]).astype(jnp.int32)
    positions = jnp.arange(block_total, dtype=jnp.int32) + 1
    return (jnp.sum(matched * positions[None, None, :], 2) - 1).astype(jnp.int32)


def steps_of(own_key, shape, shards, least, largest):
    factor_of = 1.0
    for axis_at, parts in shards:
        steps = jax.random.uniform(jax.random.fold_in(jax.random.fold_in(own_key, 6), axis_at), (parts,), jnp.float32, least / len(shards), largest / len(shards))
        factor_of = factor_of * jnp.repeat(jnp.exp(steps), shape[axis_at] // parts).reshape((-1,) + (1,) * (len(shape) - 1 - axis_at))
    return factor_of


def centred(own_key, dims, width, limit, cuts=(), held_as=jnp.bfloat16):
    gain = steps_of(own_key, dims, cuts, -0.22, 0.18) if cuts else 1.0
    values = jax.random.normal(own_key, dims, jnp.float32) * width * gain
    return jnp.minimum(jnp.maximum(values, -limit), limit).astype(held_as)


def setup_inputs(seed: int = 0) -> dict:
    arg_keys = jax.random.split(jax.random.key(seed), 11)
    return {
        "vox_feats": centred(arg_keys[0], (NB_TOTAL, BS, BS, BS * C), 1.0, 6.0, ((0, 128),)),
        "block_coords": draw_block_coords(jax.random.fold_in(arg_keys[10], 71), 0),
        "neighbors": draw_neighbors(jax.random.fold_in(arg_keys[10], 71), 0),
        "conv_w": centred(arg_keys[3], (3, 3, 3, C, C), (27 * C) ** -0.5, 0.15625),
        "conv_b": centred(arg_keys[4], (C,), 0.5, 3.0, (), jnp.float32),
        "fold_w": centred(arg_keys[5], (FOLD, BC), FOLD ** -0.5, 0.1875),
        "fold_b": centred(arg_keys[6], (BC,), 0.5, 3.0, (), jnp.float32),
        "map_w": centred(arg_keys[7], (3, 3, BC, BC), (9 * BC) ** -0.5, 0.1875),
        "map_b": centred(arg_keys[8], (BC,), 0.5, 3.0, (), jnp.float32),
        "cotangent": centred(arg_keys[9], (ROWS, COLS, BC), 1.0, 6.0, ((0, 16), (1, 8))),
    }


highest = lax.Precision.HIGHEST

def smooth_slope(pre_act):
    logistic = jax.nn.sigmoid(pre_act)
    return logistic * (1.0 + pre_act * (1.0 - logistic))

def gather_tiles(block_pool, places):
    nearby = block_pool[places]
    rim_cuts = (slice(BS - 1, BS), slice(0, BS), slice(0, 1))
    planes = []
    for along_x in range(3):
        strips = []
        for along_y in range(3):
            pieces = [nearby[:, along_x * 9 + along_y * 3 + along_z, rim_cuts[along_x], rim_cuts[along_y], rim_cuts[along_z]] for along_z in range(3)]
            strips.append(jnp.concatenate(pieces, 3))
        planes.append(jnp.concatenate(strips, 2))
    return jnp.concatenate(planes, 1)

def conv_three(tiles, kernel):
    return lax.conv_general_dilated(tiles.astype(jnp.float32), kernel.astype(jnp.float32), (1, 1, 1), 'VALID', dimension_numbers=('NDHWC', 'DHWIO', 'NDHWC'), precision=highest)

def kernel_grad(tiles, upstream):
    tile_values = tiles.astype(jnp.float32)
    upstream_f = upstream.astype(jnp.float32)
    pieces = []
    for along_x in range(3):
        for along_y in range(3):
            for along_z in range(3):
                window = tile_values[:, along_x:along_x + BS, along_y:along_y + BS, along_z:along_z + BS]
                pieces.append(jnp.einsum('nxyzi,nxyzo->io', window, upstream_f, precision=highest))
    return jnp.stack(pieces).reshape(3, 3, 3, tiles.shape[4], upstream.shape[4])

def plane_conv(plane_in, kernel):
    return lax.conv_general_dilated(plane_in[None], kernel, (1, 1), 'SAME', dimension_numbers=('NHWC', 'HWIO', 'NHWC'), precision=highest)[0]

def reference(vox_feats, block_coords, neighbors, conv_w, conv_b, fold_w, fold_b, map_w, map_b, cotangent):
    channels = conv_w.shape[3]
    mapped = map_w.shape[3]
    block_count = vox_feats.shape[0]
    group_size = block_count // N_BX
    cell_count = BS * BS
    flat_in = BS * channels
    blocks = vox_feats.reshape(block_count, BS, BS, BS, channels)
    places = jnp.where(neighbors < 0, block_count, neighbors).T.astype(jnp.int32).reshape(N_BX, group_size, 27)
    zero_block = jnp.zeros((1, BS, BS, BS, channels), jnp.bfloat16)
    block_pool = jnp.concatenate([blocks, zero_block], 0)

    def forward_group(place_rows):
        return conv_three(gather_tiles(block_pool, place_rows), conv_w) + conv_b
    conv_pre = lax.map(forward_group, places).reshape(block_count, cell_count, flat_in)
    active = jax.nn.silu(conv_pre).astype(jnp.bfloat16)
    chosen_w = fold_w.reshape(2, flat_in, mapped)[block_coords[2]]
    partial_value = jnp.einsum('bcf,bfo->bco', active.astype(jnp.float32), chosen_w.astype(jnp.float32), precision=highest)
    column = (block_coords[0] * WB + block_coords[1]).astype(jnp.int32)
    fold_cols = jax.ops.segment_sum(partial_value, column, num_segments=HB * WB) + fold_b
    fold_pre = fold_cols.reshape(HB, WB, BS, BS, mapped).transpose(0, 2, 1, 3, 4).reshape(ROWS, COLS, mapped)
    mid_map = jax.nn.silu(fold_pre).astype(jnp.bfloat16)
    out_pre = plane_conv(mid_map.astype(jnp.float32), map_w.astype(jnp.float32)) + map_b
    bev_map = jax.nn.silu(out_pre).astype(jnp.bfloat16)
    grad_out = (cotangent.astype(jnp.float32) * smooth_slope(out_pre)).astype(jnp.bfloat16)
    unused_out, pullback = jax.vjp(plane_conv, mid_map.astype(jnp.float32), map_w.astype(jnp.float32))
    mid_grad, map_grads = pullback(grad_out.astype(jnp.float32))
    fold_grad = (mid_grad * smooth_slope(fold_pre)).astype(jnp.bfloat16)
    grad_cols = fold_grad.reshape(HB, BS, WB, BS, mapped).transpose(0, 2, 1, 3, 4).reshape(HB * WB, cell_count, mapped)
    owner_grad = grad_cols[column].astype(jnp.float32)
    act_grad = jnp.einsum('bco,bfo->bcf', owner_grad, chosen_w.astype(jnp.float32), precision=highest).astype(jnp.bfloat16)
    per_block = jnp.einsum('bcf,bco->bfo', active.astype(jnp.float32), owner_grad, precision=highest)
    height_hot = (block_coords[2][:, None] == jnp.arange(2)[None, :]).astype(jnp.float32)
    fold_grads = jnp.einsum('bz,bfo->zfo', height_hot, per_block, precision=highest).reshape(2 * flat_in, mapped)
    pre_grad = (act_grad.astype(jnp.float32) * smooth_slope(conv_pre)).astype(jnp.bfloat16)
    grad_blocks = pre_grad.reshape(block_count, BS, BS, BS, channels)
    grad_pool = jnp.concatenate([grad_blocks, zero_block], 0)
    flipped = conv_w[::-1, ::-1, ::-1].swapaxes(3, 4)
    grad_groups = grad_blocks.reshape(N_BX, group_size, BS, BS, BS, channels)

    def backward_group(inputs):
        place_rows, upstream = inputs
        conv_part = kernel_grad(gather_tiles(block_pool, place_rows), upstream)
        feat_part = conv_three(gather_tiles(grad_pool, place_rows), flipped)
        return (conv_part, feat_part)
    conv_parts, feat_grad = lax.map(backward_group, (places, grad_groups))
    return (bev_map, feat_grad.reshape(block_count, BS, BS, flat_in), lax.optimization_barrier(jnp.sum(conv_parts, 0)), fold_grads, map_grads)
```

```python
import functools

import jax
import jax.numpy as jnp
from jax import lax
from jax.experimental import pallas as pl
from jax.experimental.pallas import tpu as pltpu
from jax.sharding import PartitionSpec as P

MESH = pl.DeviceIdType.MESH
BF = jnp.bfloat16
F32 = jnp.float32
BS = 8
TR = 6
TC = 4
NB = 4
NX = 16
NY = 8
GROUP = NB * NY
ROWS = TR * BS
COLS = TC * BS
VMEM = pl.BlockSpec(memory_space=pltpu.VMEM)
SMEM = pl.BlockSpec(memory_space=pltpu.SMEM)
DMA = pltpu.SemaphoreType.DMA
CAT = 3072
CHUNK = CAT // NY
SLICE = CHUNK // NX


def place():
    return lax.axis_index("bx"), lax.axis_index("by")


def remote(src, dst, send, recv, device):
    return pltpu.make_async_remote_copy(
        src_ref=src,
        dst_ref=dst,
        send_sem=send,
        recv_sem=recv,
        device_id=device,
        device_id_type=MESH,
    )


def signal(device):
    pl.semaphore_signal(
        pltpu.get_barrier_semaphore(), inc=1, device_id=device, device_id_type=MESH
    )


def slope(pre):
    s = jax.nn.sigmoid(pre)
    return s * (1.0 + pre * (1.0 - s))


def rounded(v):
    return v.astype(BF).astype(F32)


def group_barrier():
    bx, by = place()
    core = by % 2
    for k in range(1, NY):
        signal((bx, (by + k) % NY))
    prev = bx > 0
    after = bx < NX - 1

    @pl.when(prev)
    def _():
        for j in range(NY // 2):
            signal((bx - 1, core + 2 * j))

    @pl.when(after)
    def _():
        for j in range(NY // 2):
            signal((bx + 1, core + 2 * j))

    count = NY - 1 + 4 * prev.astype(jnp.int32) + 4 * after.astype(jnp.int32)
    pl.semaphore_wait(pltpu.get_barrier_semaphore(), count)


def pack_faces(cur, msg, coords):
    lane = lax.broadcasted_iota(jnp.int32, (32, 128), 1)

    def flat(v):
        return jnp.concatenate([v[:, t * 128 : (t + 1) * 128] for t in range(4)], 0)

    def one(n, carry):
        high = coords[2, n].astype(F32)
        msg[n, 0] = flat(cur[0, n]).astype(BF)
        msg[n, 1] = flat(cur[7, n]).astype(BF)
        msg[n, 2] = flat(cur[:, n, 0, :]).astype(BF)
        msg[n, 3] = flat(cur[:, n, 7, :]).astype(BF)
        top = cur[:, n, :, 384:512].reshape(64, 128)
        low = cur[:, n, :, 0:128].reshape(64, 128)
        face = pltpu.roll(top, 64, 1) * (1.0 - high) + low * high
        msg[n, 4] = jnp.where(lane < 64, face[0:32], pltpu.roll(face[32:64], 64, 1)).astype(BF)
        return carry

    lax.fori_loop(0, NB, one, 0)


class Faces:
    def __init__(self, msg, pool, side, own_s, fwd_s, side_s, sfwd_s, own_r, side_r):
        self.msg, self.pool, self.side = msg, pool, side
        self.own_s, self.fwd_s, self.side_s, self.sfwd_s = own_s, fwd_s, side_s, sfwd_s
        self.own_r, self.side_r = own_r, side_r
        self.bx, self.by = place()
        self.core = self.by % 2
        self.mate = self.by + 1 - 2 * self.core

    def first(self):
        bx, by = self.bx, self.by
        mine = pl.ds(by * NB, NB)
        out = [
            remote(self.msg, self.pool.at[mine], self.own_s.at[k], self.own_r.at[by], (bx, peer))
            for k, peer in enumerate([self.mate] + [(by + 2 * k) % NY for k in (1, 2, 3)])
        ]
        return out

    def sides(self, to):
        bx, by = self.bx, self.by
        mine = pl.ds(by * NB, NB)
        part, step = ((1, 1), (0, -1))[to]
        return [
            remote(
                self.msg.at[:, part],
                self.side.at[to, mine],
                self.side_s.at[to, j],
                self.side_r.at[to, by],
                (bx + step, self.core + 2 * j),
            )
            for j in range(4)
        ]

    def has(self, to):
        return (self.bx > 0, self.bx < NX - 1)[to]

    def sends(self, to):
        return self.has(1 - to)

    def start(self):
        for c in self.first():
            c.start()
        for to in range(2):

            @pl.when(self.sends(to))
            def _(to=to):
                for c in self.sides(to):
                    c.start()

        self.pool[pl.ds(self.by * NB, NB)] = self.msg[...]

    def own_landed(self, src, k):
        at = self.pool.at[pl.ds(src * NB, NB)]
        return remote(at, at, self.fwd_s.at[k], self.own_r.at[src], (self.bx, self.mate))

    def side_landed(self, to, src, j):
        at = self.side.at[to, pl.ds(src * NB, NB)]
        return remote(at, at, self.sfwd_s.at[to, j], self.side_r.at[to, src], (self.bx, self.mate))

    def forward(self):
        for k in (1, 3, 2):
            c = self.own_landed((self.by + 2 * k) % NY, k - 1)
            c.wait_recv()
            c.start()
        for to in range(2):

            @pl.when(self.has(to))
            def _(to=to):
                for j in range(4):
                    c = self.side_landed(to, self.core + 2 * j, j)
                    c.wait_recv()
                    c.start()

    def finish(self):
        for k in range(4):
            self.own_landed((self.mate + 2 * k) % NY, 0).wait_recv()
        for to in range(2):

            @pl.when(self.has(to))
            def _(to=to):
                for j in range(4):
                    self.side_landed(to, 1 - self.core + 2 * j, j).wait_recv()

    def drain(self):
        for c in self.first():
            c.wait_send()
        for k in (1, 2, 3):
            self.own_landed((self.by + 2 * k) % NY, k - 1).wait_send()
        for to in range(2):

            @pl.when(self.sends(to))
            def _(to=to):
                for c in self.sides(to):
                    c.wait_send()

            @pl.when(self.has(to))
            def _(to=to):
                for j in range(4):
                    self.side_landed(to, self.core + 2 * j, j).wait_send()


FACE_SCRATCH = [
    pltpu.VMEM((NB, 5, 32, 128), BF),
    pltpu.VMEM((GROUP + 1, 5, 32, 128), BF),
    pltpu.VMEM((2, GROUP + 1, 32, 128), BF),
    DMA((4,)),
    DMA((3,)),
    DMA((2, 4)),
    DMA((2, 4)),
    DMA((NY,)),
    DMA((2, NY)),
]


def assemble(cur, pool, side, own_at, side_at, shifted, edge):
    low = lax.broadcasted_iota(jnp.int32, (8, 128), 1) < 64
    sub = lax.broadcasted_iota(jnp.int32, (8, 128), 0)

    def one(n, carry):
        def face(part, k):
            return pool[own_at[k, n], part].astype(F32)

        def xface(dx, k):
            near = face(1 if dx < 0 else 0, k)
            return near + side[0 if dx < 0 else 1, side_at[k, n]].astype(F32)

        def tiles(v):
            return [v[t * 8 : (t + 1) * 8] for t in range(4)]

        def turn(v):
            return pltpu.roll(v, 64, 1)

        def padz(core, before, after):
            r = [turn(t) for t in core]
            return (
                [jnp.where(low, before, r[0])]
                + [jnp.where(low, r[t - 1], r[t]) for t in (1, 2, 3)]
                + [jnp.where(low, r[3], after)]
            )

        def put(x, t, mid, above, below):
            row = pl.multiple_of((x * NB + n) * 8, 8)
            at = (pl.ds(row, 8), pl.ds(t * 128, 128))
            shifted[(1, *at)] = mid
            shifted[(0, *at)] = jnp.where(sub == 0, above, pltpu.roll(mid, 1, 0))
            shifted[(2, *at)] = jnp.where(sub == 7, below, pltpu.roll(mid, 7, 0))

        for x, dx in ((0, -1), (9, 1)):
            z = []
            for dy in range(3):
                k = 9 * (dx + 1) + 3 * dy
                z.append(
                    padz(tiles(xface(dx, k + 1)), turn(xface(dx, k)[24:32]), turn(xface(dx, k + 2)[0:8]))
                )
            for t in range(5):
                put(x, t, z[1][t], pltpu.roll(z[0][t], 1, 0), pltpu.roll(z[2][t], 7, 0))
        for i, (k, part) in enumerate(((9, 3), (15, 2))):
            z = padz(tiles(face(part, k + 1)), turn(face(part, k)[24:32]), turn(face(part, k + 2)[0:8]))
            for t in range(5):
                edge[i, :, t * 128 : (t + 1) * 128] = z[t]
        under = face(4, 12)
        over = face(4, 14)
        for x in range(BS):
            at = slice(x % 4 * 8, x % 4 * 8 + 8)
            before = under[at] if x < 4 else turn(under[at])
            after = turn(over[at]) if x < 4 else over[at]
            z = padz([cur[x, n, :, t * 128 : (t + 1) * 128] for t in range(4)], before, after)
            for t in range(5):
                lanes = slice(t * 128, (t + 1) * 128)
                put(x + 1, t, z[t], edge[0, x : x + 1, lanes], edge[1, x : x + 1, lanes])
        return carry

    lax.fori_loop(0, NB, one, 0)


def owner_forward(
    vox, conv_w, conv_b, fold_w, coord_tile, coords, own_at, side_at,
    pre_out, act_out, wide_out, part_out, coords_out,
    cur, shifted, edge, toep, fold_both, part,
    msg, pool, side, own_s, fwd_s, side_s, sfwd_s, own_r, side_r,
    part_s, part_r, coord_s, coord_r,
):
    bx, by = place()
    faces = Faces(msg, pool, side, own_s, fwd_s, side_s, sfwd_s, own_r, side_r)
    for n in range(NB):
        cur[:, n] = vox[n].astype(F32)
    pack_faces(cur, msg, coords)
    group_barrier()
    faces.start()
    tell = [
        remote(coord_tile, coords_out.at[by], coord_s.at[k], coord_r.at[by], (bx, (by + k) % NY))
        for k in range(1, NY)
    ]
    for c in tell:
        c.start()
    coords_out[by] = coord_tile[...]
    pool[GROUP] = jnp.zeros((5, 32, 128), BF)
    for to in range(2):
        side[to, GROUP] = jnp.zeros((32, 128), BF)
    blank = jnp.zeros((64, 64), F32)

    def build(tap, carry):
        w = [blank] + [conv_w[tap * 3 + k].astype(F32) for k in range(3)] + [blank]
        for z in range(4):
            toep[tap, z * 64 : (z + 1) * 64, :] = jnp.concatenate([w[z + 1], w[z]], 1).astype(BF)
        return carry

    lax.fori_loop(0, 9, build, 0)
    faces.forward()
    faces.finish()
    assemble(cur, pool, side, own_at, side_at, shifted, edge)
    for e in range(3):
        wide_out[:, e * 640 : (e + 1) * 640] = shifted[e].astype(BF)
    bias = conv_b[...]
    for group in range(4):
        total = bias
        for a in range(3):
            for e in range(3):
                lhs = wide_out[a * 32 : a * 32 + 256, e * 640 + group * 128 : e * 640 + group * 128 + 256]
                total = total + jnp.dot(lhs, toep[a * 3 + e], preferred_element_type=F32)
        lanes = slice(group * 128, (group + 1) * 128)
        pre_out[:, lanes] = total
        act_out[:, lanes] = (total * jax.nn.sigmoid(total)).astype(BF)
    both = jnp.concatenate(
        [
            jnp.dot(act_out[...], fold_w[h], preferred_element_type=F32) for h in range(2)
        ],
        1,
    )
    fold_both[...] = both.reshape(BS, NB, BS, 256)
    for n in range(NB):
        high = coords[2, n].astype(F32)
        one = fold_both[:, n, :, 0:128] * (1.0 - high) + fold_both[:, n, :, 128:256] * high
        part[n] = one.reshape(64, 128).astype(BF)
    mine = pl.ds(by * NB, NB)
    give = [
        remote(part, part_out.at[mine], part_s.at[k], part_r.at[by], (bx, (by + k) % NY))
        for k in range(1, NY)
    ]
    for c in give:
        c.start()
    part_out[mine] = part[...]
    for k in range(1, NY):
        src = (by + k) % NY
        remote(part, part_out.at[pl.ds(src * NB, NB)], part_s.at[k], part_r.at[src], (bx, src)).wait_recv()
        remote(coord_tile, coords_out.at[src], coord_s.at[k], coord_r.at[src], (bx, src)).wait_recv()
    for c in give + tell:
        c.wait_send()
    faces.drain()


NEAR = [(-1, 0), (1, 0), (0, -1), (0, 1), (-1, -1), (-1, 1), (1, -1), (1, 1)]


class Rim:
    def __init__(self, row_out, col_out, row_in, col_in, corner_in, send, recv):
        self.row_out, self.col_out = row_out, col_out
        self.row_in, self.col_in, self.corner_in = row_in, col_in, corner_in
        self.send, self.recv = send, recv
        self.bx, self.by = place()

    def exists(self, d):
        dx, dy = NEAR[d]
        ok = None
        for v, step, size in ((self.bx, dx, NX), (self.by, dy, NY)):
            if step:
                here = v > 0 if step < 0 else v < size - 1
                ok = here if ok is None else ok & here
        return ok

    def copy(self, d):
        dx, dy = NEAR[d]
        back = NEAR.index((-dx, -dy))
        if dy == 0:
            src, dst = self.row_out.at[d], self.row_in.at[back]
        elif dx == 0:
            src, dst = self.col_out.at[d - 2], self.col_in.at[back - 2]
        else:
            src = self.row_out.at[0 if dx < 0 else 1, pl.ds(0 if dy < 0 else 16, 16)]
            dst = self.corner_in.at[back - 4]
        return remote(src, dst, self.send.at[d], self.recv.at[back], (self.bx + dx, self.by + dy))

    def landing(self, d):
        dx, dy = NEAR[d]
        if dy == 0:
            return self.row_in.at[d]
        if dx == 0:
            return self.col_in.at[d - 2]
        return self.corner_in.at[d - 4]

    def start(self, plane):
        self.row_out[0] = plane[0].astype(BF)
        self.row_out[1] = plane[ROWS - 1].astype(BF)
        self.col_out[0] = plane[:, 0, :].astype(BF)
        self.col_out[1] = plane[:, COLS - 1, :].astype(BF)
        for d in range(8):

            @pl.when(self.exists(d))
            def _(d=d):
                self.copy(d).start()

            @pl.when(jnp.logical_not(self.exists(d)))
            def _(d=d):
                at = self.landing(d)
                at[...] = jnp.zeros(at.shape, BF)

    def finish(self):
        for d in range(8):

            @pl.when(self.exists(d))
            def _(d=d):
                dx, dy = NEAR[d]
                at = self.landing(d)
                remote(at, at, self.send.at[d], self.recv.at[d], (self.bx + dx, self.by + dy)).wait_recv()

    def drain(self):
        for d in range(8):

            @pl.when(self.exists(d))
            def _(d=d):
                self.copy(d).wait_send()


def spread(plane, rim, side32, out):
    side32[0] = rim.col_in[0].astype(F32)
    side32[1] = rim.col_in[1].astype(F32)
    j = lax.broadcasted_iota(jnp.int32, (COLS, 128), 0)

    def put(at, row, left, right):
        rows = pl.ds(pl.multiple_of(at * COLS, COLS), COLS)
        out[rows, 0:128] = jnp.where(j == 0, left, pltpu.roll(row, 1, 0)).astype(BF)
        out[rows, 128:256] = row.astype(BF)
        out[rows, 256:384] = jnp.where(j == COLS - 1, right, pltpu.roll(row, COLS - 1, 0)).astype(BF)

    def inner(i, carry):
        put(i + 1, plane[i], side32[0, pl.ds(i, 1), :], side32[1, pl.ds(i, 1), :])
        return carry

    lax.fori_loop(0, ROWS, inner, 0)
    corner = [rim.corner_in[c].astype(F32) for c in range(4)]
    put(0, rim.row_in[0].astype(F32), corner[0][15:16], corner[1][0:1])
    put(ROWS + 1, rim.row_in[1].astype(F32), corner[2][15:16], corner[3][0:1])


def map_kernel(
    part, table, block_slot, cot, map_w, map_b, fold_b,
    bev_out, grads_out, back_out,
    fold, plane, gplane, spread_mid, spread_grad, flat_grad, side32, slots, ready,
    row_out, col_out, row_in, col_in, corner_in, send, recv,
    back_s, back_r,
):
    bx, by = place()
    rims = [
        Rim(row_out.at[p], col_out.at[p], row_in.at[p], col_in.at[p], corner_in.at[p], send.at[p], recv.at[p])
        for p in range(2)
    ]
    for k in range(1, NY):
        signal((bx, (by + k) % NY))
    count = jnp.int32(NY - 1)
    for d, (dx, dy) in enumerate(NEAR):
        if dx:

            @pl.when(rims[0].exists(d))
            def _(dx=dx, dy=dy):
                signal((bx + dx, by + dy))

            count = count + rims[0].exists(d).astype(jnp.int32)
    for r in range(TR):
        for c in range(TC):
            total = fold_b[...]
            for h in range(2):
                at = table[(r * TC + c) * 2 + h]
                here = (at < GROUP).astype(F32)
                total = total + part[jnp.minimum(at, GROUP - 1)].astype(F32) * here
            total = jnp.broadcast_to(total, (64, 128))
            where = (slice(r * BS, (r + 1) * BS), slice(c * BS, (c + 1) * BS))
            fold[where] = total.reshape(BS, BS, 128)
            plane[where] = rounded(total * jax.nn.sigmoid(total)).reshape(BS, BS, 128)
    pl.semaphore_wait(pltpu.get_barrier_semaphore(), count)
    rims[0].start(plane)
    rims[0].finish()
    spread(plane, rims[0], side32, spread_mid)

    def ahead(i, carry):
        start = pl.multiple_of(i * 256, 256)
        total = map_b[...]
        for a in range(3):
            lhs = spread_mid[pl.ds(start + a * COLS, 256), :]
            total = total + jnp.dot(lhs, map_w[a], preferred_element_type=F32)
        bev_out[pl.ds(i * BS, BS)] = (total * jax.nn.sigmoid(total)).reshape(BS, COLS, 128).astype(BF)
        g = cot[pl.ds(i * BS, BS)].astype(F32).reshape(256, 128) * slope(total)
        flat_grad[pl.ds(start, 256), :] = g.astype(BF)
        gplane[pl.ds(i * BS, BS)] = rounded(g).reshape(BS, COLS, 128)
        return carry

    lax.fori_loop(0, TR, ahead, 0)
    rims[1].start(gplane)
    turned = gplane[...].reshape(ROWS * COLS, 128).T.astype(BF)
    for a in range(3):
        got = jnp.dot(turned, spread_mid[a * COLS : a * COLS + ROWS * COLS, :], preferred_element_type=F32)
        for e in range(3):
            grads_out[a * 3 + e] = got[:, e * 128 : (e + 1) * 128].T
    rims[1].finish()
    spread(gplane, rims[1], side32, spread_grad)

    def behind(i, carry):
        start = pl.multiple_of(i * 256, 256)
        total = None
        for a in range(3):
            for e in range(3):
                lhs = spread_grad[pl.ds(start + a * COLS, 256), e * 128 : (e + 1) * 128]
                w = map_w[2 - a, (2 - e) * 128 : (3 - e) * 128, :]
                one = lax.dot_general(lhs, w, (((1,), (1,)), ((), ())), preferred_element_type=F32)
                total = one if total is None else total + one
        pre = fold[pl.ds(i * BS, BS)].reshape(256, 128)
        back = (total * slope(pre)).reshape(BS, COLS, 128)
        for c in range(TC):
            slots[i * TC + c] = back[:, c * BS : (c + 1) * BS, :].reshape(64, 128).astype(BF)
        return carry

    lax.fori_loop(0, TR, behind, 0)

    def fill(b, carry):
        ready[b] = slots[block_slot[b]]
        return carry

    lax.fori_loop(0, GROUP, fill, 0)
    give = []
    for k in range(1, NY):
        peer = (by + k) % NY
        give.append(
            remote(ready.at[pl.ds(peer * NB, NB)], back_out.at[by], back_s.at[k], back_r.at[by], (bx, peer))
        )
    for c in give:
        c.start()
    back_out[by] = ready[pl.ds(by * NB, NB)]
    for k in range(1, NY):
        src = (by + k) % NY
        remote(ready.at[pl.ds(0, NB)], back_out.at[src], back_s.at[k], back_r.at[src], (bx, src)).wait_recv()
    for c in give:
        c.wait_send()
    for rim in rims:
        rim.drain()


def owner_backward(
    pre, act, wide, back, conv_w, fold_w, coords, own_at, side_at,
    feat_out, conv_out, fold_out,
    cur, shifted, edge, toep, wide2, split, cur_bf,
    msg, pool, side, own_s, fwd_s, side_s, sfwd_s, own_r, side_r,
):
    faces = Faces(msg, pool, side, own_s, fwd_s, side_s, sfwd_s, own_r, side_r)
    for n in range(NB):
        high = coords[2, n].astype(F32)
        mine = back[coords[1, n] // TC, n].astype(F32).reshape(BS, BS, 128)
        split[:, n, :, 0:128] = mine * (1.0 - high)
        split[:, n, :, 128:256] = mine * high
    both = split[...].reshape(256, 256)
    act_grad = None
    for h in range(2):
        one = lax.dot_general(
            both[:, h * 128 : (h + 1) * 128].astype(BF), fold_w[h], (((1,), (1,)), ((), ())), preferred_element_type=F32
        )
        act_grad = one if act_grad is None else act_grad + one
    grad = rounded(rounded(act_grad) * slope(pre[...]))
    cur[...] = grad.reshape(BS, NB, BS, 512)
    cur_bf[...] = grad.astype(BF)
    pack_faces(cur, msg, coords)
    group_barrier()
    faces.start()
    pool[GROUP] = jnp.zeros((5, 32, 128), BF)
    for to in range(2):
        side[to, GROUP] = jnp.zeros((32, 128), BF)
    turned_fold = both.T.astype(BF)
    got = jnp.dot(turned_fold, act[...], preferred_element_type=F32)
    for h in range(2):
        fold_out[h] = got[h * 128 : (h + 1) * 128].T
    blank = jnp.zeros((64, 64), F32)

    def build(tap, carry):
        w = [conv_w[tap * 3 + k].astype(F32) for k in range(3)]
        rows = ((w[2], w[1], w[0], blank), (blank, w[2], w[1], w[0]))
        for z in range(2):
            for half in range(2):
                pair = jnp.concatenate(rows[z][half * 2 : half * 2 + 2], 1)
                toep[tap, z * 64 : (z + 1) * 64, half * 128 : (half + 1) * 128] = pair.astype(BF)
        return carry

    lax.fori_loop(0, 9, build, 0)
    faces.forward()
    turned = [cur_bf[:, g * 128 : (g + 1) * 128].astype(F32).T.astype(BF) for g in range(4)]
    low = lax.broadcasted_iota(jnp.int32, (96, 128), 1) < 64
    for a in range(3):
        for e in range(3):
            total = None
            for g in range(4):
                rhs = wide[a * 32 : a * 32 + 256, e * 640 + g * 128 : e * 640 + g * 128 + 256]
                one = jnp.dot(turned[g], rhs, preferred_element_type=F32)
                total = one if total is None else total + one
            total = total.T
            summed = total[0:192] + pltpu.roll(total[64:256], 64, 1)
            conv_out[a * 3 + e] = jnp.where(low, summed[0:96], pltpu.roll(summed[96:192], 64, 1))
    faces.finish()
    assemble(cur, pool, side, own_at, side_at, shifted, edge)
    for e in range(3):
        wide2[:, e * 640 : (e + 1) * 640] = shifted[e].astype(BF)
    for g in range(4):
        total = None
        for a in range(3):
            for e in range(3):
                lhs = wide2[a * 32 : a * 32 + 256, e * 640 + g * 128 : e * 640 + g * 128 + 256]
                one = lax.dot_general(
                    lhs, toep[(2 - a) * 3 + 2 - e], (((1,), (1,)), ((), ())), preferred_element_type=F32
                )
                total = one if total is None else total + one
        view = total.reshape(BS, NB, BS, 128)
        for n in range(NB):
            feat_out[n, :, :, g * 128 : (g + 1) * 128] = view[:, n]
    faces.drain()


def reduce_kernel(
    map_part, fold_part, conv_part,
    map_out, fold_out, conv_out,
    cat, first, acc, second, summed, third, chunk, fourth,
    s1, r1, s2, r2, s3, r3, s4, r4,
):
    bx, by = place()
    for k in range(1, NY):
        signal((bx, (by + k) % NY))
    for k in range(1, NX):
        signal(((bx + k) % NX, by))
    for t in range(9):
        cat[t * 128 : (t + 1) * 128] = map_part[t].astype(BF)
    for h in range(2):
        cat[1152 + h * 512 : 1152 + (h + 1) * 512] = fold_part[h].astype(BF)
    for t in range(9):
        cat[2176 + t * 96 : 2176 + (t + 1) * 96] = conv_part[t].astype(BF)
    cat[3040:3072] = jnp.zeros((32, 128), BF)
    pl.semaphore_wait(pltpu.get_barrier_semaphore(), NY + NX - 2)

    def piece(i):
        return pl.ds(pl.multiple_of(i * CHUNK, CHUNK), CHUNK)

    def small(i):
        return pl.ds(pl.multiple_of(i * SLICE, SLICE), SLICE)

    def peers_y(make):
        return [make(k, (by + k) % NY) for k in range(1, NY)]

    def peers_x(make):
        return [make(k, (bx + k) % NX) for k in range(1, NX)]

    out1 = peers_y(lambda k, p: remote(cat.at[piece(p)], first.at[by], s1.at[k], r1.at[by], (bx, p)))
    for c in out1:
        c.start()
    acc[...] = cat[piece(by)].astype(F32)
    for c in peers_y(lambda k, p: remote(cat.at[piece(p)], first.at[p], s1.at[k], r1.at[p], (bx, p))):
        c.wait_recv()
    for k in range(1, NY):
        acc[...] += first[(by + k) % NY].astype(F32)
    out2 = peers_x(lambda k, p: remote(acc.at[small(p)], second.at[bx], s2.at[k], r2.at[bx], (p, by)))
    for c in out2:
        c.start()
    total = acc[small(bx)]
    for c in peers_x(lambda k, p: remote(acc.at[small(p)], second.at[p], s2.at[k], r2.at[p], (p, by))):
        c.wait_recv()
    for k in range(1, NX):
        total = total + second[(bx + k) % NX]
    summed[...] = total
    out3 = peers_x(lambda k, p: remote(summed, third.at[small(bx)], s3.at[k], r3.at[bx], (p, by)))
    for c in out3:
        c.start()
    third[small(bx)] = total
    for c in peers_x(lambda k, p: remote(summed, third.at[small(p)], s3.at[k], r3.at[p], (p, by))):
        c.wait_recv()
    chunk[...] = third[...].astype(BF)
    out4 = peers_y(lambda k, p: remote(chunk, fourth.at[piece(by)], s4.at[k], r4.at[by], (bx, p)))
    for c in out4:
        c.start()
    fourth[piece(by)] = chunk[...]
    for c in peers_y(lambda k, p: remote(chunk, fourth.at[piece(p)], s4.at[k], r4.at[p], (bx, p))):
        c.wait_recv()
    for t in range(9):
        map_out[t] = fourth[t * 128 : (t + 1) * 128].astype(F32)
    for h in range(2):
        fold_out[h] = fourth[1152 + h * 512 : 1152 + (h + 1) * 512].astype(F32)
    for t in range(9):
        v = fourth[2176 + t * 96 : 2176 + (t + 1) * 96].astype(F32)
        conv_out[t, 0:96] = v[:, 0:64]
        conv_out[t, 96:192] = v[:, 64:128]
    for c in out1 + out2 + out3 + out4:
        c.wait_send()


def call(kernel, ident, ins, outs, scratch):
    return pl.pallas_call(
        kernel,
        in_specs=ins,
        out_specs=[VMEM] * len(outs),
        out_shape=[jax.ShapeDtypeStruct(s, t) for s, t in outs],
        scratch_shapes=scratch,
        compiler_params=pltpu.CompilerParams(
            collective_id=ident, has_side_effects=True, vmem_limit_bytes=50 * 2**20
        ),
    )


def body(vox_feats, block_coords, neighbors, conv_w, conv_b, fold_w, fold_b, map_w, map_b, cotangent):
    bx, by = place()
    taps = conv_w.reshape(27, 64, 64)
    fold_w2 = fold_w.reshape(2, 512, 128)
    inside = neighbors - bx * GROUP
    own_at = jnp.where((neighbors >= 0) & (inside >= 0) & (inside < GROUP), inside, GROUP)
    step = (jnp.arange(27) // 9 - 1)[:, None]
    beside = neighbors - (bx + step) * GROUP
    side_at = jnp.where(
        (neighbors >= 0) & (step != 0) & (beside >= 0) & (beside < GROUP), beside, GROUP
    )
    coord_tile = jnp.pad(block_coords, ((0, 5), (0, 124)))
    pre, act, wide, part, coords_all = call(
        owner_forward,
        1,
        [VMEM] * 5 + [SMEM] * 3,
        [
            ((256, 512), F32),
            ((256, 512), BF),
            ((320, 1920), BF),
            ((GROUP, 64, 128), BF),
            ((NY, 8, 128), jnp.int32),
        ],
        [
            pltpu.VMEM((BS, NB, BS, 512), F32),
            pltpu.VMEM((3, 320, 640), F32),
            pltpu.VMEM((2, 8, 640), F32),
            pltpu.VMEM((9, 256, 128), BF),
            pltpu.VMEM((BS, NB, BS, 256), F32),
            pltpu.VMEM((NB, 64, 128), BF),
            *FACE_SCRATCH,
            DMA((NY,)),
            DMA((NY,)),
            DMA((NY,)),
            DMA((NY,)),
        ],
    )(
        vox_feats,
        taps,
        jnp.tile(conv_b, 2)[None],
        fold_w2,
        coord_tile,
        block_coords,
        own_at,
        side_at,
    )
    group = coords_all[:, :3, :NB].transpose(1, 0, 2).reshape(3, GROUP)
    row, col = group[0] - bx * TR, group[1] - by * TC
    within = (col >= 0) & (col < TC)
    slot = row * TC + col
    key = jnp.where(within, slot * 2 + group[2], -1)
    match = key[None, :] == jnp.arange(TR * TC * 2)[:, None]
    table = jnp.min(jnp.where(match, jnp.arange(GROUP)[None, :], GROUP), 1).astype(jnp.int32)
    block_slot = jnp.clip(jnp.where(within, slot, 0), 0, TR * TC - 1).astype(jnp.int32)
    rim_scratch = [
        pltpu.VMEM((2, 2, COLS, 128), BF),
        pltpu.VMEM((2, 2, ROWS, 128), BF),
        pltpu.VMEM((2, 2, COLS, 128), BF),
        pltpu.VMEM((2, 2, ROWS, 128), BF),
        pltpu.VMEM((2, 4, 16, 128), BF),
        DMA((2, 8)),
        DMA((2, 8)),
    ]
    bev_map, map_part, back = call(
        map_kernel,
        2,
        [VMEM, SMEM, SMEM, VMEM, VMEM, VMEM, VMEM],
        [
            ((ROWS, COLS, 128), BF),
            ((9, 128, 128), F32),
            ((NY, NB, 64, 128), BF),
        ],
        [
            pltpu.VMEM((ROWS, COLS, 128), F32),
            pltpu.VMEM((ROWS, COLS, 128), F32),
            pltpu.VMEM((ROWS, COLS, 128), F32),
            pltpu.VMEM(((ROWS + 2) * COLS, 384), BF),
            pltpu.VMEM(((ROWS + 2) * COLS, 384), BF),
            pltpu.VMEM((ROWS * COLS, 128), BF),
            pltpu.VMEM((2, ROWS, 128), F32),
            pltpu.VMEM((TR * TC, 64, 128), BF),
            pltpu.VMEM((GROUP, 64, 128), BF),
            *rim_scratch,
            DMA((NY,)),
            DMA((NY,)),
        ],
    )(part, table, block_slot, cotangent, map_w.reshape(3, 384, 128), map_b[None], fold_b[None])
    feat_grad, conv_part, fold_part = call(
        owner_backward,
        3,
        [VMEM] * 6 + [SMEM] * 3,
        [
            ((NB, BS, BS, 512), F32),
            ((9, 96, 128), F32),
            ((2, 512, 128), F32),
        ],
        [
            pltpu.VMEM((BS, NB, BS, 512), F32),
            pltpu.VMEM((3, 320, 640), F32),
            pltpu.VMEM((2, 8, 640), F32),
            pltpu.VMEM((9, 128, 256), BF),
            pltpu.VMEM((320, 1920), BF),
            pltpu.VMEM((BS, NB, BS, 256), F32),
            pltpu.VMEM((256, 512), BF),
            *FACE_SCRATCH,
        ],
    )(pre, act, wide, back, taps, fold_w2, block_coords, own_at, side_at)
    map_grads, fold_grads, conv_grads = call(
        reduce_kernel,
        4,
        [VMEM] * 3,
        [
            ((9, 128, 128), F32),
            ((2, 512, 128), F32),
            ((9, 192, 64), F32),
        ],
        [
            pltpu.VMEM((CAT, 128), BF),
            pltpu.VMEM((NY, CHUNK, 128), BF),
            pltpu.VMEM((CHUNK, 128), F32),
            pltpu.VMEM((NX, SLICE, 128), F32),
            pltpu.VMEM((SLICE, 128), F32),
            pltpu.VMEM((CHUNK, 128), F32),
            pltpu.VMEM((CHUNK, 128), BF),
            pltpu.VMEM((CAT, 128), BF),
            *[DMA((size,)) for size in (NY, NY, NX, NX, NX, NX, NY, NY)],
        ],
    )(map_part, fold_part, conv_part)
    return (
        bev_map,
        feat_grad,
        conv_grads.reshape(3, 3, 3, 64, 64),
        fold_grads.reshape(1024, 128),
        map_grads.reshape(3, 3, 128, 128),
    )


def solution(mesh):
    placed = (
        P(("bx", "by"), None, None, None),
        P(None, ("bx", "by")),
        P(None, ("bx", "by")),
        P(),
        P(),
        P(),
        P(),
        P(),
        P(),
        P("bx", "by", None),
    )
    return jax.shard_map(
        body,
        mesh=mesh,
        in_specs=placed,
        out_specs=(P("bx", "by", None), P(("bx", "by"), None, None, None), P(), P(), P()),
        check_vma=False,
    )
```

```python
import functools

import jax
import jax.numpy as jnp
from jax import lax
from jax.experimental import pallas as pl
from jax.experimental.pallas import tpu as pltpu
from jax.sharding import PartitionSpec as P

MESH = pl.DeviceIdType.MESH
BF = jnp.bfloat16
F32 = jnp.float32
BS = 8
TR = 6
TC = 4
NB = 4
NX = 16
NY = 8
GROUP = NB * NY
ROWS = TR * BS
COLS = TC * BS
VMEM = pl.BlockSpec(memory_space=pltpu.VMEM)
SMEM = pl.BlockSpec(memory_space=pltpu.SMEM)
DMA = pltpu.SemaphoreType.DMA
CAT = 3072
CHUNK = CAT // NX
SLICE = CHUNK // NY


def place():
    return lax.axis_index("bx"), lax.axis_index("by")


def remote(src, dst, send, recv, device):
    return pltpu.make_async_remote_copy(
        src_ref=src,
        dst_ref=dst,
        send_sem=send,
        recv_sem=recv,
        device_id=device,
        device_id_type=MESH,
    )


def signal(device):
    pl.semaphore_signal(
        pltpu.get_barrier_semaphore(), inc=1, device_id=device, device_id_type=MESH
    )


def slope(pre):
    s = jax.nn.sigmoid(pre)
    return s * (1.0 + pre * (1.0 - s))


def rounded(v):
    return v.astype(BF).astype(F32)


def partners():
    bx, by = place()
    core = by % 2
    out = [(None, (bx, (by + k) % NY)) for k in range(1, NY)]
    out += [(None, ((bx + k) % NX, by)) for k in range(1, NX)]
    for step in (-1, 1):
        inside = bx > 0 if step < 0 else bx < NX - 1
        out += [(inside, (bx + step, core + 2 * j)) for j in range(NY // 2)]
        out.append((inside & (by > 0), (bx + step, by - 1)))
        out.append((inside & (by < NY - 1), (bx + step, by + 1)))
    return out


def greet():
    for ok, device in partners():
        if ok is None:
            signal(device)
        else:
            pl.when(ok)(functools.partial(signal, device))


def met():
    count = jnp.int32(0)
    for ok, _ in partners():
        count = count + (1 if ok is None else ok.astype(jnp.int32))
    pl.semaphore_wait(pltpu.get_barrier_semaphore(), count)


def pack_faces(cur, msg, coords):
    lane = lax.broadcasted_iota(jnp.int32, (32, 128), 1)

    def flat(v):
        return jnp.concatenate([v[:, t * 128 : (t + 1) * 128] for t in range(4)], 0)

    def one(n, carry):
        high = coords[2, n].astype(F32)
        msg[n, 0] = flat(cur[0, n]).astype(BF)
        msg[n, 1] = flat(cur[7, n]).astype(BF)
        msg[n, 2] = flat(cur[:, n, 0, :]).astype(BF)
        msg[n, 3] = flat(cur[:, n, 7, :]).astype(BF)
        top = cur[:, n, :, 384:512].reshape(64, 128)
        low = cur[:, n, :, 0:128].reshape(64, 128)
        face = pltpu.roll(top, 64, 1) * (1.0 - high) + low * high
        msg[n, 4] = jnp.where(lane < 64, face[0:32], pltpu.roll(face[32:64], 64, 1)).astype(BF)
        return carry

    lax.fori_loop(0, NB, one, 0)


class Faces:
    def __init__(self, msg, pool, side, own_s, fwd_s, side_s, sfwd_s, own_r, side_r):
        self.msg, self.pool, self.side = msg, pool, side
        self.own_s, self.fwd_s, self.side_s, self.sfwd_s = own_s, fwd_s, side_s, sfwd_s
        self.own_r, self.side_r = own_r, side_r
        self.bx, self.by = place()
        self.core = self.by % 2
        self.mate = self.by + 1 - 2 * self.core

    def first(self):
        bx, by = self.bx, self.by
        mine = pl.ds(by * NB, NB)
        out = [
            remote(self.msg, self.pool.at[mine], self.own_s.at[k], self.own_r.at[by], (bx, peer))
            for k, peer in enumerate([self.mate] + [(by + 2 * k) % NY for k in (1, 2, 3)])
        ]
        return out

    def sides(self, to):
        bx, by = self.bx, self.by
        mine = pl.ds(by * NB, NB)
        part, step = ((1, 1), (0, -1))[to]
        return [
            remote(
                self.msg.at[:, part],
                self.side.at[to, mine],
                self.side_s.at[to, j],
                self.side_r.at[to, by],
                (bx + step, self.core + 2 * j),
            )
            for j in range(4)
        ]

    def has(self, to):
        return (self.bx > 0, self.bx < NX - 1)[to]

    def sends(self, to):
        return self.has(1 - to)

    def start(self):
        for c in self.first():
            c.start()
        for to in range(2):

            @pl.when(self.sends(to))
            def _(to=to):
                for c in self.sides(to):
                    c.start()

        self.pool[pl.ds(self.by * NB, NB)] = self.msg[...]

    def own_landed(self, src, k):
        at = self.pool.at[pl.ds(src * NB, NB)]
        return remote(at, at, self.fwd_s.at[k], self.own_r.at[src], (self.bx, self.mate))

    def side_landed(self, to, src, j):
        at = self.side.at[to, pl.ds(src * NB, NB)]
        return remote(at, at, self.sfwd_s.at[to, j], self.side_r.at[to, src], (self.bx, self.mate))

    def forward(self):
        for k in (1, 3, 2):
            c = self.own_landed((self.by + 2 * k) % NY, k - 1)
            c.wait_recv()
            c.start()
        for to in range(2):

            @pl.when(self.has(to))
            def _(to=to):
                for j in range(4):
                    c = self.side_landed(to, self.core + 2 * j, j)
                    c.wait_recv()
                    c.start()

    def finish(self):
        for k in range(4):
            self.own_landed((self.mate + 2 * k) % NY, 0).wait_recv()
        for to in range(2):

            @pl.when(self.has(to))
            def _(to=to):
                for j in range(4):
                    self.side_landed(to, 1 - self.core + 2 * j, j).wait_recv()

    def drain(self):
        for c in self.first():
            c.wait_send()
        for k in (1, 2, 3):
            self.own_landed((self.by + 2 * k) % NY, k - 1).wait_send()
        for to in range(2):

            @pl.when(self.sends(to))
            def _(to=to):
                for c in self.sides(to):
                    c.wait_send()

            @pl.when(self.has(to))
            def _(to=to):
                for j in range(4):
                    self.side_landed(to, self.core + 2 * j, j).wait_send()


FACE_SCRATCH = [
    pltpu.VMEM((NB, 5, 32, 128), BF),
    pltpu.VMEM((GROUP + 1, 5, 32, 128), BF),
    pltpu.VMEM((2, GROUP + 1, 32, 128), BF),
    DMA((4,)),
    DMA((3,)),
    DMA((2, 4)),
    DMA((2, 4)),
    DMA((NY,)),
    DMA((2, NY)),
]


def assemble(cur, pool, side, neighbors, shifted, edge):
    low = lax.broadcasted_iota(jnp.int32, (8, 128), 1) < 64
    sub = lax.broadcasted_iota(jnp.int32, (8, 128), 0)

    bx, _ = place()

    def one(n, carry):
        def spot(k, group):
            at = neighbors[k, n]
            from_group = at - group * GROUP
            ok = (at >= 0) & (from_group >= 0) & (from_group < GROUP)
            return jnp.where(ok, from_group, GROUP)

        def face(part, k):
            return pool[spot(k, bx), part].astype(F32)

        def xface(dx, k):
            near = face(1 if dx < 0 else 0, k)
            return near + side[0 if dx < 0 else 1, spot(k, bx + dx)].astype(F32)

        def tiles(v):
            return [v[t * 8 : (t + 1) * 8] for t in range(4)]

        def turn(v):
            return pltpu.roll(v, 64, 1)

        def padz(core, before, after):
            r = [turn(t) for t in core]
            return (
                [jnp.where(low, before, r[0])]
                + [jnp.where(low, r[t - 1], r[t]) for t in (1, 2, 3)]
                + [jnp.where(low, r[3], after)]
            )

        def put(x, t, mid, above, below):
            row = pl.multiple_of((x * NB + n) * 8, 8)
            at = (pl.ds(row, 8), pl.ds(t * 128, 128))
            shifted[(1, *at)] = mid
            shifted[(0, *at)] = jnp.where(sub == 0, above, pltpu.roll(mid, 1, 0))
            shifted[(2, *at)] = jnp.where(sub == 7, below, pltpu.roll(mid, 7, 0))

        for x, dx in ((0, -1), (9, 1)):
            z = []
            for dy in range(3):
                k = 9 * (dx + 1) + 3 * dy
                z.append(
                    padz(tiles(xface(dx, k + 1)), turn(xface(dx, k)[24:32]), turn(xface(dx, k + 2)[0:8]))
                )
            for t in range(5):
                put(x, t, z[1][t], pltpu.roll(z[0][t], 1, 0), pltpu.roll(z[2][t], 7, 0))
        for i, (k, part) in enumerate(((9, 3), (15, 2))):
            z = padz(tiles(face(part, k + 1)), turn(face(part, k)[24:32]), turn(face(part, k + 2)[0:8]))
            for t in range(5):
                edge[i, :, t * 128 : (t + 1) * 128] = z[t]
        under = face(4, 12)
        over = face(4, 14)
        for x in range(BS):
            at = slice(x % 4 * 8, x % 4 * 8 + 8)
            before = under[at] if x < 4 else turn(under[at])
            after = turn(over[at]) if x < 4 else over[at]
            z = padz([cur[x, n, :, t * 128 : (t + 1) * 128] for t in range(4)], before, after)
            for t in range(5):
                lanes = slice(t * 128, (t + 1) * 128)
                put(x + 1, t, z[t], edge[0, x : x + 1, lanes], edge[1, x : x + 1, lanes])
        return carry

    lax.fori_loop(0, NB, one, 0)


NEAR = [(-1, 0), (1, 0), (0, -1), (0, 1), (-1, -1), (-1, 1), (1, -1), (1, 1)]


class Rim:
    def __init__(self, row_out, col_out, row_in, col_in, corner_in, send, recv):
        self.row_out, self.col_out = row_out, col_out
        self.row_in, self.col_in, self.corner_in = row_in, col_in, corner_in
        self.send, self.recv = send, recv
        self.bx, self.by = place()

    def exists(self, d):
        dx, dy = NEAR[d]
        ok = None
        for v, step, size in ((self.bx, dx, NX), (self.by, dy, NY)):
            if step:
                here = v > 0 if step < 0 else v < size - 1
                ok = here if ok is None else ok & here
        return ok

    def copy(self, d):
        dx, dy = NEAR[d]
        back = NEAR.index((-dx, -dy))
        if dy == 0:
            src, dst = self.row_out.at[d], self.row_in.at[back]
        elif dx == 0:
            src, dst = self.col_out.at[d - 2], self.col_in.at[back - 2]
        else:
            src = self.row_out.at[0 if dx < 0 else 1, pl.ds(0 if dy < 0 else 16, 16)]
            dst = self.corner_in.at[back - 4]
        return remote(src, dst, self.send.at[d], self.recv.at[back], (self.bx + dx, self.by + dy))

    def landing(self, d):
        dx, dy = NEAR[d]
        if dy == 0:
            return self.row_in.at[d]
        if dx == 0:
            return self.col_in.at[d - 2]
        return self.corner_in.at[d - 4]

    def start(self, plane):
        self.row_out[0] = plane[0].astype(BF)
        self.row_out[1] = plane[ROWS - 1].astype(BF)
        self.col_out[0] = plane[:, 0, :].astype(BF)
        self.col_out[1] = plane[:, COLS - 1, :].astype(BF)
        for d in range(8):

            @pl.when(self.exists(d))
            def _(d=d):
                self.copy(d).start()

            @pl.when(jnp.logical_not(self.exists(d)))
            def _(d=d):
                at = self.landing(d)
                at[...] = jnp.zeros(at.shape, BF)

    def finish(self):
        for d in range(8):

            @pl.when(self.exists(d))
            def _(d=d):
                dx, dy = NEAR[d]
                at = self.landing(d)
                remote(at, at, self.send.at[d], self.recv.at[d], (self.bx + dx, self.by + dy)).wait_recv()

    def drain(self):
        for d in range(8):

            @pl.when(self.exists(d))
            def _(d=d):
                self.copy(d).wait_send()


def spread(plane, rim, side32, out):
    side32[0] = rim.col_in[0].astype(F32)
    side32[1] = rim.col_in[1].astype(F32)
    j = lax.broadcasted_iota(jnp.int32, (COLS, 128), 0)

    def put(at, row, left, right):
        rows = pl.ds(pl.multiple_of(at * COLS, COLS), COLS)
        out[rows, 0:128] = jnp.where(j == 0, left, pltpu.roll(row, 1, 0)).astype(BF)
        out[rows, 128:256] = row.astype(BF)
        out[rows, 256:384] = jnp.where(j == COLS - 1, right, pltpu.roll(row, COLS - 1, 0)).astype(BF)

    def inner(i, carry):
        put(i + 1, plane[i], side32[0, pl.ds(i, 1), :], side32[1, pl.ds(i, 1), :])
        return carry

    lax.fori_loop(0, ROWS, inner, 0)
    corner = [rim.corner_in[c].astype(F32) for c in range(4)]
    put(0, rim.row_in[0].astype(F32), corner[0][15:16], corner[1][0:1])
    put(ROWS + 1, rim.row_in[1].astype(F32), corner[2][15:16], corner[3][0:1])

class Spread:
    def __init__(self, src, pool, size, own_s, fwd_s, own_r):
        self.src, self.pool, self.size = src, pool, size
        self.own_s, self.fwd_s, self.own_r = own_s, fwd_s, own_r
        self.bx, self.by = place()
        self.mate = self.by + 1 - 2 * (self.by % 2)

    def at(self, src):
        return self.pool.at[pl.ds(src * self.size, self.size)]

    def first(self):
        peers = [(self.by + 2) % NY, (self.by + 6) % NY, (self.by + 4) % NY, self.mate]
        return [
            remote(self.src, self.at(self.by), self.own_s.at[k], self.own_r.at[self.by], (self.bx, peer))
            for k, peer in enumerate(peers)
        ]

    def landed(self, src, k):
        at = self.at(src)
        return remote(at, at, self.fwd_s.at[k], self.own_r.at[src], (self.bx, self.mate))

    def start(self):
        for c in self.first():
            c.start()
        self.pool[pl.ds(self.by * self.size, self.size)] = self.src[...]

    def forward(self):
        for k in (1, 3, 2):
            c = self.landed((self.by + 2 * k) % NY, k - 1)
            c.wait_recv()
            c.start()

    def finish(self):
        for k in range(4):
            self.landed((self.mate + 2 * k) % NY, 0).wait_recv()

    def drain(self):
        for c in self.first():
            c.wait_send()
        for k in (1, 2, 3):
            self.landed((self.by + 2 * k) % NY, k - 1).wait_send()


def dot(a, b):
    return jnp.dot(a, b, preferred_element_type=F32)


def dot_t(a, b):
    return lax.dot_general(a, b, (((1,), (1,)), ((), ())), preferred_element_type=F32)


def window(wide, a, e, g):
    return wide[a * 32 : a * 32 + 256, e * 640 + g * 128 : e * 640 + g * 128 + 256]


def whole(
    vox_h, conv_w_h, fold_w_h, map_w_h, cot_h, conv_b, fold_b, map_b, coords, neighbors,
    bev_out, feat_out, conv_out, fold_out, map_out,
    vox, conv_w, fold_w, map_w, cot, load_sem,
    cur, shifted, edge, toep, toep_back, wide, pre, act, fold_both, part, part_pool,
    code, codes_v, codes, table,
    fold, plane, gplane, spread_mid, spread_grad, side32, slots, ready, back,
    split, cur_bf, cat, second, acc, third, summed, all32, chunk, fourth,
    face_a, face_f, part_sems, code_s, code_r, code_l,
    row_out, col_out, row_in, col_in, corner_in, rim_s, rim_r, back_s, back_r,
    zs, zr, ys, yr, gs, gr, ws, wr,
):
    bx, by = place()
    greet()
    loads = [
        pltpu.make_async_copy(src, dst, load_sem.at[i])
        for i, (src, dst) in enumerate(
            ((vox_h, vox), (conv_w_h, conv_w), (fold_w_h, fold_w), (map_w_h, map_w), (cot_h, cot))
        )
    ]
    for c in loads:
        c.start()
    lane = lax.broadcasted_iota(jnp.int32, (8, 128), 1)
    tile = jnp.zeros((8, 128), jnp.int32)
    for n in range(NB):
        number = ((coords[0, n] - bx * TR) * (TC * NY) + coords[1, n]) * 2 + coords[2, n]
        tile = jnp.where(lane == n, number, tile)
    code[...] = tile
    codes_v[by] = tile
    loads[0].wait()
    for n in range(NB):
        cur[:, n] = vox[n].astype(F32)
    faces = Faces(*face_a)
    pack_faces(cur, faces.msg, coords)
    met()
    tell = [
        remote(code, codes_v.at[by], code_s.at[k], code_r.at[by], (bx, (by + k) % NY)) for k in range(1, NY)
    ]
    for c in tell:
        c.start()
    faces.start()
    back_faces = Faces(*face_f)
    for f in (faces, back_faces):
        f.pool[GROUP] = jnp.zeros((5, 32, 128), BF)
        for to in range(2):
            f.side[to, GROUP] = jnp.zeros((32, 128), BF)
    loads[1].wait()
    blank = jnp.zeros((64, 64), F32)

    def build(tap, carry):
        w = [conv_w[tap * 3 + k].astype(F32) for k in range(3)]
        ahead = [blank, *w, blank]
        for z in range(4):
            toep[tap, z * 64 : (z + 1) * 64, :] = jnp.concatenate([ahead[z + 1], ahead[z]], 1).astype(BF)
        rows = ((w[2], w[1], w[0], blank), (blank, w[2], w[1], w[0]))
        for z in range(2):
            for half in range(2):
                pair = jnp.concatenate(rows[z][half * 2 : half * 2 + 2], 1)
                toep_back[tap, z * 64 : (z + 1) * 64, half * 128 : (half + 1) * 128] = pair.astype(BF)
        return carry

    lax.fori_loop(0, 9, build, 0)
    for k in range(1, NY):
        src = (by + k) % NY
        remote(code, codes_v.at[src], code_s.at[k], code_r.at[src], (bx, src)).wait_recv()
    to_scalar = pltpu.make_async_copy(codes_v.at[:, 0], codes, code_l.at[0])
    to_scalar.start()
    to_scalar.wait()

    def look(s, carry):
        want = ((s // (TC * 2)) * (TC * NY) + by * TC + (s // 2) % TC) * 2 + s % 2
        found = jnp.int32(GROUP)
        for b in range(GROUP):
            found = jnp.where(codes[b // NB, b % NB] == want, b, found)
        table[s] = found
        return carry

    lax.fori_loop(0, TR * TC * 2, look, 0)
    faces.forward()
    faces.finish()
    assemble(cur, faces.pool, faces.side, neighbors, shifted, edge)
    for e in range(3):
        wide[:, e * 640 : (e + 1) * 640] = shifted[e].astype(BF)
    for group in range(4):
        total = conv_b[...]
        for a in range(3):
            for e in range(3):
                total = total + dot(window(wide, a, e, group), toep[a * 3 + e])
        lanes = slice(group * 128, (group + 1) * 128)
        pre[:, lanes] = total
        act[:, lanes] = (total * jax.nn.sigmoid(total)).astype(BF)
    loads[2].wait()
    for h in range(2):
        fold_both[:, :, :, h * 128 : (h + 1) * 128] = dot(act[...], fold_w[h]).reshape(BS, NB, BS, 128)
    for n in range(NB):
        high = coords[2, n].astype(F32)
        one = fold_both[:, n, :, 0:128] * (1.0 - high) + fold_both[:, n, :, 128:256] * high
        part[n] = one.reshape(64, 128).astype(BF)
    parts = Spread(part, part_pool, NB, *part_sems)
    parts.start()
    loads[3].wait()
    loads[4].wait()
    parts.forward()
    parts.finish()

    rims = [
        Rim(row_out.at[p], col_out.at[p], row_in.at[p], col_in.at[p], corner_in.at[p], rim_s.at[p], rim_r.at[p])
        for p in range(2)
    ]
    for r in range(TR):
        for c in range(TC):
            total = fold_b[...]
            for h in range(2):
                at = table[(r * TC + c) * 2 + h]
                here = (at < GROUP).astype(F32)
                total = total + part_pool[jnp.minimum(at, GROUP - 1)].astype(F32) * here
            where = (slice(r * BS, (r + 1) * BS), slice(c * BS, (c + 1) * BS))
            fold[where] = total.reshape(BS, BS, 128)
            plane[where] = rounded(total * jax.nn.sigmoid(total)).reshape(BS, BS, 128)
    rims[0].start(plane)
    rims[0].finish()
    spread(plane, rims[0], side32, spread_mid)

    def ahead(i, carry):
        start = pl.multiple_of(i * 256, 256)
        total = map_b[...]
        for a in range(3):
            total = total + dot(spread_mid[pl.ds(start + a * COLS, 256), :], map_w[a])
        bev_out[pl.ds(i * BS, BS)] = (total * jax.nn.sigmoid(total)).reshape(BS, COLS, 128).astype(BF)
        g = cot[pl.ds(i * BS, BS)].astype(F32).reshape(256, 128) * slope(total)
        gplane[pl.ds(i * BS, BS)] = rounded(g).reshape(BS, COLS, 128)
        return carry

    lax.fori_loop(0, TR, ahead, 0)
    rims[1].start(gplane)
    turned = gplane[...].reshape(ROWS * COLS, 128).T.astype(BF)
    for a in range(3):
        got = dot(turned, spread_mid[a * COLS : a * COLS + ROWS * COLS, :])
        for e in range(3):
            t = a * 3 + e
            cat[t * 128 : (t + 1) * 128] = got[:, e * 128 : (e + 1) * 128].T.astype(BF)

    def gave(q):
        return remote(
            cat.at[pl.ds(q * CHUNK, CHUNK)], second.at[bx], zs.at[q], zr.at[bx], (q, by)
        )

    def give_chunks(qs):
        for q in qs:

            @pl.when(bx != q)
            def _(q=q):
                gave(q).start()

    give_chunks(range(6))
    rims[1].finish()
    spread(gplane, rims[1], side32, spread_grad)

    def behind(i, carry):
        start = pl.multiple_of(i * 256, 256)
        total = None
        for a in range(3):
            for e in range(3):
                lhs = spread_grad[pl.ds(start + a * COLS, 256), e * 128 : (e + 1) * 128]
                one = dot_t(lhs, map_w[2 - a, (2 - e) * 128 : (3 - e) * 128, :])
                total = one if total is None else total + one
        grad = (total * slope(fold[pl.ds(i * BS, BS)].reshape(256, 128))).reshape(BS, COLS, 128)
        for c in range(TC):
            slots[i * TC + c] = grad[:, c * BS : (c + 1) * BS, :].reshape(64, 128).astype(BF)
        return carry

    lax.fori_loop(0, TR, behind, 0)

    def fill(b, carry):
        number = codes[b // NB, b % NB] // 2
        c = number % (TC * NY) - by * TC
        at = number // (TC * NY) * TC + jnp.clip(c, 0, TC - 1)
        ready[b] = slots[jnp.clip(at, 0, TR * TC - 1)]
        return carry

    lax.fori_loop(0, GROUP, fill, 0)
    give = [
        remote(
            ready.at[pl.ds((by + k) % NY * NB, NB)],
            back.at[by],
            back_s.at[k],
            back_r.at[by],
            (bx, (by + k) % NY),
        )
        for k in (4, 3, 5, 2, 6, 1, 7)
    ]
    for c in give:
        c.start()
    back[by] = ready[pl.ds(by * NB, NB)]
    for k in range(1, NY):
        src = (by + k) % NY
        remote(ready.at[pl.ds(0, NB)], back.at[src], back_s.at[k], back_r.at[src], (bx, src)).wait_recv()

    for n in range(NB):
        high = coords[2, n].astype(F32)
        mine = back[jnp.clip(coords[1, n] // TC, 0, NY - 1), n].astype(F32).reshape(BS, BS, 128)
        split[:, n, :, 0:128] = mine * (1.0 - high)
        split[:, n, :, 128:256] = mine * high
    both = split[...].reshape(256, 256)
    act_grad = None
    for h in range(2):
        one = dot_t(both[:, h * 128 : (h + 1) * 128].astype(BF), fold_w[h])
        act_grad = one if act_grad is None else act_grad + one
    grad = rounded(rounded(act_grad) * slope(pre[...]))
    cur[...] = grad.reshape(BS, NB, BS, 512)
    cur_bf[...] = grad.astype(BF)
    pack_faces(cur, back_faces.msg, coords)
    back_faces.start()
    got = dot(both.T.astype(BF), act[...])
    for h in range(2):
        cat[1152 + h * 512 : 1152 + (h + 1) * 512] = got[h * 128 : (h + 1) * 128].T.astype(BF)
    give_chunks(range(6, 11))
    turned = [cur_bf[:, g * 128 : (g + 1) * 128].astype(F32).T.astype(BF) for g in range(4)]
    low = lax.broadcasted_iota(jnp.int32, (96, 128), 1) < 64
    for a in range(3):
        for e in range(3):
            total = None
            for g in range(4):
                one = dot(turned[g], window(wide, a, e, g))
                total = one if total is None else total + one
            total = total.T
            summed_z = total[0:192] + pltpu.roll(total[64:256], 64, 1)
            row = 2176 + (a * 3 + e) * 96
            cat[row : row + 96] = jnp.where(
                low, summed_z[0:96], pltpu.roll(summed_z[96:192], 64, 1)
            ).astype(BF)
    cat[3040:3072] = jnp.zeros((32, 128), BF)
    give_chunks(range(11, NX))
    acc[...] = cat[pl.ds(pl.multiple_of(bx * CHUNK, CHUNK), CHUNK)].astype(F32)
    for k in range(1, NX):
        src = (bx + k) % NX
        remote(cat.at[pl.ds(0, CHUNK)], second.at[src], zs.at[0], zr.at[src], (src, by)).wait_recv()
        acc[...] += second[src].astype(F32)

    def small(i):
        return pl.ds(pl.multiple_of(i * SLICE, SLICE), SLICE)

    def to_y(k, p):
        return remote(acc.at[small(p)], third.at[by], ys.at[k], yr.at[by], (bx, p))

    for k in range(1, NY):
        to_y(k, (by + k) % NY).start()
    back_faces.forward()
    total = acc[small(by)]
    for k in range(1, NY):
        src = (by + k) % NY
        remote(summed, third.at[src], ys.at[k], yr.at[src], (bx, src)).wait_recv()
        total = total + third[src]
    summed[...] = total
    all32[small(by)] = total

    def all_y(k, p):
        return remote(summed, all32.at[small(by)], gs.at[k], gr.at[by], (bx, p))

    for k in range(1, NY):
        all_y(k, (by + k) % NY).start()
    for k in range(1, NY):
        src = (by + k) % NY
        remote(summed, all32.at[small(src)], gs.at[k], gr.at[src], (bx, src)).wait_recv()
    chunk[...] = all32[...].astype(BF)

    def piece(i):
        return pl.ds(pl.multiple_of(i * CHUNK, CHUNK), CHUNK)

    def all_x(k):
        return remote(chunk, fourth.at[piece(bx)], ws.at[k], wr.at[bx], ((bx + k) % NX, by))

    for k in range(1, NX):
        all_x(k).start()
    fourth[piece(bx)] = chunk[...]
    back_faces.finish()
    assemble(cur, back_faces.pool, back_faces.side, neighbors, shifted, edge)
    for e in range(3):
        wide[:, e * 640 : (e + 1) * 640] = shifted[e].astype(BF)
    for g in range(4):
        total = None
        for a in range(3):
            for e in range(3):
                one = dot_t(window(wide, a, e, g), toep_back[(2 - a) * 3 + 2 - e])
                total = one if total is None else total + one
        view = total.reshape(BS, NB, BS, 128)
        for n in range(NB):
            feat_out[n, :, :, g * 128 : (g + 1) * 128] = view[:, n]
    for k in range(1, NX):
        src = (bx + k) % NX
        remote(chunk, fourth.at[piece(src)], ws.at[k], wr.at[src], (src, by)).wait_recv()
    for t in range(9):
        map_out[t] = fourth[t * 128 : (t + 1) * 128].astype(F32)
    for h in range(2):
        fold_out[h] = fourth[1152 + h * 512 : 1152 + (h + 1) * 512].astype(F32)
    for t in range(9):
        v = fourth[2176 + t * 96 : 2176 + (t + 1) * 96].astype(F32)
        conv_out[t, 0:96] = v[:, 0:64]
        conv_out[t, 96:192] = v[:, 64:128]

    for c in tell + give:
        c.wait_send()
    faces.drain()
    back_faces.drain()
    parts.drain()
    for rim in rims:
        rim.drain()
    for q in range(NX):

        @pl.when(bx != q)
        def _(q=q):
            gave(q).wait_send()

    for k in range(1, NY):
        to_y(k, (by + k) % NY).wait_send()
        all_y(k, (by + k) % NY).wait_send()
    for k in range(1, NX):
        all_x(k).wait_send()


def body(vox_feats, block_coords, neighbors, conv_w, conv_b, fold_w, fold_b, map_w, map_b, cotangent):
    far = pl.BlockSpec(memory_space=pl.ANY)
    bev_map, feat_grad, conv_grads, fold_grads, map_grads = pl.pallas_call(
        whole,
        in_specs=[far] * 5 + [VMEM] * 3 + [SMEM] * 2,
        out_specs=[VMEM] * 5,
        out_shape=[
            jax.ShapeDtypeStruct((ROWS, COLS, 128), BF),
            jax.ShapeDtypeStruct((NB, BS, BS, 512), F32),
            jax.ShapeDtypeStruct((9, 192, 64), F32),
            jax.ShapeDtypeStruct((2, 512, 128), F32),
            jax.ShapeDtypeStruct((9, 128, 128), F32),
        ],
        scratch_shapes=[
            pltpu.VMEM((NB, BS, BS, 512), BF),
            pltpu.VMEM((27, 64, 64), BF),
            pltpu.VMEM((2, 512, 128), BF),
            pltpu.VMEM((3, 384, 128), BF),
            pltpu.VMEM((ROWS, COLS, 128), BF),
            DMA((5,)),
            pltpu.VMEM((BS, NB, BS, 512), F32),
            pltpu.VMEM((3, 320, 640), F32),
            pltpu.VMEM((2, 8, 640), F32),
            pltpu.VMEM((9, 256, 128), BF),
            pltpu.VMEM((9, 128, 256), BF),
            pltpu.VMEM((320, 1920), BF),
            pltpu.VMEM((256, 512), F32),
            pltpu.VMEM((256, 512), BF),
            pltpu.VMEM((BS, NB, BS, 256), F32),
            pltpu.VMEM((NB, 64, 128), BF),
            pltpu.VMEM((GROUP, 64, 128), BF),
            pltpu.VMEM((8, 128), jnp.int32),
            pltpu.VMEM((NY, 8, 128), jnp.int32),
            pltpu.SMEM((NY, 128), jnp.int32),
            pltpu.SMEM((TR * TC * 2,), jnp.int32),
            pltpu.VMEM((ROWS, COLS, 128), F32),
            pltpu.VMEM((ROWS, COLS, 128), F32),
            pltpu.VMEM((ROWS, COLS, 128), F32),
            pltpu.VMEM(((ROWS + 2) * COLS, 384), BF),
            pltpu.VMEM(((ROWS + 2) * COLS, 384), BF),
            pltpu.VMEM((2, ROWS, 128), F32),
            pltpu.VMEM((TR * TC, 64, 128), BF),
            pltpu.VMEM((GROUP, 64, 128), BF),
            pltpu.VMEM((NY, NB, 64, 128), BF),
            pltpu.VMEM((BS, NB, BS, 256), F32),
            pltpu.VMEM((256, 512), BF),
            pltpu.VMEM((CAT, 128), BF),
            pltpu.VMEM((NX, CHUNK, 128), BF),
            pltpu.VMEM((CHUNK, 128), F32),
            pltpu.VMEM((NY, SLICE, 128), F32),
            pltpu.VMEM((SLICE, 128), F32),
            pltpu.VMEM((CHUNK, 128), F32),
            pltpu.VMEM((CHUNK, 128), BF),
            pltpu.VMEM((CAT, 128), BF),
            FACE_SCRATCH,
            FACE_SCRATCH,
            [DMA((4,)), DMA((3,)), DMA((NY,))],
            DMA((NY,)),
            DMA((NY,)),
            DMA((1,)),
            pltpu.VMEM((2, 2, COLS, 128), BF),
            pltpu.VMEM((2, 2, ROWS, 128), BF),
            pltpu.VMEM((2, 2, COLS, 128), BF),
            pltpu.VMEM((2, 2, ROWS, 128), BF),
            pltpu.VMEM((2, 4, 16, 128), BF),
            DMA((2, 8)),
            DMA((2, 8)),
            DMA((NY,)),
            DMA((NY,)),
            DMA((NX,)),
            DMA((NX,)),
            DMA((NY,)),
            DMA((NY,)),
            DMA((NY,)),
            DMA((NY,)),
            DMA((NX,)),
            DMA((NX,)),
        ],
        compiler_params=pltpu.CompilerParams(
            collective_id=1, has_side_effects=True, vmem_limit_bytes=58 * 2**20
        ),
    )(
        vox_feats,
        conv_w.reshape(27, 64, 64),
        fold_w.reshape(2, 512, 128),
        map_w.reshape(3, 384, 128),
        cotangent,
        jnp.concatenate([conv_b, conv_b])[None],
        fold_b[None],
        map_b[None],
        block_coords,
        neighbors,
    )
    return (
        bev_map,
        feat_grad,
        conv_grads.reshape(3, 3, 3, 64, 64),
        fold_grads.reshape(1024, 128),
        map_grads.reshape(3, 3, 128, 128),
    )


def solution(mesh):
    placed = (
        P(("bx", "by"), None, None, None),
        P(None, ("bx", "by")),
        P(None, ("bx", "by")),
        P(),
        P(),
        P(),
        P(),
        P(),
        P(),
        P("bx", "by", None),
    )
    return jax.shard_map(
        body,
        mesh=mesh,
        in_specs=placed,
        out_specs=(P("bx", "by", None), P(("bx", "by"), None, None, None), P(), P(), P()),
        check_vma=False,
    )
```

```python
import functools

import jax
import jax.numpy as jnp
from jax import lax
from jax.experimental import pallas as pl
from jax.experimental.pallas import tpu as pltpu
from jax.sharding import PartitionSpec as P

MESH = pl.DeviceIdType.MESH
BF = jnp.bfloat16
F32 = jnp.float32
BS = 8
TR = 6
TC = 4
NB = 4
NX = 16
NY = 8
GROUP = NB * NY
ROWS = TR * BS
COLS = TC * BS
VMEM = pl.BlockSpec(memory_space=pltpu.VMEM)
SMEM = pl.BlockSpec(memory_space=pltpu.SMEM)
DMA = pltpu.SemaphoreType.DMA
CAT = 3072


def place():
    return lax.axis_index("bx"), lax.axis_index("by")


def remote(src, dst, send, recv, device):
    return pltpu.make_async_remote_copy(
        src_ref=src,
        dst_ref=dst,
        send_sem=send,
        recv_sem=recv,
        device_id=device,
        device_id_type=MESH,
    )


def signal(device):
    pl.semaphore_signal(
        pltpu.get_barrier_semaphore(), inc=1, device_id=device, device_id_type=MESH
    )


def slope(pre):
    s = jax.nn.sigmoid(pre)
    return s * (1.0 + pre * (1.0 - s))


def rounded(v):
    return v.astype(BF).astype(F32)


def partners():
    bx, by = place()
    core = by % 2
    out = [(None, (bx, (by + k) % NY)) for k in range(1, NY)]
    out += [(None, ((bx + k) % NX, by)) for k in range(1, NX)]
    for step in (-1, 1):
        inside = bx > 0 if step < 0 else bx < NX - 1
        out += [(inside, (bx + step, core + 2 * j)) for j in range(NY // 2)]
        out.append((inside & (by > 0), (bx + step, by - 1)))
        out.append((inside & (by < NY - 1), (bx + step, by + 1)))
    return out


def greet():
    for ok, device in partners():
        if ok is None:
            signal(device)
        else:
            pl.when(ok)(functools.partial(signal, device))


def met():
    count = jnp.int32(0)
    for ok, _ in partners():
        count = count + (1 if ok is None else ok.astype(jnp.int32))
    pl.semaphore_wait(pltpu.get_barrier_semaphore(), count)


def pack_faces(cur, msg, coords):
    lane = lax.broadcasted_iota(jnp.int32, (32, 128), 1)

    def flat(v):
        return jnp.concatenate([v[:, t * 128 : (t + 1) * 128] for t in range(4)], 0)

    def one(n, carry):
        high = coords[2, n].astype(F32)
        msg[n, 0] = flat(cur[0, n]).astype(BF)
        msg[n, 1] = flat(cur[7, n]).astype(BF)
        msg[n, 2] = flat(cur[:, n, 0, :]).astype(BF)
        msg[n, 3] = flat(cur[:, n, 7, :]).astype(BF)
        top = cur[:, n, :, 384:512].reshape(64, 128)
        low = cur[:, n, :, 0:128].reshape(64, 128)
        face = pltpu.roll(top, 64, 1) * (1.0 - high) + low * high
        msg[n, 4] = jnp.where(lane < 64, face[0:32], pltpu.roll(face[32:64], 64, 1)).astype(BF)
        return carry

    lax.fori_loop(0, NB, one, 0)


class Faces:
    def __init__(self, msg, pool, side, own_s, fwd_s, side_s, sfwd_s, own_r, side_r):
        self.msg, self.pool, self.side = msg, pool, side
        self.own_s, self.fwd_s, self.side_s, self.sfwd_s = own_s, fwd_s, side_s, sfwd_s
        self.own_r, self.side_r = own_r, side_r
        self.bx, self.by = place()
        self.core = self.by % 2
        self.mate = self.by + 1 - 2 * self.core

    def first(self):
        bx, by = self.bx, self.by
        mine = pl.ds(by * NB, NB)
        out = [
            remote(self.msg, self.pool.at[mine], self.own_s.at[k], self.own_r.at[by], (bx, peer))
            for k, peer in enumerate([self.mate] + [(by + 2 * k) % NY for k in (1, 2, 3)])
        ]
        return out

    def sides(self, to):
        bx, by = self.bx, self.by
        mine = pl.ds(by * NB, NB)
        part, step = ((1, 1), (0, -1))[to]
        return [
            remote(
                self.msg.at[:, part],
                self.side.at[to, mine],
                self.side_s.at[to, j],
                self.side_r.at[to, by],
                (bx + step, self.core + 2 * j),
            )
            for j in range(4)
        ]

    def has(self, to):
        return (self.bx > 0, self.bx < NX - 1)[to]

    def sends(self, to):
        return self.has(1 - to)

    def start(self):
        for c in self.first():
            c.start()
        for to in range(2):

            @pl.when(self.sends(to))
            def _(to=to):
                for c in self.sides(to):
                    c.start()

        self.pool[pl.ds(self.by * NB, NB)] = self.msg[...]

    def own_landed(self, src, k):
        at = self.pool.at[pl.ds(src * NB, NB)]
        return remote(at, at, self.fwd_s.at[k], self.own_r.at[src], (self.bx, self.mate))

    def side_landed(self, to, src, j):
        at = self.side.at[to, pl.ds(src * NB, NB)]
        return remote(at, at, self.sfwd_s.at[to, j], self.side_r.at[to, src], (self.bx, self.mate))

    def forward(self):
        for k in (1, 3, 2):
            c = self.own_landed((self.by + 2 * k) % NY, k - 1)
            c.wait_recv()
            c.start()
        for to in range(2):

            @pl.when(self.has(to))
            def _(to=to):
                for j in range(4):
                    c = self.side_landed(to, self.core + 2 * j, j)
                    c.wait_recv()
                    c.start()

    def finish(self):
        for k in range(4):
            self.own_landed((self.mate + 2 * k) % NY, 0).wait_recv()
        for to in range(2):

            @pl.when(self.has(to))
            def _(to=to):
                for j in range(4):
                    self.side_landed(to, 1 - self.core + 2 * j, j).wait_recv()

    def drain(self):
        for c in self.first():
            c.wait_send()
        for k in (1, 2, 3):
            self.own_landed((self.by + 2 * k) % NY, k - 1).wait_send()
        for to in range(2):

            @pl.when(self.sends(to))
            def _(to=to):
                for c in self.sides(to):
                    c.wait_send()

            @pl.when(self.has(to))
            def _(to=to):
                for j in range(4):
                    self.side_landed(to, self.core + 2 * j, j).wait_send()


FACE_SCRATCH = [
    pltpu.VMEM((NB, 5, 32, 128), BF),
    pltpu.VMEM((GROUP + 1, 5, 32, 128), BF),
    pltpu.VMEM((2, GROUP + 1, 32, 128), BF),
    DMA((4,)),
    DMA((3,)),
    DMA((2, 4)),
    DMA((2, 4)),
    DMA((NY,)),
    DMA((2, NY)),
]


def assemble(cur, pool, side, neighbors, shifted, edge):
    low = lax.broadcasted_iota(jnp.int32, (8, 128), 1) < 64
    sub = lax.broadcasted_iota(jnp.int32, (8, 128), 0)

    bx, _ = place()

    def one(n, carry):
        def spot(k, group):
            at = neighbors[n, k]
            from_group = at - group * GROUP
            ok = (at >= 0) & (from_group >= 0) & (from_group < GROUP)
            return jnp.where(ok, from_group, GROUP)

        def face(part, k):
            return pool[spot(k, bx), part].astype(F32)

        def xface(dx, k):
            near = face(1 if dx < 0 else 0, k)
            return near + side[0 if dx < 0 else 1, spot(k, bx + dx)].astype(F32)

        def tiles(v):
            return [v[t * 8 : (t + 1) * 8] for t in range(4)]

        def turn(v):
            return pltpu.roll(v, 64, 1)

        def padz(core, before, after):
            r = [turn(t) for t in core]
            return (
                [jnp.where(low, before, r[0])]
                + [jnp.where(low, r[t - 1], r[t]) for t in (1, 2, 3)]
                + [jnp.where(low, r[3], after)]
            )

        def put(x, t, mid, above, below):
            row = pl.multiple_of((x * NB + n) * 8, 8)
            at = (pl.ds(row, 8), pl.ds(t * 128, 128))
            shifted[(1, *at)] = mid
            shifted[(0, *at)] = jnp.where(sub == 0, above, pltpu.roll(mid, 1, 0))
            shifted[(2, *at)] = jnp.where(sub == 7, below, pltpu.roll(mid, 7, 0))

        for x, dx in ((0, -1), (9, 1)):
            z = []
            for dy in range(3):
                k = 9 * (dx + 1) + 3 * dy
                z.append(
                    padz(tiles(xface(dx, k + 1)), turn(xface(dx, k)[24:32]), turn(xface(dx, k + 2)[0:8]))
                )
            for t in range(5):
                put(x, t, z[1][t], pltpu.roll(z[0][t], 1, 0), pltpu.roll(z[2][t], 7, 0))
        for i, (k, part) in enumerate(((9, 3), (15, 2))):
            z = padz(tiles(face(part, k + 1)), turn(face(part, k)[24:32]), turn(face(part, k + 2)[0:8]))
            for t in range(5):
                edge[i, :, t * 128 : (t + 1) * 128] = z[t]
        under = face(4, 12)
        over = face(4, 14)
        for x in range(BS):
            at = slice(x % 4 * 8, x % 4 * 8 + 8)
            before = under[at] if x < 4 else turn(under[at])
            after = turn(over[at]) if x < 4 else over[at]
            z = padz([cur[x, n, :, t * 128 : (t + 1) * 128] for t in range(4)], before, after)
            for t in range(5):
                lanes = slice(t * 128, (t + 1) * 128)
                put(x + 1, t, z[t], edge[0, x : x + 1, lanes], edge[1, x : x + 1, lanes])
        return carry

    lax.fori_loop(0, NB, one, 0)


NEAR = [(-1, 0), (1, 0), (0, -1), (0, 1), (-1, -1), (-1, 1), (1, -1), (1, 1)]


class Rim:
    def __init__(self, row_out, col_out, row_in, col_in, corner_in, send, recv):
        self.row_out, self.col_out = row_out, col_out
        self.row_in, self.col_in, self.corner_in = row_in, col_in, corner_in
        self.send, self.recv = send, recv
        self.bx, self.by = place()

    def exists(self, d):
        dx, dy = NEAR[d]
        ok = None
        for v, step, size in ((self.bx, dx, NX), (self.by, dy, NY)):
            if step:
                here = v > 0 if step < 0 else v < size - 1
                ok = here if ok is None else ok & here
        return ok

    def copy(self, d):
        dx, dy = NEAR[d]
        back = NEAR.index((-dx, -dy))
        if dy == 0:
            src, dst = self.row_out.at[d], self.row_in.at[back]
        elif dx == 0:
            src, dst = self.col_out.at[d - 2], self.col_in.at[back - 2]
        else:
            src = self.row_out.at[0 if dx < 0 else 1, pl.ds(0 if dy < 0 else 16, 16)]
            dst = self.corner_in.at[back - 4]
        return remote(src, dst, self.send.at[d], self.recv.at[back], (self.bx + dx, self.by + dy))

    def landing(self, d):
        dx, dy = NEAR[d]
        if dy == 0:
            return self.row_in.at[d]
        if dx == 0:
            return self.col_in.at[d - 2]
        return self.corner_in.at[d - 4]

    def start(self, plane):
        self.row_out[0] = plane[0].astype(BF)
        self.row_out[1] = plane[ROWS - 1].astype(BF)
        self.col_out[0] = plane[:, 0, :].astype(BF)
        self.col_out[1] = plane[:, COLS - 1, :].astype(BF)
        for d in range(8):

            @pl.when(self.exists(d))
            def _(d=d):
                self.copy(d).start()

            @pl.when(jnp.logical_not(self.exists(d)))
            def _(d=d):
                at = self.landing(d)
                at[...] = jnp.zeros(at.shape, BF)

    def finish(self):
        for d in range(8):

            @pl.when(self.exists(d))
            def _(d=d):
                dx, dy = NEAR[d]
                at = self.landing(d)
                remote(at, at, self.send.at[d], self.recv.at[d], (self.bx + dx, self.by + dy)).wait_recv()

    def drain(self):
        for d in range(8):

            @pl.when(self.exists(d))
            def _(d=d):
                self.copy(d).wait_send()


def spread(plane, rim, side32, out):
    side32[0] = rim.col_in[0].astype(F32)
    side32[1] = rim.col_in[1].astype(F32)
    j = lax.broadcasted_iota(jnp.int32, (COLS, 128), 0)

    def put(at, row, left, right):
        rows = pl.ds(pl.multiple_of(at * COLS, COLS), COLS)
        out[rows, 0:128] = jnp.where(j == 0, left, pltpu.roll(row, 1, 0)).astype(BF)
        out[rows, 128:256] = row.astype(BF)
        out[rows, 256:384] = jnp.where(j == COLS - 1, right, pltpu.roll(row, COLS - 1, 0)).astype(BF)

    def inner(i, carry):
        put(i + 1, plane[i], side32[0, pl.ds(i, 1), :], side32[1, pl.ds(i, 1), :])
        return carry

    lax.fori_loop(0, ROWS, inner, 0)
    corner = [rim.corner_in[c].astype(F32) for c in range(4)]
    put(0, rim.row_in[0].astype(F32), corner[0][15:16], corner[1][0:1])
    put(ROWS + 1, rim.row_in[1].astype(F32), corner[2][15:16], corner[3][0:1])

class Spread:
    def __init__(self, src, pool, size, own_s, fwd_s, own_r):
        self.src, self.pool, self.size = src, pool, size
        self.own_s, self.fwd_s, self.own_r = own_s, fwd_s, own_r
        self.bx, self.by = place()
        self.mate = self.by + 1 - 2 * (self.by % 2)

    def at(self, src):
        return self.pool.at[pl.ds(src * self.size, self.size)]

    def first(self):
        peers = [(self.by + 2) % NY, (self.by + 6) % NY, (self.by + 4) % NY, self.mate]
        return [
            remote(self.src, self.at(self.by), self.own_s.at[k], self.own_r.at[self.by], (self.bx, peer))
            for k, peer in enumerate(peers)
        ]

    def landed(self, src, k):
        at = self.at(src)
        return remote(at, at, self.fwd_s.at[k], self.own_r.at[src], (self.bx, self.mate))

    def start(self):
        for c in self.first():
            c.start()
        self.pool[pl.ds(self.by * self.size, self.size)] = self.src[...]

    def forward(self):
        for k in (1, 3, 2):
            c = self.landed((self.by + 2 * k) % NY, k - 1)
            c.wait_recv()
            c.start()

    def finish(self):
        for k in range(4):
            self.landed((self.mate + 2 * k) % NY, 0).wait_recv()

    def drain(self):
        for c in self.first():
            c.wait_send()
        for k in (1, 2, 3):
            self.landed((self.by + 2 * k) % NY, k - 1).wait_send()


class Total:
    def __init__(self, base, half, cat, given, sums, second, ring, full, ms, mr, zs, zr, xs, xr, ws, wr, fs, fr):
        self.base, self.half, self.chunk = base, half, half // NX
        self.cat, self.given, self.sums, self.second = cat, given, sums, second
        self.ring, self.full = ring, full
        self.ms, self.mr, self.zs, self.zr, self.xs, self.xr = ms, mr, zs, zr, xs, xr
        self.ws, self.wr, self.fs, self.fr = ws, wr, fs, fr
        self.bx, self.by = place()
        self.core = self.by % 2
        self.mate = self.by + 1 - 2 * self.core
        self.chip = self.by // 2

    def rows(self, core):
        return pl.ds(pl.multiple_of(self.base + core * self.half, self.half), self.half)

    def piece(self, core, i):
        return pl.ds(pl.multiple_of(core * self.half + i * self.chunk, self.chunk), self.chunk)

    def to_mate(self):
        at = self.cat.at[self.rows(1 - self.core)]
        return remote(at, self.given, self.ms.at[0], self.mr.at[0], (self.bx, self.mate))

    def to_x(self, q):
        at = self.sums.at[pl.ds(q * self.chunk, self.chunk)]
        return remote(at, self.second.at[self.bx], self.zs.at[q], self.zr.at[self.bx], (q, self.by))

    def combine(self):
        self.to_mate().wait_recv()
        self.sums[...] = (self.cat[self.rows(self.core)].astype(F32) + self.given[...].astype(F32)).astype(BF)
        for q in range(NX):

            @pl.when(self.bx != q)
            def _(q=q):
                self.to_x(q).start()

    def to_ring(self, k):
        at = self.ring.at[self.chip]
        to = (self.by + 2 * k) % NY
        return remote(at, at, self.xs.at[k], self.xr.at[self.chip], (self.bx, to))

    def sum_x(self):
        mine = pl.ds(pl.multiple_of(self.bx * self.chunk, self.chunk), self.chunk)
        total = self.sums[mine].astype(F32)
        for k in range(1, NX):
            src = (self.bx + k) % NX
            at = self.second.at[src]
            remote(at, at, self.zs.at[0], self.zr.at[src], (src, self.by)).wait_recv()
            total = total + self.second[src].astype(F32)
        self.ring[self.chip] = total.astype(BF)
        for k in (1, 3, 2):
            self.to_ring(k).start()

    def out_x(self, k):
        at = self.full.at[self.piece(self.core, self.bx)]
        return remote(at, at, self.ws.at[k], self.wr.at[self.bx], ((self.bx + k) % NX, self.by))

    def pass_on(self, src):
        at = self.full.at[self.piece(self.core, src)]
        return remote(at, at, self.fs.at[src], self.fr.at[src], (self.bx, self.mate))

    def sum_ring(self):
        for k in range(1, 4):
            src = (self.chip + k) % 4
            at = self.ring.at[src]
            remote(at, at, self.xs.at[k], self.xr.at[src], (self.bx, src * 2 + self.core)).wait_recv()
        total = self.ring[0].astype(F32)
        for i in range(1, 4):
            total = total + self.ring[i].astype(F32)
        self.full[self.piece(self.core, self.bx)] = total.astype(BF)
        for k in range(1, NX):
            self.out_x(k).start()
        self.pass_on(self.bx).start()

    def relay(self):
        for k in range(1, NX):
            src = (self.bx + k) % NX
            at = self.full.at[self.piece(self.core, src)]
            remote(at, at, self.ws.at[k], self.wr.at[src], (src, self.by)).wait_recv()
            self.pass_on(src).start()

    def done(self):
        for src in range(NX):
            at = self.full.at[self.piece(1 - self.core, src)]
            remote(at, at, self.fs.at[src], self.fr.at[src], (self.bx, self.mate)).wait_recv()

    def drain(self):
        self.to_mate().wait_send()
        for q in range(NX):

            @pl.when(self.bx != q)
            def _(q=q):
                self.to_x(q).wait_send()

        for k in range(1, 4):
            self.to_ring(k).wait_send()
        for k in range(1, NX):
            self.out_x(k).wait_send()
        for src in range(NX):
            self.pass_on(src).wait_send()


def total_scratch(half):
    chunk = half // NX
    return [
        pltpu.VMEM((half, 128), BF),
        pltpu.VMEM((half, 128), BF),
        pltpu.VMEM((NX, chunk, 128), BF),
        pltpu.VMEM((4, chunk, 128), BF),
        pltpu.VMEM((2 * half, 128), BF),
        *[DMA((n,)) for n in (1, 1, NX, NX, 4, 4, NX, NX, NX, NX)],
    ]


def dot(a, b):
    return jnp.dot(a, b, preferred_element_type=F32)


def dot_t(a, b):
    return lax.dot_general(a, b, (((1,), (1,)), ((), ())), preferred_element_type=F32)


def window(wide, a, e, g):
    return wide[a * 32 : a * 32 + 256, e * 640 + g * 128 : e * 640 + g * 128 + 256]


def whole(
    vox_h, conv_w_h, fold_w_h, map_w_h, cot_h, conv_b, fold_b, map_b, coords, neighbors,
    bev_far, feat_far, conv_far, fold_far, map_far,
    bev_out, feat_out, conv_out, fold_out, map_out, out_sem,
    vox, conv_w, fold_w, map_w, cot, load_sem,
    cur, shifted, edge, toep, toep_back, wide, pre, act, fold_both, part, part_pool,
    code, codes_v, codes, table,
    fold, plane, gplane, spread_mid, spread_grad, side32, slots, ready, back,
    split, cur_bf, cat, early_part, late_part,
    face_a, face_f, part_sems, code_s, code_r, code_l,
    row_out, col_out, row_in, col_in, corner_in, rim_s, rim_r, back_s, back_r,
):
    bx, by = place()
    greet()
    stores = [
        pltpu.make_async_copy(src, dst, out_sem.at[i])
        for i, (src, dst) in enumerate(
            ((bev_out, bev_far), (feat_out, feat_far), (conv_out, conv_far), (fold_out, fold_far), (map_out, map_far))
        )
    ]
    early = Total(0, 1024, cat, *early_part)
    late = Total(2048, 512, cat, *late_part)
    core = by % 2
    loads = [
        pltpu.make_async_copy(src, dst, load_sem.at[i])
        for i, (src, dst) in enumerate(
            ((vox_h, vox), (conv_w_h, conv_w), (fold_w_h, fold_w), (map_w_h, map_w), (cot_h, cot))
        )
    ]
    for c in loads:
        c.start()
    lane = lax.broadcasted_iota(jnp.int32, (8, 128), 1)
    tile = jnp.zeros((8, 128), jnp.int32)
    for n in range(NB):
        number = ((coords[0, n] - bx * TR) * (TC * NY) + coords[1, n]) * 2 + coords[2, n]
        tile = jnp.where(lane == n, number, tile)
    code[...] = tile
    codes_v[by] = tile
    loads[0].wait()
    for n in range(NB):
        cur[:, n] = vox[n].astype(F32)
    faces = Faces(*face_a)
    pack_faces(cur, faces.msg, coords)
    met()
    tell = [
        remote(code, codes_v.at[by], code_s.at[k], code_r.at[by], (bx, (by + k) % NY)) for k in range(1, NY)
    ]
    for c in tell:
        c.start()
    faces.start()
    back_faces = Faces(*face_f)
    for f in (faces, back_faces):
        f.pool[GROUP] = jnp.zeros((5, 32, 128), BF)
        for to in range(2):
            f.side[to, GROUP] = jnp.zeros((32, 128), BF)
    loads[1].wait()
    blank = jnp.zeros((64, 64), F32)

    def build(tap, carry):
        w = [conv_w[tap * 3 + k].astype(F32) for k in range(3)]
        ahead = [blank, *w, blank]
        for z in range(4):
            toep[tap, z * 64 : (z + 1) * 64, :] = jnp.concatenate([ahead[z + 1], ahead[z]], 1).astype(BF)
        rows = ((w[2], w[1], w[0], blank), (blank, w[2], w[1], w[0]))
        for z in range(2):
            for half in range(2):
                pair = jnp.concatenate(rows[z][half * 2 : half * 2 + 2], 1)
                toep_back[tap, z * 64 : (z + 1) * 64, half * 128 : (half + 1) * 128] = pair.astype(BF)
        return carry

    lax.fori_loop(0, 9, build, 0)
    for k in range(1, NY):
        src = (by + k) % NY
        remote(code, codes_v.at[src], code_s.at[k], code_r.at[src], (bx, src)).wait_recv()
    to_scalar = pltpu.make_async_copy(codes_v.at[:, 0], codes, code_l.at[0])
    to_scalar.start()
    to_scalar.wait()

    def look(s, carry):
        want = ((s // (TC * 2)) * (TC * NY) + by * TC + (s // 2) % TC) * 2 + s % 2
        found = jnp.int32(GROUP)
        for b in range(GROUP):
            found = jnp.where(codes[b // NB, b % NB] == want, b, found)
        table[s] = found
        return carry

    lax.fori_loop(0, TR * TC * 2, look, 0)
    faces.forward()
    faces.finish()
    assemble(cur, faces.pool, faces.side, neighbors, shifted, edge)
    for e in range(3):
        wide[:, e * 640 : (e + 1) * 640] = shifted[e].astype(BF)
    for group in range(4):
        total = jnp.concatenate([conv_b[...], conv_b[...]], 1)
        for a in range(3):
            for e in range(3):
                total = total + dot(window(wide, a, e, group), toep[a * 3 + e])
        lanes = slice(group * 128, (group + 1) * 128)
        pre[:, lanes] = total
        act[:, lanes] = (total * jax.nn.sigmoid(total)).astype(BF)
    loads[2].wait()
    for h in range(2):
        fold_both[:, :, :, h * 128 : (h + 1) * 128] = dot(act[...], fold_w[h]).reshape(BS, NB, BS, 128)
    for n in range(NB):
        high = coords[2, n].astype(F32)
        one = fold_both[:, n, :, 0:128] * (1.0 - high) + fold_both[:, n, :, 128:256] * high
        part[n] = one.reshape(64, 128).astype(BF)
    parts = Spread(part, part_pool, NB, *part_sems)
    parts.start()
    loads[3].wait()
    loads[4].wait()
    parts.forward()
    parts.finish()

    rims = [
        Rim(row_out.at[p], col_out.at[p], row_in.at[p], col_in.at[p], corner_in.at[p], rim_s.at[p], rim_r.at[p])
        for p in range(2)
    ]
    for r in range(TR):
        for c in range(TC):
            total = fold_b[...]
            for h in range(2):
                at = table[(r * TC + c) * 2 + h]
                here = (at < GROUP).astype(F32)
                total = total + part_pool[jnp.minimum(at, GROUP - 1)].astype(F32) * here
            where = (slice(r * BS, (r + 1) * BS), slice(c * BS, (c + 1) * BS))
            fold[where] = total.reshape(BS, BS, 128)
            plane[where] = rounded(total * jax.nn.sigmoid(total)).reshape(BS, BS, 128)
    rims[0].start(plane)
    rims[0].finish()
    spread(plane, rims[0], side32, spread_mid)

    def ahead(i, carry):
        start = pl.multiple_of(i * 256, 256)
        total = map_b[...]
        for a in range(3):
            total = total + dot(spread_mid[pl.ds(start + a * COLS, 256), :], map_w[a])
        bev_out[pl.ds(i * BS, BS)] = (total * jax.nn.sigmoid(total)).reshape(BS, COLS, 128).astype(BF)
        g = cot[pl.ds(i * BS, BS)].astype(F32).reshape(256, 128) * slope(total)
        gplane[pl.ds(i * BS, BS)] = rounded(g).reshape(BS, COLS, 128)
        return carry

    lax.fori_loop(0, TR, ahead, 0)
    stores[0].start()
    rims[1].start(gplane)
    turned = gplane[...].reshape(ROWS * COLS, 128).T.astype(BF)
    for a in range(3):
        got = dot(turned, spread_mid[a * COLS : a * COLS + ROWS * COLS, :])
        for e in range(3):
            t = a * 3 + e
            row = t * 128 if t < 8 else 2048
            cat[row : row + 128] = got[:, e * 128 : (e + 1) * 128].T.astype(BF)


    @pl.when(core == 1)
    def _():
        early.to_mate().start()

    rims[1].finish()
    spread(gplane, rims[1], side32, spread_grad)

    def behind(i, carry):
        start = pl.multiple_of(i * 256, 256)
        total = None
        for a in range(3):
            for e in range(3):
                lhs = spread_grad[pl.ds(start + a * COLS, 256), e * 128 : (e + 1) * 128]
                one = dot_t(lhs, map_w[2 - a, (2 - e) * 128 : (3 - e) * 128, :])
                total = one if total is None else total + one
        grad = (total * slope(fold[pl.ds(i * BS, BS)].reshape(256, 128))).reshape(BS, COLS, 128)
        for c in range(TC):
            slots[i * TC + c] = grad[:, c * BS : (c + 1) * BS, :].reshape(64, 128).astype(BF)
        return carry

    lax.fori_loop(0, TR, behind, 0)

    def fill(b, carry):
        number = codes[b // NB, b % NB] // 2
        c = number % (TC * NY) - by * TC
        at = number // (TC * NY) * TC + jnp.clip(c, 0, TC - 1)
        ready[b] = slots[jnp.clip(at, 0, TR * TC - 1)]
        return carry

    lax.fori_loop(0, GROUP, fill, 0)
    give = [
        remote(
            ready.at[pl.ds((by + k) % NY * NB, NB)],
            back.at[by],
            back_s.at[k],
            back_r.at[by],
            (bx, (by + k) % NY),
        )
        for k in (4, 3, 5, 2, 6, 1, 7)
    ]
    for c in give:
        c.start()
    back[by] = ready[pl.ds(by * NB, NB)]
    pl.when(core == 0)(early.combine)
    for k in range(1, NY):
        src = (by + k) % NY
        remote(ready.at[pl.ds(0, NB)], back.at[src], back_s.at[k], back_r.at[src], (bx, src)).wait_recv()

    for n in range(NB):
        high = coords[2, n].astype(F32)
        mine = back[jnp.clip(coords[1, n] // TC, 0, NY - 1), n].astype(F32).reshape(BS, BS, 128)
        split[:, n, :, 0:128] = mine * (1.0 - high)
        split[:, n, :, 128:256] = mine * high
    both = split[...].reshape(256, 256)
    act_grad = None
    for h in range(2):
        one = dot_t(both[:, h * 128 : (h + 1) * 128].astype(BF), fold_w[h])
        act_grad = one if act_grad is None else act_grad + one
    grad = rounded(rounded(act_grad) * slope(pre[...]))
    cur[...] = grad.reshape(BS, NB, BS, 512)
    cur_bf[...] = grad.astype(BF)
    pack_faces(cur, back_faces.msg, coords)
    back_faces.start()
    got = dot(both.T.astype(BF), act[...])
    for h in range(2):
        cat[1024 + h * 512 : 1024 + (h + 1) * 512] = got[h * 128 : (h + 1) * 128].T.astype(BF)

    @pl.when(core == 0)
    def _():
        early.to_mate().start()

    turned = [cur_bf[:, g * 128 : (g + 1) * 128].astype(F32).T.astype(BF) for g in range(4)]
    low = lax.broadcasted_iota(jnp.int32, (96, 128), 1) < 64
    for a in range(3):
        for e in range(3):
            total = None
            for g in range(4):
                one = dot(turned[g], window(wide, a, e, g))
                total = one if total is None else total + one
            total = total.T
            summed_z = total[0:192] + pltpu.roll(total[64:256], 64, 1)
            row = 2176 + (a * 3 + e) * 96
            cat[row : row + 96] = jnp.where(
                low, summed_z[0:96], pltpu.roll(summed_z[96:192], 64, 1)
            ).astype(BF)
    cat[3040:3072] = jnp.zeros((32, 128), BF)
    late.to_mate().start()
    pl.when(core == 1)(early.combine)
    late.combine()
    early.sum_x()
    late.sum_x()
    early.sum_ring()
    back_faces.forward()
    late.sum_ring()
    back_faces.finish()
    assemble(cur, back_faces.pool, back_faces.side, neighbors, shifted, edge)
    for e in range(3):
        wide[:, e * 640 : (e + 1) * 640] = shifted[e].astype(BF)
    for g in range(4):
        total = None
        for a in range(3):
            for e in range(3):
                one = dot_t(window(wide, a, e, g), toep_back[(2 - a) * 3 + 2 - e])
                total = one if total is None else total + one
        view = total.reshape(BS, NB, BS, 128)
        for n in range(NB):
            feat_out[n, :, :, g * 128 : (g + 1) * 128] = view[:, n]
    stores[1].start()
    early.relay()
    late.relay()
    early.done()
    for h in range(2):
        fold_out[h] = early.full[1024 + h * 512 : 1024 + (h + 1) * 512].astype(F32)
    stores[3].start()
    for t in range(8):
        map_out[t] = early.full[t * 128 : (t + 1) * 128].astype(F32)
    late.done()
    map_out[8] = late.full[0:128].astype(F32)
    stores[4].start()
    for t in range(9):
        v = late.full[128 + t * 96 : 128 + (t + 1) * 96].astype(F32)
        conv_out[t, 0:96] = v[:, 0:64]
        conv_out[t, 96:192] = v[:, 64:128]
    stores[2].start()

    for c in tell + give:
        c.wait_send()
    faces.drain()
    back_faces.drain()
    parts.drain()
    for rim in rims:
        rim.drain()
    early.drain()
    late.drain()
    for c in stores:
        c.wait()


def hand_on(*refs):
    given, results, held, sems = refs[:5], refs[5:10], refs[10:15], refs[15]
    takes = [pltpu.make_async_copy(a, b, sems.at[0, i]) for i, (a, b) in enumerate(zip(given, held, strict=True))]
    gives = [pltpu.make_async_copy(a, b, sems.at[1, i]) for i, (a, b) in enumerate(zip(held, results, strict=True))]
    for c in takes:
        c.start()
    for take, give in zip(takes, gives, strict=True):
        take.wait()
        give.start()
    for c in gives:
        c.wait()


def body(vox_feats, block_coords, neighbors, conv_w, conv_b, fold_w, fold_b, map_w, map_b, cotangent):
    far = pl.BlockSpec(memory_space=pl.ANY)
    outs = [
        jax.ShapeDtypeStruct((ROWS, COLS, 128), BF),
        jax.ShapeDtypeStruct((NB, BS, BS, 512), F32),
        jax.ShapeDtypeStruct((9, 192, 64), F32),
        jax.ShapeDtypeStruct((2, 512, 128), F32),
        jax.ShapeDtypeStruct((9, 128, 128), F32),
    ]
    made = pl.pallas_call(
        whole,
        in_specs=[far] * 5 + [VMEM] * 3 + [SMEM] * 2,
        out_specs=[far] * 5,
        out_shape=outs,
        scratch_shapes=[
            *[pltpu.VMEM(o.shape, o.dtype) for o in outs],
            DMA((5,)),
            pltpu.VMEM((NB, BS, BS, 512), BF),
            pltpu.VMEM((27, 64, 64), BF),
            pltpu.VMEM((2, 512, 128), BF),
            pltpu.VMEM((3, 384, 128), BF),
            pltpu.VMEM((ROWS, COLS, 128), BF),
            DMA((5,)),
            pltpu.VMEM((BS, NB, BS, 512), F32),
            pltpu.VMEM((3, 320, 640), F32),
            pltpu.VMEM((2, 8, 640), F32),
            pltpu.VMEM((9, 256, 128), BF),
            pltpu.VMEM((9, 128, 256), BF),
            pltpu.VMEM((320, 1920), BF),
            pltpu.VMEM((256, 512), F32),
            pltpu.VMEM((256, 512), BF),
            pltpu.VMEM((BS, NB, BS, 256), F32),
            pltpu.VMEM((NB, 64, 128), BF),
            pltpu.VMEM((GROUP, 64, 128), BF),
            pltpu.VMEM((8, 128), jnp.int32),
            pltpu.VMEM((NY, 8, 128), jnp.int32),
            pltpu.SMEM((NY, 128), jnp.int32),
            pltpu.SMEM((TR * TC * 2,), jnp.int32),
            pltpu.VMEM((ROWS, COLS, 128), F32),
            pltpu.VMEM((ROWS, COLS, 128), F32),
            pltpu.VMEM((ROWS, COLS, 128), F32),
            pltpu.VMEM(((ROWS + 2) * COLS, 384), BF),
            pltpu.VMEM(((ROWS + 2) * COLS, 384), BF),
            pltpu.VMEM((2, ROWS, 128), F32),
            pltpu.VMEM((TR * TC, 64, 128), BF),
            pltpu.VMEM((GROUP, 64, 128), BF),
            pltpu.VMEM((NY, NB, 64, 128), BF),
            pltpu.VMEM((BS, NB, BS, 256), F32),
            pltpu.VMEM((256, 512), BF),
            pltpu.VMEM((CAT, 128), BF),
            total_scratch(1024),
            total_scratch(512),
            FACE_SCRATCH,
            FACE_SCRATCH,
            [DMA((4,)), DMA((3,)), DMA((NY,))],
            DMA((NY,)),
            DMA((NY,)),
            DMA((1,)),
            pltpu.VMEM((2, 2, COLS, 128), BF),
            pltpu.VMEM((2, 2, ROWS, 128), BF),
            pltpu.VMEM((2, 2, COLS, 128), BF),
            pltpu.VMEM((2, 2, ROWS, 128), BF),
            pltpu.VMEM((2, 4, 16, 128), BF),
            DMA((2, 8)),
            DMA((2, 8)),
            DMA((NY,)),
            DMA((NY,)),
        ],
        compiler_params=pltpu.CompilerParams(
            collective_id=1, has_side_effects=True, vmem_limit_bytes=58 * 2**20
        ),
    )(
        vox_feats,
        conv_w.reshape(27, 64, 64),
        fold_w.reshape(2, 512, 128),
        map_w.reshape(3, 384, 128),
        cotangent,
        conv_b[None],
        fold_b[None],
        map_b[None],
        block_coords,
        neighbors.T,
    )
    bev_map, feat_grad, conv_grads, fold_grads, map_grads = pl.pallas_call(
        hand_on,
        in_specs=[far] * 5,
        out_specs=[far] * 5,
        out_shape=outs,
        scratch_shapes=[*[pltpu.VMEM(o.shape, o.dtype) for o in outs], DMA((2, 5))],
        compiler_params=pltpu.CompilerParams(vmem_limit_bytes=58 * 2**20),
    )(*made)
    return (
        bev_map,
        feat_grad,
        conv_grads.reshape(3, 3, 3, 64, 64),
        fold_grads.reshape(1024, 128),
        map_grads.reshape(3, 3, 128, 128),
    )


def solution(mesh):
    placed = (
        P(("bx", "by"), None, None, None),
        P(None, ("bx", "by")),
        P(None, ("bx", "by")),
        P(),
        P(),
        P(),
        P(),
        P(),
        P(),
        P("bx", "by", None),
    )
    return jax.shard_map(
        body,
        mesh=mesh,
        in_specs=placed,
        out_specs=(P("bx", "by", None), P(("bx", "by"), None, None, None), P(), P(), P()),
        check_vma=False,
    )
```

```python
import functools

import jax
import jax.numpy as jnp
from jax import lax
from jax.experimental import pallas as pl
from jax.experimental.pallas import tpu as pltpu
from jax.sharding import PartitionSpec as P

MESH = pl.DeviceIdType.MESH
BF = jnp.bfloat16
F32 = jnp.float32
BS = 8
TR = 6
TC = 4
NB = 4
NX = 16
NY = 8
GROUP = NB * NY
ROWS = TR * BS
COLS = TC * BS
VMEM = pl.BlockSpec(memory_space=pltpu.VMEM)
SMEM = pl.BlockSpec(memory_space=pltpu.SMEM)
DMA = pltpu.SemaphoreType.DMA
CAT = 3072


def place():
    return lax.axis_index("bx"), lax.axis_index("by")


def remote(src, dst, send, recv, device):
    return pltpu.make_async_remote_copy(
        src_ref=src,
        dst_ref=dst,
        send_sem=send,
        recv_sem=recv,
        device_id=device,
        device_id_type=MESH,
    )


def signal(device):
    pl.semaphore_signal(
        pltpu.get_barrier_semaphore(), inc=1, device_id=device, device_id_type=MESH
    )


def slope(pre):
    s = jax.nn.sigmoid(pre)
    return s * (1.0 + pre * (1.0 - s))


def rounded(v):
    return v.astype(BF).astype(F32)


def partners():
    bx, by = place()
    core = by % 2
    out = [(None, (bx, (by + k) % NY)) for k in range(1, NY)]
    out += [(None, ((bx + k) % NX, by)) for k in range(1, NX)]
    for step in (-1, 1):
        inside = bx > 0 if step < 0 else bx < NX - 1
        out += [(inside, (bx + step, core + 2 * j)) for j in range(NY // 2)]
        out.append((inside & (by > 0), (bx + step, by - 1)))
        out.append((inside & (by < NY - 1), (bx + step, by + 1)))
    return out


def greet():
    for ok, device in partners():
        if ok is None:
            signal(device)
        else:
            pl.when(ok)(functools.partial(signal, device))


def met():
    count = jnp.int32(0)
    for ok, _ in partners():
        count = count + (1 if ok is None else ok.astype(jnp.int32))
    pl.semaphore_wait(pltpu.get_barrier_semaphore(), count)


def pack_faces(cur, msg, coords):
    lane = lax.broadcasted_iota(jnp.int32, (32, 128), 1)

    def flat(v):
        return jnp.concatenate([v[:, t * 128 : (t + 1) * 128] for t in range(4)], 0)

    def one(n, carry):
        high = coords[2, n].astype(F32)
        msg[n, 0] = flat(cur[0, n]).astype(BF)
        msg[n, 1] = flat(cur[7, n]).astype(BF)
        msg[n, 2] = flat(cur[:, n, 0, :]).astype(BF)
        msg[n, 3] = flat(cur[:, n, 7, :]).astype(BF)
        top = cur[:, n, :, 384:512].reshape(64, 128)
        low = cur[:, n, :, 0:128].reshape(64, 128)
        face = pltpu.roll(top, 64, 1) * (1.0 - high) + low * high
        msg[n, 4] = jnp.where(lane < 64, face[0:32], pltpu.roll(face[32:64], 64, 1)).astype(BF)
        return carry

    lax.fori_loop(0, NB, one, 0)


class Stream:
    def __init__(self, src, pool, step, out_s, in_r):
        self.src, self.pool, self.step = src, pool, step
        self.out_s, self.in_r = out_s, in_r
        self.bx, self.by = place()
        self.mate = self.by + 1 - 2 * (self.by % 2)
        if step:
            self.kinds = [(6, None), (2, None), (0, None), (4, 0), (4, 1)]
            self.sends = self.bx > 0 if step < 0 else self.bx < NX - 1
            self.takes = self.bx < NX - 1 if step < 0 else self.bx > 0
        else:
            self.kinds = [(6, 0), (2, 1), (6, 1), (2, 0), (4, 0), (4, 1)]

    def view(self, origin, half):
        if half is None:
            return self.pool.at[pl.ds(origin * NB, NB)]
        return self.pool.at[pl.ds(origin * NB + half * (NB // 2), NB // 2)]

    def when(self, ok, run):
        if self.step:
            pl.when(ok)(run)
        else:
            run()

    def copy(self, src, origin, half, sem, kind, device):
        got = self.in_r.at[7 if kind is None else self.kinds.index(kind)]
        return remote(src, self.view(origin, half), self.out_s.at[sem], got, device)

    def start(self):
        def run():
            for off, half in self.kinds:
                if off == 4:
                    continue
                src = self.src if half is None else self.src.at[pl.ds(half * (NB // 2), NB // 2)]
                to = (self.bx + self.step, (self.by + 8 - off) % NY)
                self.copy(src, self.by, half, 0, (off, half), to).start()
            if not self.step:
                self.copy(self.src, self.by, None, 0, None, (self.bx, self.mate)).start()

        self.when(self.sends if self.step else None, run)

    def take(self, far):
        def run():
            for off, half in self.kinds:
                if (off == 4) != far:
                    continue
                origin = (self.by + off) % NY
                at = self.view(origin, half)
                to_mate = self.copy(at, origin, half, 1, None, (self.bx, self.mate))
                self.copy(at, origin, half, 1, (off, half), (self.bx, self.mate)).wait_recv()
                part = 0 if off == 6 else 1
                if off in (2, 6) and half in (None, part):
                    piece = self.view(origin, part)
                    to = (self.bx, (self.by + 8 - off) % NY)
                    self.copy(piece, origin, part, 1, (4, part), to).start()
                to_mate.start()

        self.when(self.takes if self.step else None, run)

    def bytes_of(self, messages, sem):
        at = self.pool.at[pl.ds(0, messages * NB)]
        return remote(at, at, self.out_s.at[sem], self.in_r.at[7], (self.bx, self.mate))

    def finish(self):
        self.when(self.takes if self.step else None, lambda: self.bytes_of(4, 1).wait_recv())

    def drain(self):
        self.when(self.sends if self.step else None, lambda: self.bytes_of(3, 0).wait_send())
        passed = 5 if self.step else 4
        self.when(self.takes if self.step else None, lambda: self.bytes_of(passed, 1).wait_send())


STREAM_SEMS = [DMA((2,)), DMA((8,))]


class Faces:
    def __init__(self, msg, pool, side, own, before, after):
        self.msg, self.pool, self.side = msg, pool, side
        self.by = place()[1]
        self.streams = [
            Stream(msg, pool, 0, *own),
            Stream(msg.at[:, 1], side.at[0], 1, *before),
            Stream(msg.at[:, 0], side.at[1], -1, *after),
        ]

    def start(self):
        for x in self.streams:
            x.start()
        self.pool[pl.ds(self.by * NB, NB)] = self.msg[...]

    def forward(self):
        for far in (False, True):
            for x in self.streams:
                x.take(far)

    def finish(self):
        for x in self.streams:
            x.finish()

    def drain(self):
        for x in self.streams:
            x.drain()


FACE_SCRATCH = [
    pltpu.VMEM((NB, 5, 32, 128), BF),
    pltpu.VMEM((GROUP + 1, 5, 32, 128), BF),
    pltpu.VMEM((2, GROUP + 1, 32, 128), BF),
    STREAM_SEMS,
    STREAM_SEMS,
    STREAM_SEMS,
]


def assemble(cur, pool, side, neighbors, shifted, edge):
    low = lax.broadcasted_iota(jnp.int32, (8, 128), 1) < 64
    sub = lax.broadcasted_iota(jnp.int32, (8, 128), 0)

    bx, _ = place()

    def one(n, carry):
        def spot(k, group):
            at = neighbors[n, k]
            from_group = at - group * GROUP
            ok = (at >= 0) & (from_group >= 0) & (from_group < GROUP)
            return jnp.where(ok, from_group, GROUP)

        def face(part, k):
            return pool[spot(k, bx), part].astype(F32)

        def xface(dx, k):
            near = face(1 if dx < 0 else 0, k)
            return near + side[0 if dx < 0 else 1, spot(k, bx + dx)].astype(F32)

        def tiles(v):
            return [v[t * 8 : (t + 1) * 8] for t in range(4)]

        def turn(v):
            return pltpu.roll(v, 64, 1)

        def padz(core, before, after):
            r = [turn(t) for t in core]
            return (
                [jnp.where(low, before, r[0])]
                + [jnp.where(low, r[t - 1], r[t]) for t in (1, 2, 3)]
                + [jnp.where(low, r[3], after)]
            )

        def put(x, t, mid, above, below):
            row = pl.multiple_of((x * NB + n) * 8, 8)
            at = (pl.ds(row, 8), pl.ds(t * 128, 128))
            shifted[(1, *at)] = mid
            shifted[(0, *at)] = jnp.where(sub == 0, above, pltpu.roll(mid, 1, 0))
            shifted[(2, *at)] = jnp.where(sub == 7, below, pltpu.roll(mid, 7, 0))

        for x, dx in ((0, -1), (9, 1)):
            z = []
            for dy in range(3):
                k = 9 * (dx + 1) + 3 * dy
                z.append(
                    padz(tiles(xface(dx, k + 1)), turn(xface(dx, k)[24:32]), turn(xface(dx, k + 2)[0:8]))
                )
            for t in range(5):
                put(x, t, z[1][t], pltpu.roll(z[0][t], 1, 0), pltpu.roll(z[2][t], 7, 0))
        for i, (k, part) in enumerate(((9, 3), (15, 2))):
            z = padz(tiles(face(part, k + 1)), turn(face(part, k)[24:32]), turn(face(part, k + 2)[0:8]))
            for t in range(5):
                edge[i, :, t * 128 : (t + 1) * 128] = z[t]
        under = face(4, 12)
        over = face(4, 14)
        for x in range(BS):
            at = slice(x % 4 * 8, x % 4 * 8 + 8)
            before = under[at] if x < 4 else turn(under[at])
            after = turn(over[at]) if x < 4 else over[at]
            z = padz([cur[x, n, :, t * 128 : (t + 1) * 128] for t in range(4)], before, after)
            for t in range(5):
                lanes = slice(t * 128, (t + 1) * 128)
                put(x + 1, t, z[t], edge[0, x : x + 1, lanes], edge[1, x : x + 1, lanes])
        return carry

    lax.fori_loop(0, NB, one, 0)


NEAR = [(-1, 0), (1, 0), (0, -1), (0, 1), (-1, -1), (-1, 1), (1, -1), (1, 1)]


class Rim:
    def __init__(self, row_out, col_out, row_in, col_in, corner_in, send, recv):
        self.row_out, self.col_out = row_out, col_out
        self.row_in, self.col_in, self.corner_in = row_in, col_in, corner_in
        self.send, self.recv = send, recv
        self.bx, self.by = place()

    def exists(self, d):
        dx, dy = NEAR[d]
        ok = None
        for v, step, size in ((self.bx, dx, NX), (self.by, dy, NY)):
            if step:
                here = v > 0 if step < 0 else v < size - 1
                ok = here if ok is None else ok & here
        return ok

    def copy(self, d):
        dx, dy = NEAR[d]
        back = NEAR.index((-dx, -dy))
        if dy == 0:
            src, dst = self.row_out.at[d], self.row_in.at[back]
        elif dx == 0:
            src, dst = self.col_out.at[d - 2], self.col_in.at[back - 2]
        else:
            src = self.row_out.at[0 if dx < 0 else 1, pl.ds(0 if dy < 0 else 16, 16)]
            dst = self.corner_in.at[back - 4]
        return remote(src, dst, self.send.at[d], self.recv.at[back], (self.bx + dx, self.by + dy))

    def landing(self, d):
        dx, dy = NEAR[d]
        if dy == 0:
            return self.row_in.at[d]
        if dx == 0:
            return self.col_in.at[d - 2]
        return self.corner_in.at[d - 4]

    def start(self, plane):
        self.row_out[0] = plane[0].astype(BF)
        self.row_out[1] = plane[ROWS - 1].astype(BF)
        self.col_out[0] = plane[:, 0, :].astype(BF)
        self.col_out[1] = plane[:, COLS - 1, :].astype(BF)
        for d in range(8):

            @pl.when(self.exists(d))
            def _(d=d):
                self.copy(d).start()

            @pl.when(jnp.logical_not(self.exists(d)))
            def _(d=d):
                at = self.landing(d)
                at[...] = jnp.zeros(at.shape, BF)

    def finish(self):
        for d in range(8):

            @pl.when(self.exists(d))
            def _(d=d):
                dx, dy = NEAR[d]
                at = self.landing(d)
                remote(at, at, self.send.at[d], self.recv.at[d], (self.bx + dx, self.by + dy)).wait_recv()

    def drain(self):
        for d in range(8):

            @pl.when(self.exists(d))
            def _(d=d):
                self.copy(d).wait_send()


def spread(plane, rim, side32, out):
    side32[0] = rim.col_in[0].astype(F32)
    side32[1] = rim.col_in[1].astype(F32)
    j = lax.broadcasted_iota(jnp.int32, (COLS, 128), 0)

    def put(at, row, left, right):
        rows = pl.ds(pl.multiple_of(at * COLS, COLS), COLS)
        out[rows, 0:128] = jnp.where(j == 0, left, pltpu.roll(row, 1, 0)).astype(BF)
        out[rows, 128:256] = row.astype(BF)
        out[rows, 256:384] = jnp.where(j == COLS - 1, right, pltpu.roll(row, COLS - 1, 0)).astype(BF)

    def inner(i, carry):
        put(i + 1, plane[i], side32[0, pl.ds(i, 1), :], side32[1, pl.ds(i, 1), :])
        return carry

    lax.fori_loop(0, ROWS, inner, 0)
    corner = [rim.corner_in[c].astype(F32) for c in range(4)]
    put(0, rim.row_in[0].astype(F32), corner[0][15:16], corner[1][0:1])
    put(ROWS + 1, rim.row_in[1].astype(F32), corner[2][15:16], corner[3][0:1])

class Total:
    def __init__(self, base, half, cat, given, sums, second, ring, full, sems):
        self.base, self.half, self.chunk = base, half, half // NX
        self.cat, self.given, self.sums, self.second = cat, given, sums, second
        self.ring, self.full = ring, full
        self.sems = sems
        self.bx, self.by = place()
        self.core = self.by % 2
        self.mate = self.by + 1 - 2 * self.core
        self.chip = self.by // 2

    def rows(self, core):
        return pl.ds(pl.multiple_of(self.base + core * self.half, self.half), self.half)

    def piece(self, core, i):
        return pl.ds(pl.multiple_of(core * self.half + i * self.chunk, self.chunk), self.chunk)

    def to_mate(self):
        at = self.cat.at[self.rows(1 - self.core)]
        return remote(at, self.given, self.sems.at[0], self.sems.at[1], (self.bx, self.mate))

    def all_of(self, at, stage):
        return remote(at, at, self.sems.at[2 * stage], self.sems.at[2 * stage + 1], (self.bx, self.mate))

    def combine(self):
        self.to_mate().wait_recv()
        self.sums[...] = (self.cat[self.rows(self.core)].astype(F32) + self.given[...].astype(F32)).astype(BF)
        for q in range(NX):

            @pl.when(self.bx != q)
            def _(q=q):
                at = self.sums.at[pl.ds(q * self.chunk, self.chunk)]
                remote(at, self.second.at[self.bx], self.sems.at[2], self.sems.at[3], (q, self.by)).start()

    def sum_x(self):
        self.all_of(self.second.at[pl.ds(0, NX - 1)], 1).wait_recv()
        mine = pl.ds(pl.multiple_of(self.bx * self.chunk, self.chunk), self.chunk)
        total = self.sums[mine].astype(F32)
        for k in range(1, NX):
            total = total + self.second[(self.bx + k) % NX].astype(F32)
        self.ring[self.chip] = total.astype(BF)
        at = self.ring.at[self.chip]
        for k in (1, 3, 2):
            to = (self.bx, (self.by + 2 * k) % NY)
            remote(at, at, self.sems.at[4], self.sems.at[5], to).start()

    def sum_ring(self):
        self.all_of(self.ring.at[pl.ds(0, 3)], 2).wait_recv()
        total = self.ring[0].astype(F32)
        for i in range(1, 4):
            total = total + self.ring[i].astype(F32)
        self.full[self.piece(self.core, self.bx)] = total.astype(BF)
        at = self.full.at[self.piece(self.core, self.bx)]
        for k in range(1, NX):
            remote(at, at, self.sems.at[6], self.sems.at[7], ((self.bx + k) % NX, self.by)).start()

    def share(self):
        at = self.full.at[pl.ds(pl.multiple_of(self.core * self.half, self.half), self.half)]
        return remote(at, at, self.sems.at[8], self.sems.at[9], (self.bx, self.mate))

    def relay(self):
        self.all_of(self.full.at[pl.ds(0, (NX - 1) * self.chunk)], 3).wait_recv()
        self.share().start()

    def done(self):
        self.share().wait_recv()

    def drain(self):
        self.to_mate().wait_send()
        self.all_of(self.second.at[pl.ds(0, NX - 1)], 1).wait_send()
        self.all_of(self.ring.at[pl.ds(0, 3)], 2).wait_send()
        self.all_of(self.full.at[pl.ds(0, (NX - 1) * self.chunk)], 3).wait_send()
        self.share().wait_send()


def total_scratch(half):
    chunk = half // NX
    return [
        pltpu.VMEM((half, 128), BF),
        pltpu.VMEM((half, 128), BF),
        pltpu.VMEM((NX, chunk, 128), BF),
        pltpu.VMEM((4, chunk, 128), BF),
        pltpu.VMEM((2 * half, 128), BF),
        DMA((10,)),
    ]


def dot(a, b):
    return jnp.dot(a, b, preferred_element_type=F32)


def dot_t(a, b):
    return lax.dot_general(a, b, (((1,), (1,)), ((), ())), preferred_element_type=F32)


def window(wide, a, e, g):
    return wide[a * 32 : a * 32 + 256, e * 640 + g * 128 : e * 640 + g * 128 + 256]


def whole(
    vox_h, conv_w_h, fold_w_h, map_w_h, cot_h, conv_b, fold_b, map_b, coords, neighbors,
    bev_far, feat_far, conv_far, fold_far, map_far,
    bev_out, feat_out, conv_out, fold_out, map_out, out_sem,
    vox, conv_w, fold_w, map_w, cot, load_sem,
    cur, shifted, edge, toep, toep_back, wide, pre, act, fold_both, part, part_pool,
    code, codes_v, codes, table,
    fold, plane, gplane, spread_mid, spread_grad, side32, slots, ready, back,
    split, cur_bf, cat, early_part, late_part,
    face_a, face_f, part_sems, code_s, code_r, code_l,
    row_out, col_out, row_in, col_in, corner_in, rim_s, rim_r, back_s, back_r,
):
    bx, by = place()
    greet()
    stores = [
        pltpu.make_async_copy(src, dst, out_sem.at[i])
        for i, (src, dst) in enumerate(
            ((bev_out, bev_far), (feat_out, feat_far), (conv_out, conv_far), (fold_out, fold_far), (map_out, map_far))
        )
    ]
    early = Total(0, 1024, cat, *early_part)
    late = Total(2048, 512, cat, *late_part)
    core = by % 2
    loads = [
        pltpu.make_async_copy(src, dst, load_sem.at[i])
        for i, (src, dst) in enumerate(
            ((vox_h, vox), (conv_w_h, conv_w), (fold_w_h, fold_w), (map_w_h, map_w), (cot_h, cot))
        )
    ]
    for c in loads:
        c.start()
    lane = lax.broadcasted_iota(jnp.int32, (8, 128), 1)
    tile = jnp.zeros((8, 128), jnp.int32)
    for n in range(NB):
        number = ((coords[0, n] - bx * TR) * (TC * NY) + coords[1, n]) * 2 + coords[2, n]
        tile = jnp.where(lane == n, number, tile)
    code[...] = tile
    codes_v[by] = tile
    loads[0].wait()
    for n in range(NB):
        cur[:, n] = vox[n].astype(F32)
    faces = Faces(*face_a)
    pack_faces(cur, faces.msg, coords)
    met()
    tell = [
        remote(code, codes_v.at[by], code_s.at[0], code_r.at[0], (bx, (by + k) % NY)) for k in range(1, NY)
    ]
    for c in tell:
        c.start()
    faces.start()
    back_faces = Faces(*face_f)
    for f in (faces, back_faces):
        f.pool[GROUP] = jnp.zeros((5, 32, 128), BF)
        for to in range(2):
            f.side[to, GROUP] = jnp.zeros((32, 128), BF)
    loads[1].wait()
    blank = jnp.zeros((64, 64), F32)

    def build(tap, carry):
        w = [conv_w[tap * 3 + k].astype(F32) for k in range(3)]
        ahead = [blank, *w, blank]
        for z in range(4):
            toep[tap, z * 64 : (z + 1) * 64, :] = jnp.concatenate([ahead[z + 1], ahead[z]], 1).astype(BF)
        rows = ((w[2], w[1], w[0], blank), (blank, w[2], w[1], w[0]))
        for z in range(2):
            for half in range(2):
                pair = jnp.concatenate(rows[z][half * 2 : half * 2 + 2], 1)
                toep_back[tap, z * 64 : (z + 1) * 64, half * 128 : (half + 1) * 128] = pair.astype(BF)
        return carry

    lax.fori_loop(0, 9, build, 0)
    others = codes_v.at[pl.ds(0, NY - 1)]
    told = remote(others, others, code_s.at[0], code_r.at[0], (bx, (by + 1) % NY))
    told.wait_recv()
    to_scalar = pltpu.make_async_copy(codes_v.at[:, 0], codes, code_l.at[0])
    to_scalar.start()
    to_scalar.wait()

    def look(s, carry):
        want = ((s // (TC * 2)) * (TC * NY) + by * TC + (s // 2) % TC) * 2 + s % 2
        found = jnp.int32(GROUP)
        for b in range(GROUP):
            found = jnp.where(codes[b // NB, b % NB] == want, b, found)
        table[s] = found
        return carry

    lax.fori_loop(0, TR * TC * 2, look, 0)
    faces.forward()
    faces.finish()
    assemble(cur, faces.pool, faces.side, neighbors, shifted, edge)
    for e in range(3):
        wide[:, e * 640 : (e + 1) * 640] = shifted[e].astype(BF)
    for group in range(4):
        total = jnp.concatenate([conv_b[...], conv_b[...]], 1)
        for a in range(3):
            for e in range(3):
                total = total + dot(window(wide, a, e, group), toep[a * 3 + e])
        lanes = slice(group * 128, (group + 1) * 128)
        pre[:, lanes] = total
        act[:, lanes] = (total * jax.nn.sigmoid(total)).astype(BF)
    loads[2].wait()
    for h in range(2):
        fold_both[:, :, :, h * 128 : (h + 1) * 128] = dot(act[...], fold_w[h]).reshape(BS, NB, BS, 128)
    for n in range(NB):
        high = coords[2, n].astype(F32)
        one = fold_both[:, n, :, 0:128] * (1.0 - high) + fold_both[:, n, :, 128:256] * high
        part[n] = one.reshape(64, 128).astype(BF)
    parts = Stream(part, part_pool, 0, *part_sems)
    parts.start()
    part_pool[pl.ds(by * NB, NB)] = part[...]
    loads[3].wait()
    loads[4].wait()
    parts.take(False)
    parts.take(True)
    parts.finish()

    rims = [
        Rim(row_out.at[p], col_out.at[p], row_in.at[p], col_in.at[p], corner_in.at[p], rim_s.at[p], rim_r.at[p])
        for p in range(2)
    ]
    for r in range(TR):
        for c in range(TC):
            total = fold_b[...]
            for h in range(2):
                at = table[(r * TC + c) * 2 + h]
                here = (at < GROUP).astype(F32)
                total = total + part_pool[jnp.minimum(at, GROUP - 1)].astype(F32) * here
            where = (slice(r * BS, (r + 1) * BS), slice(c * BS, (c + 1) * BS))
            fold[where] = total.reshape(BS, BS, 128)
            plane[where] = rounded(total * jax.nn.sigmoid(total)).reshape(BS, BS, 128)
    rims[0].start(plane)
    rims[0].finish()
    spread(plane, rims[0], side32, spread_mid)

    def ahead(i, carry):
        start = pl.multiple_of(i * 256, 256)
        total = map_b[...]
        for a in range(3):
            total = total + dot(spread_mid[pl.ds(start + a * COLS, 256), :], map_w[a])
        bev_out[pl.ds(i * BS, BS)] = (total * jax.nn.sigmoid(total)).reshape(BS, COLS, 128).astype(BF)
        g = cot[pl.ds(i * BS, BS)].astype(F32).reshape(256, 128) * slope(total)
        gplane[pl.ds(i * BS, BS)] = rounded(g).reshape(BS, COLS, 128)
        return carry

    lax.fori_loop(0, TR, ahead, 0)
    stores[0].start()
    rims[1].start(gplane)
    turned = gplane[...].reshape(ROWS * COLS, 128).T.astype(BF)
    for a in range(3):
        got = dot(turned, spread_mid[a * COLS : a * COLS + ROWS * COLS, :])
        for e in range(3):
            t = a * 3 + e
            row = t * 128 if t < 8 else 2048
            cat[row : row + 128] = got[:, e * 128 : (e + 1) * 128].T.astype(BF)


    @pl.when(core == 1)
    def _():
        early.to_mate().start()

    rims[1].finish()
    spread(gplane, rims[1], side32, spread_grad)

    def behind(i, carry):
        start = pl.multiple_of(i * 256, 256)
        total = None
        for a in range(3):
            for e in range(3):
                lhs = spread_grad[pl.ds(start + a * COLS, 256), e * 128 : (e + 1) * 128]
                one = dot_t(lhs, map_w[2 - a, (2 - e) * 128 : (3 - e) * 128, :])
                total = one if total is None else total + one
        grad = (total * slope(fold[pl.ds(i * BS, BS)].reshape(256, 128))).reshape(BS, COLS, 128)
        for c in range(TC):
            slots[i * TC + c] = grad[:, c * BS : (c + 1) * BS, :].reshape(64, 128).astype(BF)
        return carry

    lax.fori_loop(0, TR, behind, 0)

    def fill(b, carry):
        number = codes[b // NB, b % NB] // 2
        c = number % (TC * NY) - by * TC
        at = number // (TC * NY) * TC + jnp.clip(c, 0, TC - 1)
        ready[b] = slots[jnp.clip(at, 0, TR * TC - 1)]
        return carry

    lax.fori_loop(0, GROUP, fill, 0)
    give = [
        remote(
            ready.at[pl.ds((by + k) % NY * NB, NB)],
            back.at[by],
            back_s.at[0],
            back_r.at[0],
            (bx, (by + k) % NY),
        )
        for k in (4, 3, 5, 2, 6, 1, 7)
    ]
    for c in give:
        c.start()
    back[by] = ready[pl.ds(by * NB, NB)]
    pl.when(core == 0)(early.combine)
    others = back.at[pl.ds(0, NY - 1)]
    came = remote(others, others, back_s.at[0], back_r.at[0], (bx, (by + 1) % NY))
    came.wait_recv()

    for n in range(NB):
        high = coords[2, n].astype(F32)
        mine = back[jnp.clip(coords[1, n] // TC, 0, NY - 1), n].astype(F32).reshape(BS, BS, 128)
        split[:, n, :, 0:128] = mine * (1.0 - high)
        split[:, n, :, 128:256] = mine * high
    both = split[...].reshape(256, 256)
    act_grad = None
    for h in range(2):
        one = dot_t(both[:, h * 128 : (h + 1) * 128].astype(BF), fold_w[h])
        act_grad = one if act_grad is None else act_grad + one
    grad = rounded(rounded(act_grad) * slope(pre[...]))
    cur[...] = grad.reshape(BS, NB, BS, 512)
    cur_bf[...] = grad.astype(BF)
    pack_faces(cur, back_faces.msg, coords)
    back_faces.start()
    got = dot(both.T.astype(BF), act[...])
    for h in range(2):
        cat[1024 + h * 512 : 1024 + (h + 1) * 512] = got[h * 128 : (h + 1) * 128].T.astype(BF)

    @pl.when(core == 0)
    def _():
        early.to_mate().start()

    turned = [cur_bf[:, g * 128 : (g + 1) * 128].astype(F32).T.astype(BF) for g in range(4)]
    low = lax.broadcasted_iota(jnp.int32, (96, 128), 1) < 64
    for a in range(3):
        for e in range(3):
            total = None
            for g in range(4):
                one = dot(turned[g], window(wide, a, e, g))
                total = one if total is None else total + one
            total = total.T
            summed_z = total[0:192] + pltpu.roll(total[64:256], 64, 1)
            row = 2176 + (a * 3 + e) * 96
            cat[row : row + 96] = jnp.where(
                low, summed_z[0:96], pltpu.roll(summed_z[96:192], 64, 1)
            ).astype(BF)
    cat[3040:3072] = jnp.zeros((32, 128), BF)
    late.to_mate().start()
    pl.when(core == 1)(early.combine)
    late.combine()
    early.sum_x()
    late.sum_x()
    early.sum_ring()
    back_faces.forward()
    late.sum_ring()
    back_faces.finish()
    assemble(cur, back_faces.pool, back_faces.side, neighbors, shifted, edge)
    for e in range(3):
        wide[:, e * 640 : (e + 1) * 640] = shifted[e].astype(BF)
    for g in range(4):
        total = None
        for a in range(3):
            for e in range(3):
                one = dot_t(window(wide, a, e, g), toep_back[(2 - a) * 3 + 2 - e])
                total = one if total is None else total + one
        view = total.reshape(BS, NB, BS, 128)
        for n in range(NB):
            feat_out[n, :, :, g * 128 : (g + 1) * 128] = view[:, n]
    stores[1].start()
    early.relay()
    late.relay()
    early.done()
    for h in range(2):
        fold_out[h] = early.full[1024 + h * 512 : 1024 + (h + 1) * 512].astype(F32)
    stores[3].start()
    for t in range(8):
        map_out[t] = early.full[t * 128 : (t + 1) * 128].astype(F32)
    late.done()
    map_out[8] = late.full[0:128].astype(F32)
    stores[4].start()
    for t in range(9):
        v = late.full[128 + t * 96 : 128 + (t + 1) * 96].astype(F32)
        conv_out[t, 0:96] = v[:, 0:64]
        conv_out[t, 96:192] = v[:, 64:128]
    stores[2].start()

    told.wait_send()
    came.wait_send()
    faces.drain()
    back_faces.drain()
    parts.drain()
    for rim in rims:
        rim.drain()
    early.drain()
    late.drain()
    for c in stores:
        c.wait()


def hand_on(*refs):
    given, results, held, sems = refs[:5], refs[5:10], refs[10:15], refs[15]
    takes = [pltpu.make_async_copy(a, b, sems.at[0, i]) for i, (a, b) in enumerate(zip(given, held, strict=True))]
    gives = [pltpu.make_async_copy(a, b, sems.at[1, i]) for i, (a, b) in enumerate(zip(held, results, strict=True))]
    for c in takes:
        c.start()
    for take, give in zip(takes, gives, strict=True):
        take.wait()
        give.start()
    for c in gives:
        c.wait()


def body(vox_feats, block_coords, neighbors, conv_w, conv_b, fold_w, fold_b, map_w, map_b, cotangent):
    far = pl.BlockSpec(memory_space=pl.ANY)
    outs = [
        jax.ShapeDtypeStruct((ROWS, COLS, 128), BF),
        jax.ShapeDtypeStruct((NB, BS, BS, 512), F32),
        jax.ShapeDtypeStruct((9, 192, 64), F32),
        jax.ShapeDtypeStruct((2, 512, 128), F32),
        jax.ShapeDtypeStruct((9, 128, 128), F32),
    ]
    made = pl.pallas_call(
        whole,
        in_specs=[far] * 5 + [VMEM] * 3 + [SMEM] * 2,
        out_specs=[far] * 5,
        out_shape=outs,
        scratch_shapes=[
            *[pltpu.VMEM(o.shape, o.dtype) for o in outs],
            DMA((5,)),
            pltpu.VMEM((NB, BS, BS, 512), BF),
            pltpu.VMEM((27, 64, 64), BF),
            pltpu.VMEM((2, 512, 128), BF),
            pltpu.VMEM((3, 384, 128), BF),
            pltpu.VMEM((ROWS, COLS, 128), BF),
            DMA((5,)),
            pltpu.VMEM((BS, NB, BS, 512), F32),
            pltpu.VMEM((3, 320, 640), F32),
            pltpu.VMEM((2, 8, 640), F32),
            pltpu.VMEM((9, 256, 128), BF),
            pltpu.VMEM((9, 128, 256), BF),
            pltpu.VMEM((320, 1920), BF),
            pltpu.VMEM((256, 512), F32),
            pltpu.VMEM((256, 512), BF),
            pltpu.VMEM((BS, NB, BS, 256), F32),
            pltpu.VMEM((NB, 64, 128), BF),
            pltpu.VMEM((GROUP, 64, 128), BF),
            pltpu.VMEM((8, 128), jnp.int32),
            pltpu.VMEM((NY, 8, 128), jnp.int32),
            pltpu.SMEM((NY, 128), jnp.int32),
            pltpu.SMEM((TR * TC * 2,), jnp.int32),
            pltpu.VMEM((ROWS, COLS, 128), F32),
            pltpu.VMEM((ROWS, COLS, 128), F32),
            pltpu.VMEM((ROWS, COLS, 128), F32),
            pltpu.VMEM(((ROWS + 2) * COLS, 384), BF),
            pltpu.VMEM(((ROWS + 2) * COLS, 384), BF),
            pltpu.VMEM((2, ROWS, 128), F32),
            pltpu.VMEM((TR * TC, 64, 128), BF),
            pltpu.VMEM((GROUP, 64, 128), BF),
            pltpu.VMEM((NY, NB, 64, 128), BF),
            pltpu.VMEM((BS, NB, BS, 256), F32),
            pltpu.VMEM((256, 512), BF),
            pltpu.VMEM((CAT, 128), BF),
            total_scratch(1024),
            total_scratch(512),
            FACE_SCRATCH,
            FACE_SCRATCH,
            STREAM_SEMS,
            DMA((1,)),
            DMA((1,)),
            DMA((1,)),
            pltpu.VMEM((2, 2, COLS, 128), BF),
            pltpu.VMEM((2, 2, ROWS, 128), BF),
            pltpu.VMEM((2, 2, COLS, 128), BF),
            pltpu.VMEM((2, 2, ROWS, 128), BF),
            pltpu.VMEM((2, 4, 16, 128), BF),
            DMA((2, 8)),
            DMA((2, 8)),
            DMA((1,)),
            DMA((1,)),
        ],
        compiler_params=pltpu.CompilerParams(
            collective_id=1, has_side_effects=True, vmem_limit_bytes=58 * 2**20
        ),
    )(
        vox_feats,
        conv_w.reshape(27, 64, 64),
        fold_w.reshape(2, 512, 128),
        map_w.reshape(3, 384, 128),
        cotangent,
        conv_b[None],
        fold_b[None],
        map_b[None],
        block_coords,
        neighbors.T,
    )
    bev_map, feat_grad, conv_grads, fold_grads, map_grads = pl.pallas_call(
        hand_on,
        in_specs=[far] * 5,
        out_specs=[far] * 5,
        out_shape=outs,
        scratch_shapes=[*[pltpu.VMEM(o.shape, o.dtype) for o in outs], DMA((2, 5))],
        compiler_params=pltpu.CompilerParams(vmem_limit_bytes=58 * 2**20),
    )(*made)
    return (
        bev_map,
        feat_grad,
        conv_grads.reshape(3, 3, 3, 64, 64),
        fold_grads.reshape(1024, 128),
        map_grads.reshape(3, 3, 128, 128),
    )


def solution(mesh):
    placed = (
        P(("bx", "by"), None, None, None),
        P(None, ("bx", "by")),
        P(None, ("bx", "by")),
        P(),
        P(),
        P(),
        P(),
        P(),
        P(),
        P("bx", "by", None),
    )
    return jax.shard_map(
        body,
        mesh=mesh,
        in_specs=placed,
        out_specs=(P("bx", "by", None), P(("bx", "by"), None, None, None), P(), P(), P()),
        check_vma=False,
    )
```

```python
import functools

import jax
import jax.numpy as jnp
from jax import lax
from jax.experimental import pallas as pl
from jax.experimental.pallas import tpu as pltpu
from jax.sharding import PartitionSpec as P

MESH = pl.DeviceIdType.MESH
BF = jnp.bfloat16
F32 = jnp.float32
BS = 8
TR = 6
TC = 4
NB = 4
NX = 16
NY = 8
GROUP = NB * NY
ROWS = TR * BS
COLS = TC * BS
VMEM = pl.BlockSpec(memory_space=pltpu.VMEM)
SMEM = pl.BlockSpec(memory_space=pltpu.SMEM)
DMA = pltpu.SemaphoreType.DMA
CAT = 3072


def place():
    return lax.axis_index("bx"), lax.axis_index("by")


def remote(src, dst, send, recv, device):
    return pltpu.make_async_remote_copy(
        src_ref=src,
        dst_ref=dst,
        send_sem=send,
        recv_sem=recv,
        device_id=device,
        device_id_type=MESH,
    )


def signal(device):
    pl.semaphore_signal(
        pltpu.get_barrier_semaphore(), inc=1, device_id=device, device_id_type=MESH
    )


def slope(pre):
    s = jax.nn.sigmoid(pre)
    return s * (1.0 + pre * (1.0 - s))


def rounded(v):
    return v.astype(BF).astype(F32)


def partners():
    bx, by = place()
    core = by % 2
    out = [(None, (bx, (by + k) % NY)) for k in range(1, NY)]
    out += [(None, ((bx + k) % NX, by)) for k in range(1, NX)]
    for step in (-1, 1):
        inside = bx > 0 if step < 0 else bx < NX - 1
        out += [(inside, (bx + step, core + 2 * j)) for j in range(NY // 2)]
        out.append((inside & (by > 0), (bx + step, by - 1)))
        out.append((inside & (by < NY - 1), (bx + step, by + 1)))
    return out


def greet():
    for ok, device in partners():
        if ok is None:
            signal(device)
        else:
            pl.when(ok)(functools.partial(signal, device))


def met():
    count = jnp.int32(0)
    for ok, _ in partners():
        count = count + (1 if ok is None else ok.astype(jnp.int32))
    pl.semaphore_wait(pltpu.get_barrier_semaphore(), count)


def pack_faces(cur, msg, coords):
    lane = lax.broadcasted_iota(jnp.int32, (32, 128), 1)

    def flat(v):
        return jnp.concatenate([v[:, t * 128 : (t + 1) * 128] for t in range(4)], 0)

    def one(n, carry):
        high = coords[2, n].astype(F32)
        msg[n, 0] = flat(cur[0, n]).astype(BF)
        msg[n, 1] = flat(cur[7, n]).astype(BF)
        msg[n, 2] = flat(cur[:, n, 0, :]).astype(BF)
        msg[n, 3] = flat(cur[:, n, 7, :]).astype(BF)
        top = cur[:, n, :, 384:512].reshape(64, 128)
        low = cur[:, n, :, 0:128].reshape(64, 128)
        face = pltpu.roll(top, 64, 1) * (1.0 - high) + low * high
        msg[n, 4] = jnp.where(lane < 64, face[0:32], pltpu.roll(face[32:64], 64, 1)).astype(BF)
        return carry

    lax.fori_loop(0, NB, one, 0, unroll=True)


class Stream:
    def __init__(self, src, pool, step, out_s, in_r, straight=False):
        self.src, self.pool, self.step, self.straight = src, pool, step, straight
        self.out_s, self.in_r = out_s, in_r
        self.bx, self.by = place()
        self.mate = self.by + 1 - 2 * (self.by % 2)
        if step:
            self.kinds = [(6, None), (2, None), (0, None), (4, 0), (4, 1)]
            self.sends = self.bx > 0 if step < 0 else self.bx < NX - 1
            self.takes = self.bx < NX - 1 if step < 0 else self.bx > 0
        elif straight:
            self.kinds = [(4, None), (6, None), (2, None)]
        else:
            self.kinds = [(6, 0), (2, 1), (6, 1), (2, 0), (4, 0), (4, 1)]

    def view(self, origin, half):
        if half is None:
            return self.pool.at[pl.ds(origin * NB, NB)]
        return self.pool.at[pl.ds(origin * NB + half * (NB // 2), NB // 2)]

    def when(self, ok, run):
        if self.step:
            pl.when(ok)(run)
        else:
            run()

    def copy(self, src, origin, half, sem, kind, device):
        got = self.in_r.at[7 if kind is None else self.kinds.index(kind)]
        return remote(src, self.view(origin, half), self.out_s.at[sem], got, device)

    def start(self):
        def run():
            for off, half in self.kinds:
                if off == 4 and not self.straight:
                    continue
                src = self.src if half is None else self.src.at[pl.ds(half * (NB // 2), NB // 2)]
                to = (self.bx + self.step, (self.by + 8 - off) % NY)
                self.copy(src, self.by, half, 0, (off, half), to).start()
            if not self.step:
                self.copy(self.src, self.by, None, 0, None, (self.bx, self.mate)).start()

        self.when(self.sends if self.step else None, run)

    def take(self, far):
        def run():
            for off, half in reversed(self.kinds) if self.straight else self.kinds:
                if (off == 4) != far:
                    continue
                origin = (self.by + off) % NY
                at = self.view(origin, half)
                to_mate = self.copy(at, origin, half, 1, None, (self.bx, self.mate))
                self.copy(at, origin, half, 1, (off, half), (self.bx, self.mate)).wait_recv()
                part = 0 if off == 6 else 1
                if off in (2, 6) and half in (None, part) and not self.straight:
                    piece = self.view(origin, part)
                    to = (self.bx, (self.by + 8 - off) % NY)
                    self.copy(piece, origin, part, 1, (4, part), to).start()
                to_mate.start()

        self.when(self.takes if self.step else None, run)

    def bytes_of(self, messages, sem):
        at = self.pool.at[pl.ds(0, messages * NB)]
        return remote(at, at, self.out_s.at[sem], self.in_r.at[7], (self.bx, self.mate))

    def finish(self):
        self.when(self.takes if self.step else None, lambda: self.bytes_of(4, 1).wait_recv())

    def drain(self):
        self.when(self.sends if self.step else None, lambda: self.bytes_of(4 if self.straight else 3, 0).wait_send())
        passed = 5 if self.step else 3 if self.straight else 4
        self.when(self.takes if self.step else None, lambda: self.bytes_of(passed, 1).wait_send())


STREAM_SEMS = [DMA((2,)), DMA((8,))]


class Faces:
    def __init__(self, msg, pool, side, own, before, after):
        self.msg, self.pool, self.side = msg, pool, side
        self.by = place()[1]
        self.streams = [
            Stream(msg, pool, 0, *own),
            Stream(msg.at[:, 1], side.at[0], 1, *before),
            Stream(msg.at[:, 0], side.at[1], -1, *after),
        ]

    def start(self):
        for x in self.streams:
            x.start()
        self.pool[pl.ds(self.by * NB, NB)] = self.msg[...]

    def forward(self):
        for far in (False, True):
            for x in self.streams:
                x.take(far)

    def finish(self):
        for x in self.streams:
            x.finish()

    def drain(self):
        for x in self.streams:
            x.drain()


FACE_SCRATCH = [
    pltpu.VMEM((NB, 5, 32, 128), BF),
    pltpu.VMEM((GROUP + 1, 5, 32, 128), BF),
    pltpu.VMEM((2, GROUP + 1, 32, 128), BF),
    STREAM_SEMS,
    STREAM_SEMS,
    STREAM_SEMS,
]


def assemble(cur, pool, side, neighbors, shifted, edge):
    low = lax.broadcasted_iota(jnp.int32, (8, 128), 1) < 64
    sub = lax.broadcasted_iota(jnp.int32, (8, 128), 0)

    bx, _ = place()

    def one(n, carry):
        def spot(k, group):
            at = neighbors[n, k]
            from_group = at - group * GROUP
            ok = (at >= 0) & (from_group >= 0) & (from_group < GROUP)
            return jnp.where(ok, from_group, GROUP)

        def face(part, k):
            return pool[spot(k, bx), part].astype(F32)

        def xface(dx, k):
            near = face(1 if dx < 0 else 0, k)
            return near + side[0 if dx < 0 else 1, spot(k, bx + dx)].astype(F32)

        def tiles(v):
            return [v[t * 8 : (t + 1) * 8] for t in range(4)]

        def turn(v):
            return pltpu.roll(v, 64, 1)

        def padz(core, before, after):
            r = [turn(t) for t in core]
            return (
                [jnp.where(low, before, r[0])]
                + [jnp.where(low, r[t - 1], r[t]) for t in (1, 2, 3)]
                + [jnp.where(low, r[3], after)]
            )

        def put(x, t, mid, above, below):
            row = pl.multiple_of((x * NB + n) * 8, 8)
            at = (pl.ds(row, 8), pl.ds(t * 128, 128))
            shifted[(1, *at)] = mid
            shifted[(0, *at)] = jnp.where(sub == 0, above, pltpu.roll(mid, 1, 0))
            shifted[(2, *at)] = jnp.where(sub == 7, below, pltpu.roll(mid, 7, 0))

        for x, dx in ((0, -1), (9, 1)):
            z = []
            for dy in range(3):
                k = 9 * (dx + 1) + 3 * dy
                z.append(
                    padz(tiles(xface(dx, k + 1)), turn(xface(dx, k)[24:32]), turn(xface(dx, k + 2)[0:8]))
                )
            for t in range(5):
                put(x, t, z[1][t], pltpu.roll(z[0][t], 1, 0), pltpu.roll(z[2][t], 7, 0))
        for i, (k, part) in enumerate(((9, 3), (15, 2))):
            z = padz(tiles(face(part, k + 1)), turn(face(part, k)[24:32]), turn(face(part, k + 2)[0:8]))
            for t in range(5):
                edge[i, :, t * 128 : (t + 1) * 128] = z[t]
        under = face(4, 12)
        over = face(4, 14)
        for x in range(BS):
            at = slice(x % 4 * 8, x % 4 * 8 + 8)
            before = under[at] if x < 4 else turn(under[at])
            after = turn(over[at]) if x < 4 else over[at]
            z = padz([cur[x, n, :, t * 128 : (t + 1) * 128] for t in range(4)], before, after)
            for t in range(5):
                lanes = slice(t * 128, (t + 1) * 128)
                put(x + 1, t, z[t], edge[0, x : x + 1, lanes], edge[1, x : x + 1, lanes])
        return carry

    lax.fori_loop(0, NB, one, 0, unroll=2)


NEAR = [(-1, 0), (1, 0), (0, -1), (0, 1), (-1, -1), (-1, 1), (1, -1), (1, 1)]


class Rim:
    def __init__(self, row_out, col_out, row_in, col_in, corner_in, send, recv):
        self.row_out, self.col_out = row_out, col_out
        self.row_in, self.col_in, self.corner_in = row_in, col_in, corner_in
        self.send, self.recv = send, recv
        self.bx, self.by = place()

    def exists(self, d):
        dx, dy = NEAR[d]
        ok = None
        for v, step, size in ((self.bx, dx, NX), (self.by, dy, NY)):
            if step:
                here = v > 0 if step < 0 else v < size - 1
                ok = here if ok is None else ok & here
        return ok

    def copy(self, d):
        dx, dy = NEAR[d]
        back = NEAR.index((-dx, -dy))
        if dy == 0:
            src, dst = self.row_out.at[d], self.row_in.at[back]
        elif dx == 0:
            src, dst = self.col_out.at[d - 2], self.col_in.at[back - 2]
        else:
            src = self.row_out.at[0 if dx < 0 else 1, pl.ds(0 if dy < 0 else 16, 16)]
            dst = self.corner_in.at[back - 4]
        return remote(src, dst, self.send.at[d], self.recv.at[back], (self.bx + dx, self.by + dy))

    def landing(self, d):
        dx, dy = NEAR[d]
        if dy == 0:
            return self.row_in.at[d]
        if dx == 0:
            return self.col_in.at[d - 2]
        return self.corner_in.at[d - 4]

    def start(self, plane):
        self.row_out[0] = plane[0].astype(BF)
        self.row_out[1] = plane[ROWS - 1].astype(BF)
        self.col_out[0] = plane[:, 0, :].astype(BF)
        self.col_out[1] = plane[:, COLS - 1, :].astype(BF)
        for d in range(8):

            @pl.when(self.exists(d))
            def _(d=d):
                self.copy(d).start()

            @pl.when(jnp.logical_not(self.exists(d)))
            def _(d=d):
                at = self.landing(d)
                at[...] = jnp.zeros(at.shape, BF)

    def finish(self):
        for d in range(8):

            @pl.when(self.exists(d))
            def _(d=d):
                dx, dy = NEAR[d]
                at = self.landing(d)
                remote(at, at, self.send.at[d], self.recv.at[d], (self.bx + dx, self.by + dy)).wait_recv()

    def drain(self):
        for d in range(8):

            @pl.when(self.exists(d))
            def _(d=d):
                self.copy(d).wait_send()


def spread(plane, rim, side32, out):
    side32[0] = rim.col_in[0].astype(F32)
    side32[1] = rim.col_in[1].astype(F32)
    j = lax.broadcasted_iota(jnp.int32, (COLS, 128), 0)

    def put(at, row, left, right):
        rows = pl.ds(pl.multiple_of(at * COLS, COLS), COLS)
        out[rows, 0:128] = jnp.where(j == 0, left, pltpu.roll(row, 1, 0)).astype(BF)
        out[rows, 128:256] = row.astype(BF)
        out[rows, 256:384] = jnp.where(j == COLS - 1, right, pltpu.roll(row, COLS - 1, 0)).astype(BF)

    def inner(i, carry):
        put(i + 1, plane[i], side32[0, pl.ds(i, 1), :], side32[1, pl.ds(i, 1), :])
        return carry

    lax.fori_loop(0, ROWS, inner, 0, unroll=8)
    corner = [rim.corner_in[c].astype(F32) for c in range(4)]
    put(0, rim.row_in[0].astype(F32), corner[0][15:16], corner[1][0:1])
    put(ROWS + 1, rim.row_in[1].astype(F32), corner[2][15:16], corner[3][0:1])

class Total:
    def __init__(self, base, half, cat, given, sums, second, ring, full, sems):
        self.base, self.half, self.chunk = base, half, half // NX
        self.cat, self.given, self.sums, self.second = cat, given, sums, second
        self.ring, self.full = ring, full
        self.sems = sems
        self.bx, self.by = place()
        self.core = self.by % 2
        self.mate = self.by + 1 - 2 * self.core
        self.chip = self.by // 2

    def rows(self, core):
        return pl.ds(pl.multiple_of(self.base + core * self.half, self.half), self.half)

    def piece(self, core, i):
        return pl.ds(pl.multiple_of(core * self.half + i * self.chunk, self.chunk), self.chunk)

    def to_mate(self):
        at = self.cat.at[self.rows(1 - self.core)]
        return remote(at, self.given, self.sems.at[0], self.sems.at[1], (self.bx, self.mate))

    def all_of(self, at, stage):
        return remote(at, at, self.sems.at[2 * stage], self.sems.at[2 * stage + 1], (self.bx, self.mate))

    def combine(self):
        self.to_mate().wait_recv()
        self.sums[...] = (self.cat[self.rows(self.core)].astype(F32) + self.given[...].astype(F32)).astype(BF)
        for q in range(NX):

            @pl.when(self.bx != q)
            def _(q=q):
                at = self.sums.at[pl.ds(q * self.chunk, self.chunk)]
                remote(at, self.second.at[self.bx], self.sems.at[2], self.sems.at[3], (q, self.by)).start()

    def sum_x(self):
        self.all_of(self.second.at[pl.ds(0, NX - 1)], 1).wait_recv()
        mine = pl.ds(pl.multiple_of(self.bx * self.chunk, self.chunk), self.chunk)
        total = self.sums[mine].astype(F32)
        for k in range(1, NX):
            total = total + self.second[(self.bx + k) % NX].astype(F32)
        self.ring[self.chip] = total.astype(BF)
        at = self.ring.at[self.chip]
        for k in (1, 3, 2):
            to = (self.bx, (self.by + 2 * k) % NY)
            remote(at, at, self.sems.at[4], self.sems.at[5], to).start()

    def sum_ring(self):
        self.all_of(self.ring.at[pl.ds(0, 3)], 2).wait_recv()
        total = self.ring[0].astype(F32)
        for i in range(1, 4):
            total = total + self.ring[i].astype(F32)
        self.full[self.piece(self.core, self.bx)] = total.astype(BF)
        at = self.full.at[self.piece(self.core, self.bx)]
        for k in range(1, NX):
            remote(at, at, self.sems.at[6], self.sems.at[7], ((self.bx + k) % NX, self.by)).start()

    def share(self):
        at = self.full.at[pl.ds(pl.multiple_of(self.core * self.half, self.half), self.half)]
        return remote(at, at, self.sems.at[8], self.sems.at[9], (self.bx, self.mate))

    def relay(self):
        self.all_of(self.full.at[pl.ds(0, (NX - 1) * self.chunk)], 3).wait_recv()
        self.share().start()

    def done(self):
        self.share().wait_recv()

    def drain(self):
        self.to_mate().wait_send()
        self.all_of(self.second.at[pl.ds(0, NX - 1)], 1).wait_send()
        self.all_of(self.ring.at[pl.ds(0, 3)], 2).wait_send()
        self.all_of(self.full.at[pl.ds(0, (NX - 1) * self.chunk)], 3).wait_send()
        self.share().wait_send()


def total_scratch(half):
    chunk = half // NX
    return [
        pltpu.VMEM((half, 128), BF),
        pltpu.VMEM((half, 128), BF),
        pltpu.VMEM((NX, chunk, 128), BF),
        pltpu.VMEM((4, chunk, 128), BF),
        pltpu.VMEM((2 * half, 128), BF),
        DMA((10,)),
    ]


def dot(a, b):
    return jnp.dot(a, b, preferred_element_type=F32)


def dot_t(a, b):
    return lax.dot_general(a, b, (((1,), (1,)), ((), ())), preferred_element_type=F32)


def window(wide, a, e, g):
    return wide[a * 32 : a * 32 + 256, e * 640 + g * 128 : e * 640 + g * 128 + 256]


def whole(
    vox_h, conv_w_h, fold_w_h, map_w_h, cot_h, conv_b, fold_b, map_b, coords, neighbors,
    bev_far, feat_far, conv_far, fold_far, map_far,
    bev_out, feat_out, conv_out, fold_out, map_out, out_sem,
    vox, conv_w, fold_w, map_w, cot, load_sem,
    cur, shifted, edge, toep, toep_back, wide, pre, act, fold_both, part, part_pool,
    code, codes_v, codes, table,
    fold, plane, gplane, spread_mid, spread_grad, side32, slots, ready, back,
    split, cur_bf, cat, early_part, late_part,
    face_a, face_f, part_sems, code_s, code_r, code_l,
    row_out, col_out, row_in, col_in, corner_in, rim_s, rim_r, back_s, back_r,
):
    bx, by = place()
    greet()
    stores = [
        pltpu.make_async_copy(src, dst, out_sem.at[i])
        for i, (src, dst) in enumerate(
            ((bev_out, bev_far), (feat_out, feat_far), (conv_out, conv_far), (fold_out, fold_far), (map_out, map_far))
        )
    ]
    early = Total(0, 1024, cat, *early_part)
    late = Total(2048, 512, cat, *late_part)
    core = by % 2
    loads = [
        pltpu.make_async_copy(src, dst, load_sem.at[i])
        for i, (src, dst) in enumerate(
            ((vox_h, vox), (conv_w_h, conv_w), (fold_w_h, fold_w), (map_w_h, map_w), (cot_h, cot))
        )
    ]
    for c in loads:
        c.start()
    lane = lax.broadcasted_iota(jnp.int32, (8, 128), 1)
    tile = jnp.zeros((8, 128), jnp.int32)
    for n in range(NB):
        number = ((coords[0, n] - bx * TR) * (TC * NY) + coords[1, n]) * 2 + coords[2, n]
        tile = jnp.where(lane == n, number, tile)
    code[...] = tile
    codes_v[by] = tile
    loads[0].wait()
    for n in range(NB):
        cur[:, n] = vox[n].astype(F32)
    faces = Faces(*face_a)
    pack_faces(cur, faces.msg, coords)
    met()
    tell = [
        remote(code, codes_v.at[by], code_s.at[0], code_r.at[0], (bx, (by + k) % NY)) for k in range(1, NY)
    ]
    for c in tell:
        c.start()
    faces.start()
    back_faces = Faces(*face_f)
    for f in (faces, back_faces):
        f.pool[GROUP] = jnp.zeros((5, 32, 128), BF)
        for to in range(2):
            f.side[to, GROUP] = jnp.zeros((32, 128), BF)
    loads[1].wait()
    blank = jnp.zeros((64, 64), F32)

    def build(tap, carry):
        w = [conv_w[tap * 3 + k].astype(F32) for k in range(3)]
        ahead = [blank, *w, blank]
        for z in range(4):
            toep[tap, z * 64 : (z + 1) * 64, :] = jnp.concatenate([ahead[z + 1], ahead[z]], 1).astype(BF)
        rows = ((w[2], w[1], w[0], blank), (blank, w[2], w[1], w[0]))
        for z in range(2):
            for half in range(2):
                pair = jnp.concatenate(rows[z][half * 2 : half * 2 + 2], 1)
                toep_back[tap, z * 64 : (z + 1) * 64, half * 128 : (half + 1) * 128] = pair.astype(BF)
        return carry

    lax.fori_loop(0, 9, build, 0)
    others = codes_v.at[pl.ds(0, NY - 1)]
    told = remote(others, others, code_s.at[0], code_r.at[0], (bx, (by + 1) % NY))
    told.wait_recv()
    to_scalar = pltpu.make_async_copy(codes_v.at[:, 0], codes, code_l.at[0])
    to_scalar.start()
    to_scalar.wait()

    def look(s, carry):
        want = ((s // (TC * 2)) * (TC * NY) + by * TC + (s // 2) % TC) * 2 + s % 2
        found = jnp.int32(GROUP)
        for b in range(GROUP):
            found = jnp.where(codes[b // NB, b % NB] == want, b, found)
        table[s] = found
        return carry

    lax.fori_loop(0, TR * TC * 2, look, 0)
    faces.forward()
    faces.finish()
    assemble(cur, faces.pool, faces.side, neighbors, shifted, edge)
    for e in range(3):
        wide[:, e * 640 : (e + 1) * 640] = shifted[e].astype(BF)
    for group in range(4):
        total = jnp.concatenate([conv_b[...], conv_b[...]], 1)
        for a in range(3):
            for e in range(3):
                total = total + dot(window(wide, a, e, group), toep[a * 3 + e])
        lanes = slice(group * 128, (group + 1) * 128)
        pre[:, lanes] = total
        act[:, lanes] = (total * jax.nn.sigmoid(total)).astype(BF)
    loads[2].wait()
    for h in range(2):
        fold_both[:, :, :, h * 128 : (h + 1) * 128] = dot(act[...], fold_w[h]).reshape(BS, NB, BS, 128)
    for n in range(NB):
        high = coords[2, n].astype(F32)
        one = fold_both[:, n, :, 0:128] * (1.0 - high) + fold_both[:, n, :, 128:256] * high
        part[n] = one.reshape(64, 128).astype(BF)
    parts = Stream(part, part_pool, 0, *part_sems, straight=True)
    parts.start()
    part_pool[pl.ds(by * NB, NB)] = part[...]
    loads[3].wait()
    loads[4].wait()
    parts.take(False)
    parts.take(True)
    parts.finish()

    rims = [
        Rim(row_out.at[p], col_out.at[p], row_in.at[p], col_in.at[p], corner_in.at[p], rim_s.at[p], rim_r.at[p])
        for p in range(2)
    ]
    for r in range(TR):
        for c in range(TC):
            total = fold_b[...]
            for h in range(2):
                at = table[(r * TC + c) * 2 + h]
                here = (at < GROUP).astype(F32)
                total = total + part_pool[jnp.minimum(at, GROUP - 1)].astype(F32) * here
            where = (slice(r * BS, (r + 1) * BS), slice(c * BS, (c + 1) * BS))
            fold[where] = total.reshape(BS, BS, 128)
            plane[where] = rounded(total * jax.nn.sigmoid(total)).reshape(BS, BS, 128)
    rims[0].start(plane)
    rims[0].finish()
    spread(plane, rims[0], side32, spread_mid)

    def ahead(i, carry):
        start = pl.multiple_of(i * 256, 256)
        total = map_b[...]
        for a in range(3):
            total = total + dot(spread_mid[pl.ds(start + a * COLS, 256), :], map_w[a])
        bev_out[pl.ds(i * BS, BS)] = (total * jax.nn.sigmoid(total)).reshape(BS, COLS, 128).astype(BF)
        g = cot[pl.ds(i * BS, BS)].astype(F32).reshape(256, 128) * slope(total)
        gplane[pl.ds(i * BS, BS)] = rounded(g).reshape(BS, COLS, 128)
        return carry

    lax.fori_loop(0, TR, ahead, 0, unroll=3)
    stores[0].start()
    rims[1].start(gplane)
    turned = gplane[...].reshape(ROWS * COLS, 128).T.astype(BF)
    for a in range(3):
        got = dot(turned, spread_mid[a * COLS : a * COLS + ROWS * COLS, :])
        for e in range(3):
            t = a * 3 + e
            row = t * 128 if t < 8 else 2048
            cat[row : row + 128] = got[:, e * 128 : (e + 1) * 128].T.astype(BF)


    @pl.when(core == 1)
    def _():
        early.to_mate().start()

    rims[1].finish()
    spread(gplane, rims[1], side32, spread_grad)

    def behind(i, carry):
        start = pl.multiple_of(i * 256, 256)
        total = None
        for a in range(3):
            for e in range(3):
                lhs = spread_grad[pl.ds(start + a * COLS, 256), e * 128 : (e + 1) * 128]
                one = dot_t(lhs, map_w[2 - a, (2 - e) * 128 : (3 - e) * 128, :])
                total = one if total is None else total + one
        grad = (total * slope(fold[pl.ds(i * BS, BS)].reshape(256, 128))).reshape(BS, COLS, 128)
        for c in range(TC):
            slots[i * TC + c] = grad[:, c * BS : (c + 1) * BS, :].reshape(64, 128).astype(BF)
        return carry

    lax.fori_loop(0, TR, behind, 0, unroll=3)

    def fill(b, carry):
        number = codes[b // NB, b % NB] // 2
        c = number % (TC * NY) - by * TC
        at = number // (TC * NY) * TC + jnp.clip(c, 0, TC - 1)
        ready[b] = slots[jnp.clip(at, 0, TR * TC - 1)]
        return carry

    lax.fori_loop(0, GROUP, fill, 0, unroll=8)
    give = [
        remote(
            ready.at[pl.ds((by + k) % NY * NB, NB)],
            back.at[by],
            back_s.at[0],
            back_r.at[0],
            (bx, (by + k) % NY),
        )
        for k in (4, 3, 5, 2, 6, 1, 7)
    ]
    for c in give:
        c.start()
    back[by] = ready[pl.ds(by * NB, NB)]
    pl.when(core == 0)(early.combine)
    others = back.at[pl.ds(0, NY - 1)]
    came = remote(others, others, back_s.at[0], back_r.at[0], (bx, (by + 1) % NY))
    came.wait_recv()

    for n in range(NB):
        high = coords[2, n].astype(F32)
        mine = back[jnp.clip(coords[1, n] // TC, 0, NY - 1), n].astype(F32).reshape(BS, BS, 128)
        split[:, n, :, 0:128] = mine * (1.0 - high)
        split[:, n, :, 128:256] = mine * high
    both = split[...].reshape(256, 256)
    act_grad = None
    for h in range(2):
        one = dot_t(both[:, h * 128 : (h + 1) * 128].astype(BF), fold_w[h])
        act_grad = one if act_grad is None else act_grad + one
    grad = rounded(rounded(act_grad) * slope(pre[...]))
    cur[...] = grad.reshape(BS, NB, BS, 512)
    cur_bf[...] = grad.astype(BF)
    pack_faces(cur, back_faces.msg, coords)
    back_faces.start()
    got = dot(both.T.astype(BF), act[...])
    for h in range(2):
        cat[1024 + h * 512 : 1024 + (h + 1) * 512] = got[h * 128 : (h + 1) * 128].T.astype(BF)

    @pl.when(core == 0)
    def _():
        early.to_mate().start()

    turned = [cur_bf[:, g * 128 : (g + 1) * 128].astype(F32).T.astype(BF) for g in range(4)]
    low = lax.broadcasted_iota(jnp.int32, (96, 128), 1) < 64
    for a in range(3):
        for e in range(3):
            total = None
            for g in range(4):
                one = dot(turned[g], window(wide, a, e, g))
                total = one if total is None else total + one
            total = total.T
            summed_z = total[0:192] + pltpu.roll(total[64:256], 64, 1)
            row = 2176 + (a * 3 + e) * 96
            cat[row : row + 96] = jnp.where(
                low, summed_z[0:96], pltpu.roll(summed_z[96:192], 64, 1)
            ).astype(BF)
    cat[3040:3072] = jnp.zeros((32, 128), BF)
    late.to_mate().start()
    pl.when(core == 1)(early.combine)
    late.combine()
    early.sum_x()
    for x in back_faces.streams:
        x.take(False)
    late.sum_x()
    early.sum_ring()
    for x in back_faces.streams:
        x.take(True)
    late.sum_ring()
    back_faces.finish()
    assemble(cur, back_faces.pool, back_faces.side, neighbors, shifted, edge)
    for e in range(3):
        wide[:, e * 640 : (e + 1) * 640] = shifted[e].astype(BF)
    for g in range(4):
        total = None
        for a in range(3):
            for e in range(3):
                one = dot_t(window(wide, a, e, g), toep_back[(2 - a) * 3 + 2 - e])
                total = one if total is None else total + one
        view = total.reshape(BS, NB, BS, 128)
        for n in range(NB):
            feat_out[n, :, :, g * 128 : (g + 1) * 128] = view[:, n]
    stores[1].start()
    early.relay()
    late.relay()
    early.done()
    for h in range(2):
        fold_out[h] = early.full[1024 + h * 512 : 1024 + (h + 1) * 512].astype(F32)
    stores[3].start()
    for t in range(8):
        map_out[t] = early.full[t * 128 : (t + 1) * 128].astype(F32)
    late.done()
    map_out[8] = late.full[0:128].astype(F32)
    stores[4].start()
    for t in range(9):
        v = late.full[128 + t * 96 : 128 + (t + 1) * 96].astype(F32)
        conv_out[t, 0:96] = v[:, 0:64]
        conv_out[t, 96:192] = v[:, 64:128]
    stores[2].start()

    told.wait_send()
    came.wait_send()
    faces.drain()
    back_faces.drain()
    parts.drain()
    for rim in rims:
        rim.drain()
    early.drain()
    late.drain()
    for c in stores:
        c.wait()


def hand_on(*refs):
    given, results, held, sems = refs[:5], refs[5:10], refs[10:15], refs[15]
    takes = [pltpu.make_async_copy(a, b, sems.at[0, i]) for i, (a, b) in enumerate(zip(given, held, strict=True))]
    gives = [pltpu.make_async_copy(a, b, sems.at[1, i]) for i, (a, b) in enumerate(zip(held, results, strict=True))]
    for c in takes:
        c.start()
    for take, give in zip(takes, gives, strict=True):
        take.wait()
        give.start()
    for c in gives:
        c.wait()


def body(vox_feats, block_coords, neighbors, conv_w, conv_b, fold_w, fold_b, map_w, map_b, cotangent):
    far = pl.BlockSpec(memory_space=pl.ANY)
    outs = [
        jax.ShapeDtypeStruct((ROWS, COLS, 128), BF),
        jax.ShapeDtypeStruct((NB, BS, BS, 512), F32),
        jax.ShapeDtypeStruct((9, 192, 64), F32),
        jax.ShapeDtypeStruct((2, 512, 128), F32),
        jax.ShapeDtypeStruct((9, 128, 128), F32),
    ]
    made = pl.pallas_call(
        whole,
        in_specs=[far] * 5 + [VMEM] * 3 + [SMEM] * 2,
        out_specs=[far] * 5,
        out_shape=outs,
        scratch_shapes=[
            *[pltpu.VMEM(o.shape, o.dtype) for o in outs],
            DMA((5,)),
            pltpu.VMEM((NB, BS, BS, 512), BF),
            pltpu.VMEM((27, 64, 64), BF),
            pltpu.VMEM((2, 512, 128), BF),
            pltpu.VMEM((3, 384, 128), BF),
            pltpu.VMEM((ROWS, COLS, 128), BF),
            DMA((5,)),
            pltpu.VMEM((BS, NB, BS, 512), F32),
            pltpu.VMEM((3, 320, 640), F32),
            pltpu.VMEM((2, 8, 640), F32),
            pltpu.VMEM((9, 256, 128), BF),
            pltpu.VMEM((9, 128, 256), BF),
            pltpu.VMEM((320, 1920), BF),
            pltpu.VMEM((256, 512), F32),
            pltpu.VMEM((256, 512), BF),
            pltpu.VMEM((BS, NB, BS, 256), F32),
            pltpu.VMEM((NB, 64, 128), BF),
            pltpu.VMEM((GROUP, 64, 128), BF),
            pltpu.VMEM((8, 128), jnp.int32),
            pltpu.VMEM((NY, 8, 128), jnp.int32),
            pltpu.SMEM((NY, 128), jnp.int32),
            pltpu.SMEM((TR * TC * 2,), jnp.int32),
            pltpu.VMEM((ROWS, COLS, 128), F32),
            pltpu.VMEM((ROWS, COLS, 128), F32),
            pltpu.VMEM((ROWS, COLS, 128), F32),
            pltpu.VMEM(((ROWS + 2) * COLS, 384), BF),
            pltpu.VMEM(((ROWS + 2) * COLS, 384), BF),
            pltpu.VMEM((2, ROWS, 128), F32),
            pltpu.VMEM((TR * TC, 64, 128), BF),
            pltpu.VMEM((GROUP, 64, 128), BF),
            pltpu.VMEM((NY, NB, 64, 128), BF),
            pltpu.VMEM((BS, NB, BS, 256), F32),
            pltpu.VMEM((256, 512), BF),
            pltpu.VMEM((CAT, 128), BF),
            total_scratch(1024),
            total_scratch(512),
            FACE_SCRATCH,
            FACE_SCRATCH,
            STREAM_SEMS,
            DMA((1,)),
            DMA((1,)),
            DMA((1,)),
            pltpu.VMEM((2, 2, COLS, 128), BF),
            pltpu.VMEM((2, 2, ROWS, 128), BF),
            pltpu.VMEM((2, 2, COLS, 128), BF),
            pltpu.VMEM((2, 2, ROWS, 128), BF),
            pltpu.VMEM((2, 4, 16, 128), BF),
            DMA((2, 8)),
            DMA((2, 8)),
            DMA((1,)),
            DMA((1,)),
        ],
        compiler_params=pltpu.CompilerParams(
            collective_id=1, has_side_effects=True, vmem_limit_bytes=58 * 2**20
        ),
    )(
        vox_feats,
        conv_w.reshape(27, 64, 64),
        fold_w.reshape(2, 512, 128),
        map_w.reshape(3, 384, 128),
        cotangent,
        conv_b[None],
        fold_b[None],
        map_b[None],
        block_coords,
        neighbors.T,
    )
    bev_map, feat_grad, conv_grads, fold_grads, map_grads = pl.pallas_call(
        hand_on,
        in_specs=[far] * 5,
        out_specs=[far] * 5,
        out_shape=outs,
        scratch_shapes=[*[pltpu.VMEM(o.shape, o.dtype) for o in outs], DMA((2, 5))],
        compiler_params=pltpu.CompilerParams(vmem_limit_bytes=58 * 2**20),
    )(*made)
    return (
        bev_map,
        feat_grad,
        conv_grads.reshape(3, 3, 3, 64, 64),
        fold_grads.reshape(1024, 128),
        map_grads.reshape(3, 3, 128, 128),
    )


def solution(mesh):
    placed = (
        P(("bx", "by"), None, None, None),
        P(None, ("bx", "by")),
        P(None, ("bx", "by")),
        P(),
        P(),
        P(),
        P(),
        P(),
        P(),
        P("bx", "by", None),
    )
    return jax.shard_map(
        body,
        mesh=mesh,
        in_specs=placed,
        out_specs=(P("bx", "by", None), P(("bx", "by"), None, None, None), P(), P(), P()),
        check_vma=False,
    )
```

```python
import functools

import jax
import jax.numpy as jnp
from jax import lax
from jax.experimental import pallas as pl
from jax.experimental.pallas import tpu as pltpu
from jax.sharding import PartitionSpec as P

MESH = pl.DeviceIdType.MESH
BF = jnp.bfloat16
F32 = jnp.float32
BS = 8
TR = 6
TC = 4
NB = 4
NX = 16
NY = 8
GROUP = NB * NY
ROWS = TR * BS
COLS = TC * BS
VMEM = pl.BlockSpec(memory_space=pltpu.VMEM)
SMEM = pl.BlockSpec(memory_space=pltpu.SMEM)
DMA = pltpu.SemaphoreType.DMA
CAT = 3072


def place():
    return lax.axis_index("bx"), lax.axis_index("by")


def remote(src, dst, send, recv, device):
    return pltpu.make_async_remote_copy(
        src_ref=src,
        dst_ref=dst,
        send_sem=send,
        recv_sem=recv,
        device_id=device,
        device_id_type=MESH,
    )


def signal(device):
    pl.semaphore_signal(
        pltpu.get_barrier_semaphore(), inc=1, device_id=device, device_id_type=MESH
    )


def slope(pre):
    s = jax.nn.sigmoid(pre)
    return s * (1.0 + pre * (1.0 - s))


def rounded(v):
    return v.astype(BF).astype(F32)


def partners():
    bx, by = place()
    core = by % 2
    out = [(None, (bx, (by + k) % NY)) for k in range(1, NY)]
    out += [(None, ((bx + k) % NX, by)) for k in range(1, NX)]
    for step in (-1, 1):
        inside = bx > 0 if step < 0 else bx < NX - 1
        out += [(inside, (bx + step, core + 2 * j)) for j in range(NY // 2)]
        out.append((inside & (by > 0), (bx + step, by - 1)))
        out.append((inside & (by < NY - 1), (bx + step, by + 1)))
    return out


def greet():
    for ok, device in partners():
        if ok is None:
            signal(device)
        else:
            pl.when(ok)(functools.partial(signal, device))


def met():
    count = jnp.int32(0)
    for ok, _ in partners():
        count = count + (1 if ok is None else ok.astype(jnp.int32))
    pl.semaphore_wait(pltpu.get_barrier_semaphore(), count)


def pack_faces(cur, msg, coords):
    lane = lax.broadcasted_iota(jnp.int32, (32, 128), 1)

    def flat(v):
        return jnp.concatenate([v[:, t * 128 : (t + 1) * 128] for t in range(4)], 0)

    def one(n, carry):
        high = coords[2, n].astype(F32)
        msg[n, 0] = flat(cur[0, n]).astype(BF)
        msg[n, 1] = flat(cur[7, n]).astype(BF)
        msg[n, 2] = flat(cur[:, n, 0, :]).astype(BF)
        msg[n, 3] = flat(cur[:, n, 7, :]).astype(BF)
        top = cur[:, n, :, 384:512].reshape(64, 128)
        low = cur[:, n, :, 0:128].reshape(64, 128)
        face = pltpu.roll(top, 64, 1) * (1.0 - high) + low * high
        msg[n, 4] = jnp.where(lane < 64, face[0:32], pltpu.roll(face[32:64], 64, 1)).astype(BF)
        return carry

    lax.fori_loop(0, NB, one, 0, unroll=True)


class Stream:
    def __init__(self, src, pool, step, out_s, in_r, straight=False):
        self.src, self.pool, self.step, self.straight = src, pool, step, straight
        self.out_s, self.in_r = out_s, in_r
        self.bx, self.by = place()
        self.mate = self.by + 1 - 2 * (self.by % 2)
        if step:
            self.kinds = [(6, None), (2, None), (0, None), (4, 0), (4, 1)]
            self.sends = self.bx > 0 if step < 0 else self.bx < NX - 1
            self.takes = self.bx < NX - 1 if step < 0 else self.bx > 0
        elif straight:
            self.kinds = [(4, None), (6, None), (2, None)]
        else:
            self.kinds = [(6, 0), (2, 1), (6, 1), (2, 0), (4, 0), (4, 1)]

    def view(self, origin, half):
        if half is None:
            return self.pool.at[pl.ds(origin * NB, NB)]
        return self.pool.at[pl.ds(origin * NB + half * (NB // 2), NB // 2)]

    def when(self, ok, run):
        if self.step:
            pl.when(ok)(run)
        else:
            run()

    def copy(self, src, origin, half, sem, kind, device):
        got = self.in_r.at[7 if kind is None else self.kinds.index(kind)]
        return remote(src, self.view(origin, half), self.out_s.at[sem], got, device)

    def start(self):
        def run():
            for off, half in self.kinds:
                if off == 4 and not self.straight:
                    continue
                src = self.src if half is None else self.src.at[pl.ds(half * (NB // 2), NB // 2)]
                to = (self.bx + self.step, (self.by + 8 - off) % NY)
                self.copy(src, self.by, half, 0, (off, half), to).start()
            if not self.step:
                self.copy(self.src, self.by, None, 0, None, (self.bx, self.mate)).start()

        self.when(self.sends if self.step else None, run)

    def take(self, far):
        def run():
            for off, half in reversed(self.kinds) if self.straight else self.kinds:
                if (off == 4) != far:
                    continue
                origin = (self.by + off) % NY
                at = self.view(origin, half)
                to_mate = self.copy(at, origin, half, 1, None, (self.bx, self.mate))
                self.copy(at, origin, half, 1, (off, half), (self.bx, self.mate)).wait_recv()
                part = 0 if off == 6 else 1
                if off in (2, 6) and half in (None, part) and not self.straight:
                    piece = self.view(origin, part)
                    to = (self.bx, (self.by + 8 - off) % NY)
                    self.copy(piece, origin, part, 1, (4, part), to).start()
                to_mate.start()

        self.when(self.takes if self.step else None, run)

    def bytes_of(self, messages, sem):
        at = self.pool.at[pl.ds(0, messages * NB)]
        return remote(at, at, self.out_s.at[sem], self.in_r.at[7], (self.bx, self.mate))

    def finish(self):
        self.when(self.takes if self.step else None, lambda: self.bytes_of(4, 1).wait_recv())

    def drain(self):
        self.when(self.sends if self.step else None, lambda: self.bytes_of(4 if self.straight else 3, 0).wait_send())
        passed = 5 if self.step else 3 if self.straight else 4
        self.when(self.takes if self.step else None, lambda: self.bytes_of(passed, 1).wait_send())


STREAM_SEMS = [DMA((2,)), DMA((8,))]


class Faces:
    def __init__(self, msg, pool, side, own, before, after):
        self.msg, self.pool, self.side = msg, pool, side
        self.by = place()[1]
        self.streams = [
            Stream(msg, pool, 0, *own),
            Stream(msg.at[:, 1], side.at[0], 1, *before),
            Stream(msg.at[:, 0], side.at[1], -1, *after),
        ]

    def start(self):
        for x in self.streams:
            x.start()
        self.pool[pl.ds(self.by * NB, NB)] = self.msg[...]

    def forward(self):
        for far in (False, True):
            for x in self.streams:
                x.take(far)

    def finish(self):
        for x in self.streams:
            x.finish()

    def drain(self):
        for x in self.streams:
            x.drain()


FACE_SCRATCH = [
    pltpu.VMEM((NB, 5, 32, 128), BF),
    pltpu.VMEM((GROUP + 1, 5, 32, 128), BF),
    pltpu.VMEM((2, GROUP + 1, 32, 128), BF),
    STREAM_SEMS,
    STREAM_SEMS,
    STREAM_SEMS,
]


def assemble(cur, pool, side, neighbors, shifted, edge):
    low = lax.broadcasted_iota(jnp.int32, (8, 128), 1) < 64
    sub = lax.broadcasted_iota(jnp.int32, (8, 128), 0)

    bx, _ = place()

    def one(n, carry):
        def spot(k, group):
            at = neighbors[n, k]
            from_group = at - group * GROUP
            ok = (at >= 0) & (from_group >= 0) & (from_group < GROUP)
            return jnp.where(ok, from_group, GROUP)

        def face(part, k):
            return pool[spot(k, bx), part].astype(F32)

        def xface(dx, k):
            near = face(1 if dx < 0 else 0, k)
            return near + side[0 if dx < 0 else 1, spot(k, bx + dx)].astype(F32)

        def tiles(v):
            return [v[t * 8 : (t + 1) * 8] for t in range(4)]

        def turn(v):
            return pltpu.roll(v, 64, 1)

        def padz(core, before, after):
            r = [turn(t) for t in core]
            return (
                [jnp.where(low, before, r[0])]
                + [jnp.where(low, r[t - 1], r[t]) for t in (1, 2, 3)]
                + [jnp.where(low, r[3], after)]
            )

        def put(x, t, mid, above, below):
            row = pl.multiple_of((x * NB + n) * 8, 8)
            at = (pl.ds(row, 8), pl.ds(t * 128, 128))
            shifted[(1, *at)] = mid
            shifted[(0, *at)] = jnp.where(sub == 0, above, pltpu.roll(mid, 1, 0))
            shifted[(2, *at)] = jnp.where(sub == 7, below, pltpu.roll(mid, 7, 0))

        for x, dx in ((0, -1), (9, 1)):
            z = []
            for dy in range(3):
                k = 9 * (dx + 1) + 3 * dy
                z.append(
                    padz(tiles(xface(dx, k + 1)), turn(xface(dx, k)[24:32]), turn(xface(dx, k + 2)[0:8]))
                )
            for t in range(5):
                put(x, t, z[1][t], pltpu.roll(z[0][t], 1, 0), pltpu.roll(z[2][t], 7, 0))
        for i, (k, part) in enumerate(((9, 3), (15, 2))):
            z = padz(tiles(face(part, k + 1)), turn(face(part, k)[24:32]), turn(face(part, k + 2)[0:8]))
            for t in range(5):
                edge[i, :, t * 128 : (t + 1) * 128] = z[t]
        under = face(4, 12)
        over = face(4, 14)
        for x in range(BS):
            at = slice(x % 4 * 8, x % 4 * 8 + 8)
            before = under[at] if x < 4 else turn(under[at])
            after = turn(over[at]) if x < 4 else over[at]
            z = padz([cur[x, n, :, t * 128 : (t + 1) * 128] for t in range(4)], before, after)
            for t in range(5):
                lanes = slice(t * 128, (t + 1) * 128)
                put(x + 1, t, z[t], edge[0, x : x + 1, lanes], edge[1, x : x + 1, lanes])
        return carry

    lax.fori_loop(0, NB, one, 0, unroll=True)


NEAR = [(-1, 0), (1, 0), (0, -1), (0, 1), (-1, -1), (-1, 1), (1, -1), (1, 1)]


class Rim:
    def __init__(self, row_out, col_out, row_in, col_in, corner_in, send, recv):
        self.row_out, self.col_out = row_out, col_out
        self.row_in, self.col_in, self.corner_in = row_in, col_in, corner_in
        self.send, self.recv = send, recv
        self.bx, self.by = place()

    def exists(self, d):
        dx, dy = NEAR[d]
        ok = None
        for v, step, size in ((self.bx, dx, NX), (self.by, dy, NY)):
            if step:
                here = v > 0 if step < 0 else v < size - 1
                ok = here if ok is None else ok & here
        return ok

    def copy(self, d):
        dx, dy = NEAR[d]
        back = NEAR.index((-dx, -dy))
        if dy == 0:
            src, dst = self.row_out.at[d], self.row_in.at[back]
        elif dx == 0:
            src, dst = self.col_out.at[d - 2], self.col_in.at[back - 2]
        else:
            src = self.row_out.at[0 if dx < 0 else 1, pl.ds(0 if dy < 0 else 16, 16)]
            dst = self.corner_in.at[back - 4]
        return remote(src, dst, self.send.at[d], self.recv.at[back], (self.bx + dx, self.by + dy))

    def landing(self, d):
        dx, dy = NEAR[d]
        if dy == 0:
            return self.row_in.at[d]
        if dx == 0:
            return self.col_in.at[d - 2]
        return self.corner_in.at[d - 4]

    def start(self, plane):
        self.row_out[0] = plane[0].astype(BF)
        self.row_out[1] = plane[ROWS - 1].astype(BF)
        self.col_out[0] = plane[:, 0, :].astype(BF)
        self.col_out[1] = plane[:, COLS - 1, :].astype(BF)
        for d in range(8):

            @pl.when(self.exists(d))
            def _(d=d):
                self.copy(d).start()

            @pl.when(jnp.logical_not(self.exists(d)))
            def _(d=d):
                at = self.landing(d)
                at[...] = jnp.zeros(at.shape, BF)

    def finish(self):
        for d in range(8):

            @pl.when(self.exists(d))
            def _(d=d):
                dx, dy = NEAR[d]
                at = self.landing(d)
                remote(at, at, self.send.at[d], self.recv.at[d], (self.bx + dx, self.by + dy)).wait_recv()

    def drain(self):
        for d in range(8):

            @pl.when(self.exists(d))
            def _(d=d):
                self.copy(d).wait_send()


def spread(plane, rim, side32, out):
    side32[0] = rim.col_in[0].astype(F32)
    side32[1] = rim.col_in[1].astype(F32)
    j = lax.broadcasted_iota(jnp.int32, (COLS, 128), 0)

    def put(at, row, left, right):
        rows = pl.ds(pl.multiple_of(at * COLS, COLS), COLS)
        out[rows, 0:128] = jnp.where(j == 0, left, pltpu.roll(row, 1, 0)).astype(BF)
        out[rows, 128:256] = row.astype(BF)
        out[rows, 256:384] = jnp.where(j == COLS - 1, right, pltpu.roll(row, COLS - 1, 0)).astype(BF)

    def inner(i, carry):
        put(i + 1, plane[i], side32[0, pl.ds(i, 1), :], side32[1, pl.ds(i, 1), :])
        return carry

    lax.fori_loop(0, ROWS, inner, 0, unroll=16)
    corner = [rim.corner_in[c].astype(F32) for c in range(4)]
    put(0, rim.row_in[0].astype(F32), corner[0][15:16], corner[1][0:1])
    put(ROWS + 1, rim.row_in[1].astype(F32), corner[2][15:16], corner[3][0:1])

class Total:
    def __init__(self, base, half, cat, given, sums, second, ring, full, sems):
        self.base, self.half, self.chunk = base, half, half // NX
        self.cat, self.given, self.sums, self.second = cat, given, sums, second
        self.ring, self.full = ring, full
        self.sems = sems
        self.bx, self.by = place()
        self.core = self.by % 2
        self.mate = self.by + 1 - 2 * self.core
        self.chip = self.by // 2

    def rows(self, core):
        return pl.ds(pl.multiple_of(self.base + core * self.half, self.half), self.half)

    def piece(self, core, i):
        return pl.ds(pl.multiple_of(core * self.half + i * self.chunk, self.chunk), self.chunk)

    def to_mate(self):
        at = self.cat.at[self.rows(1 - self.core)]
        return remote(at, self.given, self.sems.at[0], self.sems.at[1], (self.bx, self.mate))

    def all_of(self, at, stage):
        return remote(at, at, self.sems.at[2 * stage], self.sems.at[2 * stage + 1], (self.bx, self.mate))

    def combine(self):
        self.to_mate().wait_recv()
        self.sums[...] = (self.cat[self.rows(self.core)].astype(F32) + self.given[...].astype(F32)).astype(BF)
        for q in range(NX):

            @pl.when(self.bx != q)
            def _(q=q):
                at = self.sums.at[pl.ds(q * self.chunk, self.chunk)]
                remote(at, self.second.at[self.bx], self.sems.at[2], self.sems.at[3], (q, self.by)).start()

    def sum_x(self):
        self.all_of(self.second.at[pl.ds(0, NX - 1)], 1).wait_recv()
        mine = pl.ds(pl.multiple_of(self.bx * self.chunk, self.chunk), self.chunk)
        total = self.sums[mine].astype(F32)
        for k in range(1, NX):
            total = total + self.second[(self.bx + k) % NX].astype(F32)
        self.ring[self.chip] = total.astype(BF)
        at = self.ring.at[self.chip]
        for k in (1, 3, 2):
            to = (self.bx, (self.by + 2 * k) % NY)
            remote(at, at, self.sems.at[4], self.sems.at[5], to).start()

    def sum_ring(self):
        self.all_of(self.ring.at[pl.ds(0, 3)], 2).wait_recv()
        total = self.ring[0].astype(F32)
        for i in range(1, 4):
            total = total + self.ring[i].astype(F32)
        self.full[self.piece(self.core, self.bx)] = total.astype(BF)
        at = self.full.at[self.piece(self.core, self.bx)]
        for k in range(1, NX):
            remote(at, at, self.sems.at[6], self.sems.at[7], ((self.bx + k) % NX, self.by)).start()

    def share(self):
        at = self.full.at[pl.ds(pl.multiple_of(self.core * self.half, self.half), self.half)]
        return remote(at, at, self.sems.at[8], self.sems.at[9], (self.bx, self.mate))

    def relay(self):
        self.all_of(self.full.at[pl.ds(0, (NX - 1) * self.chunk)], 3).wait_recv()
        self.share().start()

    def done(self):
        self.share().wait_recv()

    def drain(self):
        self.to_mate().wait_send()
        self.all_of(self.second.at[pl.ds(0, NX - 1)], 1).wait_send()
        self.all_of(self.ring.at[pl.ds(0, 3)], 2).wait_send()
        self.all_of(self.full.at[pl.ds(0, (NX - 1) * self.chunk)], 3).wait_send()
        self.share().wait_send()


def total_scratch(half):
    chunk = half // NX
    return [
        pltpu.VMEM((half, 128), BF),
        pltpu.VMEM((half, 128), BF),
        pltpu.VMEM((NX, chunk, 128), BF),
        pltpu.VMEM((4, chunk, 128), BF),
        pltpu.VMEM((2 * half, 128), BF),
        DMA((10,)),
    ]


def dot(a, b):
    return jnp.dot(a, b, preferred_element_type=F32)


def dot_t(a, b):
    return lax.dot_general(a, b, (((1,), (1,)), ((), ())), preferred_element_type=F32)


def window(wide, a, e, g):
    return wide[a * 32 : a * 32 + 256, e * 640 + g * 128 : e * 640 + g * 128 + 256]


def whole(
    vox_h, conv_w_h, fold_w_h, map_w_h, cot_h, conv_b, fold_b, map_b, coords, neighbors,
    bev_far, feat_far, early_far, late_far,
    bev_out, feat_out, out_sem,
    vox, conv_w, fold_w, map_w, cot, load_sem,
    cur, shifted, edge, toep, toep_back, wide, pre, act, fold_both, part, part_pool,
    code, codes_v, codes, table,
    fold, plane, gplane, spread_mid, spread_grad, side32, slots, ready, back,
    split, cur_bf, cat, early_part, late_part,
    face_a, face_f, part_sems, code_s, code_r, code_l,
    row_out, col_out, row_in, col_in, corner_in, rim_s, rim_r, back_s, back_r,
):
    bx, by = place()
    greet()
    stores = [
        pltpu.make_async_copy(src, dst, out_sem.at[i])
        for i, (src, dst) in enumerate(
            (
                (bev_out, bev_far),
                (feat_out, feat_far),
                (early_part[4], early_far),
                (late_part[4], late_far),
            )
        )
    ]
    early = Total(0, 1024, cat, *early_part)
    late = Total(2048, 512, cat, *late_part)
    core = by % 2
    loads = [
        pltpu.make_async_copy(src, dst, load_sem.at[i])
        for i, (src, dst) in enumerate(
            ((vox_h, vox), (conv_w_h, conv_w), (fold_w_h, fold_w), (map_w_h, map_w), (cot_h, cot))
        )
    ]
    for c in loads:
        c.start()
    lane = lax.broadcasted_iota(jnp.int32, (8, 128), 1)
    tile = jnp.zeros((8, 128), jnp.int32)
    for n in range(NB):
        number = ((coords[0, n] - bx * TR) * (TC * NY) + coords[1, n]) * 2 + coords[2, n]
        tile = jnp.where(lane == n, number, tile)
    code[...] = tile
    codes_v[by] = tile
    loads[0].wait()
    for n in range(NB):
        cur[:, n] = vox[n].astype(F32)
    faces = Faces(*face_a)
    pack_faces(cur, faces.msg, coords)
    met()
    tell = [
        remote(code, codes_v.at[by], code_s.at[0], code_r.at[0], (bx, (by + k) % NY)) for k in range(1, NY)
    ]
    for c in tell:
        c.start()
    faces.start()
    back_faces = Faces(*face_f)
    for f in (faces, back_faces):
        f.pool[GROUP] = jnp.zeros((5, 32, 128), BF)
        for to in range(2):
            f.side[to, GROUP] = jnp.zeros((32, 128), BF)
    loads[1].wait()
    blank = jnp.zeros((64, 64), F32)

    def build(tap, carry):
        w = [conv_w[tap * 3 + k].astype(F32) for k in range(3)]
        ahead = [blank, *w, blank]
        for z in range(4):
            toep[tap, z * 64 : (z + 1) * 64, :] = jnp.concatenate([ahead[z + 1], ahead[z]], 1).astype(BF)
        rows = ((w[2], w[1], w[0], blank), (blank, w[2], w[1], w[0]))
        for z in range(2):
            for half in range(2):
                pair = jnp.concatenate(rows[z][half * 2 : half * 2 + 2], 1)
                toep_back[tap, z * 64 : (z + 1) * 64, half * 128 : (half + 1) * 128] = pair.astype(BF)
        return carry

    lax.fori_loop(0, 9, build, 0)
    others = codes_v.at[pl.ds(0, NY - 1)]
    told = remote(others, others, code_s.at[0], code_r.at[0], (bx, (by + 1) % NY))
    told.wait_recv()
    to_scalar = pltpu.make_async_copy(codes_v.at[:, 0], codes, code_l.at[0])
    to_scalar.start()
    to_scalar.wait()

    def look(s, carry):
        want = ((s // (TC * 2)) * (TC * NY) + by * TC + (s // 2) % TC) * 2 + s % 2
        found = jnp.int32(GROUP)
        for b in range(GROUP):
            found = jnp.where(codes[b // NB, b % NB] == want, b, found)
        table[s] = found
        return carry

    lax.fori_loop(0, TR * TC * 2, look, 0)
    faces.forward()
    loads[3].wait()
    faces.finish()
    assemble(cur, faces.pool, faces.side, neighbors, shifted, edge)
    for e in range(3):
        wide[:, e * 640 : (e + 1) * 640] = shifted[e].astype(BF)
    for group in range(4):
        total = jnp.concatenate([conv_b[...], conv_b[...]], 1)
        for a in range(3):
            for e in range(3):
                total = total + dot(window(wide, a, e, group), toep[a * 3 + e])
        lanes = slice(group * 128, (group + 1) * 128)
        pre[:, lanes] = total
        act[:, lanes] = (total * jax.nn.sigmoid(total)).astype(BF)
    loads[2].wait()
    for h in range(2):
        fold_both[:, :, :, h * 128 : (h + 1) * 128] = dot(act[...], fold_w[h]).reshape(BS, NB, BS, 128)
    for n in range(NB):
        high = coords[2, n].astype(F32)
        one = fold_both[:, n, :, 0:128] * (1.0 - high) + fold_both[:, n, :, 128:256] * high
        part[n] = one.reshape(64, 128).astype(BF)
    parts = Stream(part, part_pool, 0, *part_sems, straight=True)
    parts.start()
    part_pool[pl.ds(by * NB, NB)] = part[...]
    loads[4].wait()
    parts.take(False)
    parts.take(True)
    parts.finish()

    def fill_slot(r, c):
        total = fold_b[...]
        for h in range(2):
            at = table[(r * TC + c) * 2 + h]
            here = (at < GROUP).astype(F32)
            total = total + part_pool[jnp.minimum(at, GROUP - 1)].astype(F32) * here
        where = (slice(r * BS, (r + 1) * BS), slice(c * BS, (c + 1) * BS))
        fold[where] = total.reshape(BS, BS, 128)
        plane[where] = rounded(total * jax.nn.sigmoid(total)).reshape(BS, BS, 128)

    rims = [
        Rim(row_out.at[p], col_out.at[p], row_in.at[p], col_in.at[p], corner_in.at[p], rim_s.at[p], rim_r.at[p])
        for p in range(2)
    ]
    for r in range(TR):
        for c in range(TC):
            fill_slot(r, c)
    rims[0].start(plane)
    rims[0].finish()
    spread(plane, rims[0], side32, spread_mid)

    def ahead(i, carry):
        start = pl.multiple_of(i * 256, 256)
        total = map_b[...]
        for a in range(3):
            total = total + dot(spread_mid[pl.ds(start + a * COLS, 256), :], map_w[a])
        bev_out[pl.ds(i * BS, BS)] = (total * jax.nn.sigmoid(total)).reshape(BS, COLS, 128).astype(BF)
        g = cot[pl.ds(i * BS, BS)].astype(F32).reshape(256, 128) * slope(total)
        gplane[pl.ds(i * BS, BS)] = rounded(g).reshape(BS, COLS, 128)
        return carry

    lax.fori_loop(0, TR, ahead, 0, unroll=True)
    stores[0].start()
    rims[1].start(gplane)
    turned = gplane[...].reshape(ROWS * COLS, 128).T.astype(BF)
    for a in range(3):
        got = dot(turned, spread_mid[a * COLS : a * COLS + ROWS * COLS, :])
        for e in range(3):
            t = a * 3 + e
            row = t * 128 if t < 8 else 2048
            cat[row : row + 128] = got[:, e * 128 : (e + 1) * 128].T.astype(BF)


    @pl.when(core == 1)
    def _():
        early.to_mate().start()

    rims[1].finish()
    spread(gplane, rims[1], side32, spread_grad)

    def behind(i, carry):
        start = pl.multiple_of(i * 256, 256)
        total = None
        for a in range(3):
            for e in range(3):
                lhs = spread_grad[pl.ds(start + a * COLS, 256), e * 128 : (e + 1) * 128]
                one = dot_t(lhs, map_w[2 - a, (2 - e) * 128 : (3 - e) * 128, :])
                total = one if total is None else total + one
        grad = (total * slope(fold[pl.ds(i * BS, BS)].reshape(256, 128))).reshape(BS, COLS, 128)
        for c in range(TC):
            slots[i * TC + c] = grad[:, c * BS : (c + 1) * BS, :].reshape(64, 128).astype(BF)
        return carry

    lax.fori_loop(0, TR, behind, 0, unroll=True)

    def fill(b, carry):
        number = codes[b // NB, b % NB] // 2
        c = number % (TC * NY) - by * TC
        at = number // (TC * NY) * TC + jnp.clip(c, 0, TC - 1)
        ready[b] = slots[jnp.clip(at, 0, TR * TC - 1)]
        return carry

    lax.fori_loop(0, GROUP, fill, 0, unroll=True)
    give = [
        remote(
            ready.at[pl.ds((by + k) % NY * NB, NB)],
            back.at[by],
            back_s.at[0],
            back_r.at[0],
            (bx, (by + k) % NY),
        )
        for k in (4, 3, 5, 2, 6, 1, 7)
    ]
    for c in give:
        c.start()
    back[by] = ready[pl.ds(by * NB, NB)]
    pl.when(core == 0)(early.combine)
    others = back.at[pl.ds(0, NY - 1)]
    came = remote(others, others, back_s.at[0], back_r.at[0], (bx, (by + 1) % NY))
    came.wait_recv()

    for n in range(NB):
        high = coords[2, n].astype(F32)
        mine = back[jnp.clip(coords[1, n] // TC, 0, NY - 1), n].astype(F32).reshape(BS, BS, 128)
        split[:, n, :, 0:128] = mine * (1.0 - high)
        split[:, n, :, 128:256] = mine * high
    both = split[...].reshape(256, 256)
    act_grad = None
    for h in range(2):
        one = dot_t(both[:, h * 128 : (h + 1) * 128].astype(BF), fold_w[h])
        act_grad = one if act_grad is None else act_grad + one
    grad = rounded(rounded(act_grad) * slope(pre[...]))
    cur[...] = grad.reshape(BS, NB, BS, 512)
    cur_bf[...] = grad.astype(BF)
    pack_faces(cur, back_faces.msg, coords)
    back_faces.start()
    got = dot(both.T.astype(BF), act[...])
    for h in range(2):
        cat[1024 + h * 512 : 1024 + (h + 1) * 512] = got[h * 128 : (h + 1) * 128].T.astype(BF)

    @pl.when(core == 0)
    def _():
        early.to_mate().start()

    turned = [cur_bf[:, g * 128 : (g + 1) * 128].astype(F32).T.astype(BF) for g in range(4)]
    low = lax.broadcasted_iota(jnp.int32, (96, 128), 1) < 64
    for a in range(3):
        for e in range(3):
            total = None
            for g in range(4):
                one = dot(turned[g], window(wide, a, e, g))
                total = one if total is None else total + one
            total = total.T
            summed_z = total[0:192] + pltpu.roll(total[64:256], 64, 1)
            row = 2176 + (a * 3 + e) * 96
            cat[row : row + 96] = jnp.where(
                low, summed_z[0:96], pltpu.roll(summed_z[96:192], 64, 1)
            ).astype(BF)
    cat[3040:3072] = jnp.zeros((32, 128), BF)
    late.to_mate().start()
    pl.when(core == 1)(early.combine)
    late.combine()
    early.sum_x()
    for x in back_faces.streams:
        x.take(False)
    late.sum_x()
    early.sum_ring()
    for x in back_faces.streams:
        x.take(True)
    late.sum_ring()
    back_faces.finish()
    assemble(cur, back_faces.pool, back_faces.side, neighbors, shifted, edge)
    for e in range(3):
        wide[:, e * 640 : (e + 1) * 640] = shifted[e].astype(BF)
    for g in range(4):
        total = None
        for a in range(3):
            for e in range(3):
                one = dot_t(window(wide, a, e, g), toep_back[(2 - a) * 3 + 2 - e])
                total = one if total is None else total + one
        view = total.reshape(BS, NB, BS, 128)
        for n in range(NB):
            feat_out[n, :, :, g * 128 : (g + 1) * 128] = view[:, n]
    stores[1].start()
    early.relay()
    late.relay()
    early.done()
    stores[2].start()
    late.done()
    stores[3].start()

    told.wait_send()
    came.wait_send()
    faces.drain()
    back_faces.drain()
    parts.drain()
    for rim in rims:
        rim.drain()
    early.drain()
    late.drain()
    for c in stores:
        c.wait()


def hand_on(
    bev_in, feat_in, early_in, late_in, bev_far, feat_far, conv_far, fold_far, map_far,
    bev, feat, early, late, conv, fold, grads, sems,
):
    takes = [
        pltpu.make_async_copy(a, b, sems.at[0, i])
        for i, (a, b) in enumerate(((early_in, early), (late_in, late), (bev_in, bev), (feat_in, feat)))
    ]
    for c in takes:
        c.start()
    gives = [
        pltpu.make_async_copy(a, b, sems.at[1, i])
        for i, (a, b) in enumerate(
            ((grads, map_far), (fold, fold_far), (conv, conv_far), (bev, bev_far), (feat, feat_far))
        )
    ]
    takes[2].wait()
    gives[3].start()
    takes[3].wait()
    gives[4].start()
    takes[0].wait()
    for h in range(2):
        fold[h] = early[1024 + h * 512 : 1024 + (h + 1) * 512].astype(F32)
    gives[1].start()
    for t in range(8):
        grads[t] = early[t * 128 : (t + 1) * 128].astype(F32)
    takes[1].wait()
    grads[8] = late[0:128].astype(F32)
    gives[0].start()
    for t in range(9):
        v = late[128 + t * 96 : 128 + (t + 1) * 96].astype(F32)
        conv[t, 0:96] = v[:, 0:64]
        conv[t, 96:192] = v[:, 64:128]
    gives[2].start()
    for c in gives:
        c.wait()


def body(vox_feats, block_coords, neighbors, conv_w, conv_b, fold_w, fold_b, map_w, map_b, cotangent):
    far = pl.BlockSpec(memory_space=pl.ANY)
    outs = [
        jax.ShapeDtypeStruct((ROWS, COLS, 128), BF),
        jax.ShapeDtypeStruct((NB, BS, BS, 512), F32),
        jax.ShapeDtypeStruct((9, 192, 64), F32),
        jax.ShapeDtypeStruct((2, 512, 128), F32),
        jax.ShapeDtypeStruct((9, 128, 128), F32),
    ]
    between = outs[:2] + [jax.ShapeDtypeStruct((2048, 128), BF), jax.ShapeDtypeStruct((1024, 128), BF)]
    made = pl.pallas_call(
        whole,
        in_specs=[far] * 5 + [VMEM] * 3 + [SMEM] * 2,
        out_specs=[far] * 4,
        out_shape=between,
        scratch_shapes=[
            *[pltpu.VMEM(o.shape, o.dtype) for o in outs[:2]],
            DMA((4,)),
            pltpu.VMEM((NB, BS, BS, 512), BF),
            pltpu.VMEM((27, 64, 64), BF),
            pltpu.VMEM((2, 512, 128), BF),
            pltpu.VMEM((3, 384, 128), BF),
            pltpu.VMEM((ROWS, COLS, 128), BF),
            DMA((5,)),
            pltpu.VMEM((BS, NB, BS, 512), F32),
            pltpu.VMEM((3, 320, 640), F32),
            pltpu.VMEM((2, 8, 640), F32),
            pltpu.VMEM((9, 256, 128), BF),
            pltpu.VMEM((9, 128, 256), BF),
            pltpu.VMEM((320, 1920), BF),
            pltpu.VMEM((256, 512), F32),
            pltpu.VMEM((256, 512), BF),
            pltpu.VMEM((BS, NB, BS, 256), F32),
            pltpu.VMEM((NB, 64, 128), BF),
            pltpu.VMEM((GROUP, 64, 128), BF),
            pltpu.VMEM((8, 128), jnp.int32),
            pltpu.VMEM((NY, 8, 128), jnp.int32),
            pltpu.SMEM((NY, 128), jnp.int32),
            pltpu.SMEM((TR * TC * 2,), jnp.int32),
            pltpu.VMEM((ROWS, COLS, 128), F32),
            pltpu.VMEM((ROWS, COLS, 128), F32),
            pltpu.VMEM((ROWS, COLS, 128), F32),
            pltpu.VMEM(((ROWS + 2) * COLS, 384), BF),
            pltpu.VMEM(((ROWS + 2) * COLS, 384), BF),
            pltpu.VMEM((2, ROWS, 128), F32),
            pltpu.VMEM((TR * TC, 64, 128), BF),
            pltpu.VMEM((GROUP, 64, 128), BF),
            pltpu.VMEM((NY, NB, 64, 128), BF),
            pltpu.VMEM((BS, NB, BS, 256), F32),
            pltpu.VMEM((256, 512), BF),
            pltpu.VMEM((CAT, 128), BF),
            total_scratch(1024),
            total_scratch(512),
            FACE_SCRATCH,
            FACE_SCRATCH,
            STREAM_SEMS,
            DMA((1,)),
            DMA((1,)),
            DMA((1,)),
            pltpu.VMEM((2, 2, COLS, 128), BF),
            pltpu.VMEM((2, 2, ROWS, 128), BF),
            pltpu.VMEM((2, 2, COLS, 128), BF),
            pltpu.VMEM((2, 2, ROWS, 128), BF),
            pltpu.VMEM((2, 4, 16, 128), BF),
            DMA((2, 8)),
            DMA((2, 8)),
            DMA((1,)),
            DMA((1,)),
        ],
        compiler_params=pltpu.CompilerParams(
            collective_id=1, has_side_effects=True, vmem_limit_bytes=58 * 2**20
        ),
    )(
        vox_feats,
        conv_w.reshape(27, 64, 64),
        fold_w.reshape(2, 512, 128),
        map_w.reshape(3, 384, 128),
        cotangent,
        conv_b[None],
        fold_b[None],
        map_b[None],
        block_coords,
        neighbors.T,
    )
    bev_map, feat_grad, conv_grads, fold_grads, map_grads = pl.pallas_call(
        hand_on,
        in_specs=[far] * 4,
        out_specs=[far] * 5,
        out_shape=outs,
        scratch_shapes=[*[pltpu.VMEM(o.shape, o.dtype) for o in between + outs[2:]], DMA((2, 5))],
        compiler_params=pltpu.CompilerParams(vmem_limit_bytes=58 * 2**20),
    )(*made)
    return (
        bev_map,
        feat_grad,
        conv_grads.reshape(3, 3, 3, 64, 64),
        fold_grads.reshape(1024, 128),
        map_grads.reshape(3, 3, 128, 128),
    )


def solution(mesh):
    placed = (
        P(("bx", "by"), None, None, None),
        P(None, ("bx", "by")),
        P(None, ("bx", "by")),
        P(),
        P(),
        P(),
        P(),
        P(),
        P(),
        P("bx", "by", None),
    )
    return jax.shard_map(
        body,
        mesh=mesh,
        in_specs=placed,
        out_specs=(P("bx", "by", None), P(("bx", "by"), None, None, None), P(), P(), P()),
        check_vma=False,
    )
```

```python
import functools

import jax
import jax.numpy as jnp
from jax import lax
from jax.experimental import pallas as pl
from jax.experimental.pallas import tpu as pltpu
from jax.sharding import PartitionSpec as P

MESH = pl.DeviceIdType.MESH
BF = jnp.bfloat16
F32 = jnp.float32
BS = 8
TR = 6
TC = 4
NB = 4
NX = 16
NY = 8
GROUP = NB * NY
ROWS = TR * BS
COLS = TC * BS
VMEM = pl.BlockSpec(memory_space=pltpu.VMEM)
SMEM = pl.BlockSpec(memory_space=pltpu.SMEM)
DMA = pltpu.SemaphoreType.DMA
CAT = 3072


def place():
    return lax.axis_index("bx"), lax.axis_index("by")


def remote(src, dst, send, recv, device):
    return pltpu.make_async_remote_copy(
        src_ref=src,
        dst_ref=dst,
        send_sem=send,
        recv_sem=recv,
        device_id=device,
        device_id_type=MESH,
    )


def signal(device):
    pl.semaphore_signal(
        pltpu.get_barrier_semaphore(), inc=1, device_id=device, device_id_type=MESH
    )


def slope(pre):
    s = jax.nn.sigmoid(pre)
    return s * (1.0 + pre * (1.0 - s))


def rounded(v):
    return v.astype(BF).astype(F32)


def partners():
    bx, by = place()
    core = by % 2
    out = [(None, (bx, (by + k) % NY)) for k in range(1, NY)]
    out += [(None, ((bx + k) % NX, by)) for k in range(1, NX)]
    for step in (-1, 1):
        inside = bx > 0 if step < 0 else bx < NX - 1
        out += [(inside, (bx + step, core + 2 * j)) for j in range(NY // 2)]
        out.append((inside & (by > 0), (bx + step, by - 1)))
        out.append((inside & (by < NY - 1), (bx + step, by + 1)))
    return out


def greet():
    for ok, device in partners():
        if ok is None:
            signal(device)
        else:
            pl.when(ok)(functools.partial(signal, device))


def met():
    count = jnp.int32(0)
    for ok, _ in partners():
        count = count + (1 if ok is None else ok.astype(jnp.int32))
    pl.semaphore_wait(pltpu.get_barrier_semaphore(), count)


def pack_faces(cur, msg, coords):
    lane = lax.broadcasted_iota(jnp.int32, (32, 128), 1)

    def flat(v):
        return jnp.concatenate([v[:, t * 128 : (t + 1) * 128] for t in range(4)], 0)

    def one(n, carry):
        high = coords[2, n].astype(F32)
        msg[n, 0] = flat(cur[0, n]).astype(BF)
        msg[n, 1] = flat(cur[7, n]).astype(BF)
        msg[n, 2] = flat(cur[:, n, 0, :]).astype(BF)
        msg[n, 3] = flat(cur[:, n, 7, :]).astype(BF)
        top = cur[:, n, :, 384:512].reshape(64, 128)
        low = cur[:, n, :, 0:128].reshape(64, 128)
        face = pltpu.roll(top, 64, 1) * (1.0 - high) + low * high
        msg[n, 4] = jnp.where(lane < 64, face[0:32], pltpu.roll(face[32:64], 64, 1)).astype(BF)
        return carry

    lax.fori_loop(0, NB, one, 0, unroll=True)


class Stream:
    def __init__(self, src, pool, step, out_s, in_r, straight=False):
        self.src, self.pool, self.step, self.straight = src, pool, step, straight
        self.out_s, self.in_r = out_s, in_r
        self.bx, self.by = place()
        self.mate = self.by + 1 - 2 * (self.by % 2)
        if step:
            self.kinds = [(6, None), (2, None), (0, None), (4, 0), (4, 1)]
            self.sends = self.bx > 0 if step < 0 else self.bx < NX - 1
            self.takes = self.bx < NX - 1 if step < 0 else self.bx > 0
        elif straight:
            self.kinds = [(4, None), (6, None), (2, None)]
        else:
            self.kinds = [(6, 0), (2, 1), (6, 1), (2, 0), (4, 0), (4, 1)]

    def view(self, origin, half):
        if half is None:
            return self.pool.at[pl.ds(origin * NB, NB)]
        return self.pool.at[pl.ds(origin * NB + half * (NB // 2), NB // 2)]

    def when(self, ok, run):
        if self.step:
            pl.when(ok)(run)
        else:
            run()

    def copy(self, src, origin, half, sem, kind, device):
        got = self.in_r.at[7 if kind is None else self.kinds.index(kind)]
        return remote(src, self.view(origin, half), self.out_s.at[sem], got, device)

    def start(self):
        def run():
            for off, half in self.kinds:
                if off == 4 and not self.straight:
                    continue
                src = self.src if half is None else self.src.at[pl.ds(half * (NB // 2), NB // 2)]
                to = (self.bx + self.step, (self.by + 8 - off) % NY)
                self.copy(src, self.by, half, 0, (off, half), to).start()
            if not self.step:
                self.copy(self.src, self.by, None, 0, None, (self.bx, self.mate)).start()

        self.when(self.sends if self.step else None, run)

    def take(self, far):
        def run():
            for off, half in reversed(self.kinds) if self.straight else self.kinds:
                if (off == 4) != far:
                    continue
                origin = (self.by + off) % NY
                at = self.view(origin, half)
                to_mate = self.copy(at, origin, half, 1, None, (self.bx, self.mate))
                self.copy(at, origin, half, 1, (off, half), (self.bx, self.mate)).wait_recv()
                part = 0 if off == 6 else 1
                if off in (2, 6) and half in (None, part) and not self.straight:
                    piece = self.view(origin, part)
                    to = (self.bx, (self.by + 8 - off) % NY)
                    self.copy(piece, origin, part, 1, (4, part), to).start()
                to_mate.start()

        self.when(self.takes if self.step else None, run)

    def bytes_of(self, messages, sem):
        at = self.pool.at[pl.ds(0, messages * NB)]
        return remote(at, at, self.out_s.at[sem], self.in_r.at[7], (self.bx, self.mate))

    def finish(self):
        self.when(self.takes if self.step else None, lambda: self.bytes_of(4, 1).wait_recv())

    def drain(self):
        self.when(self.sends if self.step else None, lambda: self.bytes_of(4 if self.straight else 3, 0).wait_send())
        passed = 5 if self.step else 3 if self.straight else 4
        self.when(self.takes if self.step else None, lambda: self.bytes_of(passed, 1).wait_send())


STREAM_SEMS = [DMA((2,)), DMA((8,))]


class Faces:
    def __init__(self, msg, pool, side, own, before, after):
        self.msg, self.pool, self.side = msg, pool, side
        self.by = place()[1]
        self.streams = [
            Stream(msg, pool, 0, *own),
            Stream(msg.at[:, 1], side.at[0], 1, *before),
            Stream(msg.at[:, 0], side.at[1], -1, *after),
        ]

    def start(self):
        for x in self.streams:
            x.start()
        self.pool[pl.ds(self.by * NB, NB)] = self.msg[...]

    def forward(self):
        for far in (False, True):
            for x in self.streams:
                x.take(far)

    def finish(self):
        for x in self.streams:
            x.finish()

    def drain(self):
        for x in self.streams:
            x.drain()


FACE_SCRATCH = [
    pltpu.VMEM((NB, 5, 32, 128), BF),
    pltpu.VMEM((GROUP + 1, 5, 32, 128), BF),
    pltpu.VMEM((2, GROUP + 1, 32, 128), BF),
    STREAM_SEMS,
    STREAM_SEMS,
    STREAM_SEMS,
]


def assemble(cur, pool, side, neighbors, shifted, edge):
    low = lax.broadcasted_iota(jnp.int32, (8, 128), 1) < 64
    sub = lax.broadcasted_iota(jnp.int32, (8, 128), 0)

    bx, _ = place()

    def one(n, carry):
        def spot(k, group):
            at = neighbors[n, k]
            from_group = at - group * GROUP
            ok = (at >= 0) & (from_group >= 0) & (from_group < GROUP)
            return jnp.where(ok, from_group, GROUP)

        def face(part, k):
            return pool[spot(k, bx), part].astype(F32)

        def xface(dx, k):
            near = face(1 if dx < 0 else 0, k)
            return near + side[0 if dx < 0 else 1, spot(k, bx + dx)].astype(F32)

        def tiles(v):
            return [v[t * 8 : (t + 1) * 8] for t in range(4)]

        def turn(v):
            return pltpu.roll(v, 64, 1)

        def padz(core, before, after):
            r = [turn(t) for t in core]
            return (
                [jnp.where(low, before, r[0])]
                + [jnp.where(low, r[t - 1], r[t]) for t in (1, 2, 3)]
                + [jnp.where(low, r[3], after)]
            )

        def put(x, t, mid, above, below):
            row = pl.multiple_of((x * NB + n) * 8, 8)
            at = (pl.ds(row, 8), pl.ds(t * 128, 128))
            shifted[(1, *at)] = mid
            shifted[(0, *at)] = jnp.where(sub == 0, above, pltpu.roll(mid, 1, 0))
            shifted[(2, *at)] = jnp.where(sub == 7, below, pltpu.roll(mid, 7, 0))

        for x, dx in ((0, -1), (9, 1)):
            z = []
            for dy in range(3):
                k = 9 * (dx + 1) + 3 * dy
                z.append(
                    padz(tiles(xface(dx, k + 1)), turn(xface(dx, k)[24:32]), turn(xface(dx, k + 2)[0:8]))
                )
            for t in range(5):
                put(x, t, z[1][t], pltpu.roll(z[0][t], 1, 0), pltpu.roll(z[2][t], 7, 0))
        for i, (k, part) in enumerate(((9, 3), (15, 2))):
            z = padz(tiles(face(part, k + 1)), turn(face(part, k)[24:32]), turn(face(part, k + 2)[0:8]))
            for t in range(5):
                edge[i, :, t * 128 : (t + 1) * 128] = z[t]
        under = face(4, 12)
        over = face(4, 14)
        for x in range(BS):
            at = slice(x % 4 * 8, x % 4 * 8 + 8)
            before = under[at] if x < 4 else turn(under[at])
            after = turn(over[at]) if x < 4 else over[at]
            z = padz([cur[x, n, :, t * 128 : (t + 1) * 128] for t in range(4)], before, after)
            for t in range(5):
                lanes = slice(t * 128, (t + 1) * 128)
                put(x + 1, t, z[t], edge[0, x : x + 1, lanes], edge[1, x : x + 1, lanes])
        return carry

    lax.fori_loop(0, NB, one, 0, unroll=True)


NEAR = [(-1, 0), (1, 0), (0, -1), (0, 1), (-1, -1), (-1, 1), (1, -1), (1, 1)]


class Rim:
    def __init__(self, row_out, col_out, row_in, col_in, corner_in, send, recv):
        self.row_out, self.col_out = row_out, col_out
        self.row_in, self.col_in, self.corner_in = row_in, col_in, corner_in
        self.send, self.recv = send, recv
        self.bx, self.by = place()

    def exists(self, d):
        dx, dy = NEAR[d]
        ok = None
        for v, step, size in ((self.bx, dx, NX), (self.by, dy, NY)):
            if step:
                here = v > 0 if step < 0 else v < size - 1
                ok = here if ok is None else ok & here
        return ok

    def copy(self, d):
        dx, dy = NEAR[d]
        back = NEAR.index((-dx, -dy))
        if dy == 0:
            src, dst = self.row_out.at[d], self.row_in.at[back]
        elif dx == 0:
            src, dst = self.col_out.at[d - 2], self.col_in.at[back - 2]
        else:
            src = self.row_out.at[0 if dx < 0 else 1, pl.ds(0 if dy < 0 else 16, 16)]
            dst = self.corner_in.at[back - 4]
        return remote(src, dst, self.send.at[d], self.recv.at[back], (self.bx + dx, self.by + dy))

    def landing(self, d):
        dx, dy = NEAR[d]
        if dy == 0:
            return self.row_in.at[d]
        if dx == 0:
            return self.col_in.at[d - 2]
        return self.corner_in.at[d - 4]

    def start(self, plane):
        self.row_out[0] = plane[0].astype(BF)
        self.row_out[1] = plane[ROWS - 1].astype(BF)
        self.col_out[0] = plane[:, 0, :].astype(BF)
        self.col_out[1] = plane[:, COLS - 1, :].astype(BF)
        for d in range(8):

            @pl.when(self.exists(d))
            def _(d=d):
                self.copy(d).start()

            @pl.when(jnp.logical_not(self.exists(d)))
            def _(d=d):
                at = self.landing(d)
                at[...] = jnp.zeros(at.shape, BF)

    def finish(self):
        for d in range(8):

            @pl.when(self.exists(d))
            def _(d=d):
                dx, dy = NEAR[d]
                at = self.landing(d)
                remote(at, at, self.send.at[d], self.recv.at[d], (self.bx + dx, self.by + dy)).wait_recv()

    def drain(self):
        for d in range(8):

            @pl.when(self.exists(d))
            def _(d=d):
                self.copy(d).wait_send()


def spread(plane, rim, side32, out):
    side32[0] = rim.col_in[0].astype(F32)
    side32[1] = rim.col_in[1].astype(F32)
    j = lax.broadcasted_iota(jnp.int32, (COLS, 128), 0)

    def put(at, row, left, right):
        rows = pl.ds(pl.multiple_of(at * COLS, COLS), COLS)
        out[rows, 0:128] = jnp.where(j == 0, left, pltpu.roll(row, 1, 0)).astype(BF)
        out[rows, 128:256] = row.astype(BF)
        out[rows, 256:384] = jnp.where(j == COLS - 1, right, pltpu.roll(row, COLS - 1, 0)).astype(BF)

    def inner(i, carry):
        put(i + 1, plane[i], side32[0, pl.ds(i, 1), :], side32[1, pl.ds(i, 1), :])
        return carry

    lax.fori_loop(0, ROWS, inner, 0, unroll=16)
    corner = [rim.corner_in[c].astype(F32) for c in range(4)]
    put(0, rim.row_in[0].astype(F32), corner[0][15:16], corner[1][0:1])
    put(ROWS + 1, rim.row_in[1].astype(F32), corner[2][15:16], corner[3][0:1])

class Total:
    def __init__(self, base, half, cat, given, sums, second, ring, full, sems):
        self.base, self.half, self.chunk = base, half, half // NX
        self.cat, self.given, self.sums, self.second = cat, given, sums, second
        self.ring, self.full = ring, full
        self.sems = sems
        self.bx, self.by = place()
        self.core = self.by % 2
        self.mate = self.by + 1 - 2 * self.core
        self.chip = self.by // 2

    def rows(self, core):
        return pl.ds(pl.multiple_of(self.base + core * self.half, self.half), self.half)

    def piece(self, core, i):
        return pl.ds(pl.multiple_of(core * self.half + i * self.chunk, self.chunk), self.chunk)

    def to_mate(self):
        at = self.cat.at[self.rows(1 - self.core)]
        return remote(at, self.given, self.sems.at[0], self.sems.at[1], (self.bx, self.mate))

    def all_of(self, at, stage):
        return remote(at, at, self.sems.at[2 * stage], self.sems.at[2 * stage + 1], (self.bx, self.mate))

    def combine(self):
        self.to_mate().wait_recv()
        self.sums[...] = (self.cat[self.rows(self.core)].astype(F32) + self.given[...].astype(F32)).astype(BF)
        for q in range(NX):

            @pl.when(self.bx != q)
            def _(q=q):
                at = self.sums.at[pl.ds(q * self.chunk, self.chunk)]
                remote(at, self.second.at[self.bx], self.sems.at[2], self.sems.at[3], (q, self.by)).start()

    def sum_x(self):
        self.all_of(self.second.at[pl.ds(0, NX - 1)], 1).wait_recv()
        mine = pl.ds(pl.multiple_of(self.bx * self.chunk, self.chunk), self.chunk)
        total = self.sums[mine].astype(F32)
        for k in range(1, NX):
            total = total + self.second[(self.bx + k) % NX].astype(F32)
        self.ring[self.chip] = total.astype(BF)
        at = self.ring.at[self.chip]
        for k in (1, 3, 2):
            to = (self.bx, (self.by + 2 * k) % NY)
            remote(at, at, self.sems.at[4], self.sems.at[5], to).start()

    def sum_ring(self):
        self.all_of(self.ring.at[pl.ds(0, 3)], 2).wait_recv()
        total = self.ring[0].astype(F32)
        for i in range(1, 4):
            total = total + self.ring[i].astype(F32)
        self.full[self.piece(self.core, self.bx)] = total.astype(BF)
        at = self.full.at[self.piece(self.core, self.bx)]
        for k in range(1, NX):
            remote(at, at, self.sems.at[6], self.sems.at[7], ((self.bx + k) % NX, self.by)).start()

    def share(self):
        at = self.full.at[pl.ds(pl.multiple_of(self.core * self.half, self.half), self.half)]
        return remote(at, at, self.sems.at[8], self.sems.at[9], (self.bx, self.mate))

    def relay(self):
        self.all_of(self.full.at[pl.ds(0, (NX - 1) * self.chunk)], 3).wait_recv()
        self.share().start()

    def done(self):
        self.share().wait_recv()

    def drain(self):
        self.to_mate().wait_send()
        self.all_of(self.second.at[pl.ds(0, NX - 1)], 1).wait_send()
        self.all_of(self.ring.at[pl.ds(0, 3)], 2).wait_send()
        self.all_of(self.full.at[pl.ds(0, (NX - 1) * self.chunk)], 3).wait_send()
        self.share().wait_send()


def total_scratch(half):
    chunk = half // NX
    return [
        pltpu.VMEM((half, 128), BF),
        pltpu.VMEM((half, 128), BF),
        pltpu.VMEM((NX, chunk, 128), BF),
        pltpu.VMEM((4, chunk, 128), BF),
        pltpu.VMEM((2 * half, 128), BF),
        DMA((10,)),
    ]


def dot(a, b):
    return jnp.dot(a, b, preferred_element_type=F32)


def dot_t(a, b):
    return lax.dot_general(a, b, (((1,), (1,)), ((), ())), preferred_element_type=F32)


def window(wide, a, e, g):
    return wide[a * 32 : a * 32 + 256, e * 640 + g * 128 : e * 640 + g * 128 + 256]


def whole(
    vox_h, conv_w_h, fold_w_h, map_w_h, cot_h, conv_b, fold_b, map_b, coords, neighbors,
    bev_far, feat_far, early_far, late_far,
    bev_out, feat_out, out_sem,
    vox, conv_w, fold_w, map_w, cot, load_sem,
    cur, shifted, edge, toep, toep_back, wide, pre, act, fold_both, part, part_pool,
    code, codes_v, codes, table,
    fold, plane, gplane, spread_mid, spread_grad, side32, slots, ready, back,
    split, cur_bf, cat, early_part, late_part,
    face_a, face_f, part_sems, code_s, code_r, code_l,
    row_out, col_out, row_in, col_in, corner_in, rim_s, rim_r, back_s, back_r,
):
    bx, by = place()
    greet()
    stores = [
        pltpu.make_async_copy(src, dst, out_sem.at[i])
        for i, (src, dst) in enumerate(
            (
                (bev_out, bev_far),
                (feat_out, feat_far),
                (early_part[4], early_far),
                (late_part[4], late_far),
            )
        )
    ]
    early = Total(0, 1024, cat, *early_part)
    late = Total(2048, 512, cat, *late_part)
    core = by % 2
    loads = [
        pltpu.make_async_copy(src, dst, load_sem.at[i])
        for i, (src, dst) in enumerate(
            ((vox_h, vox), (conv_w_h, conv_w), (fold_w_h, fold_w), (map_w_h, map_w), (cot_h, cot))
        )
    ]
    for c in loads:
        c.start()
    lane = lax.broadcasted_iota(jnp.int32, (8, 128), 1)
    tile = jnp.zeros((8, 128), jnp.int32)
    for n in range(NB):
        number = ((coords[0, n] - bx * TR) * (TC * NY) + coords[1, n]) * 2 + coords[2, n]
        tile = jnp.where(lane == n, number, tile)
    code[...] = tile
    codes_v[by] = tile
    loads[0].wait()
    for n in range(NB):
        cur[:, n] = vox[n].astype(F32)
    faces = Faces(*face_a)
    pack_faces(cur, faces.msg, coords)
    met()
    tell = [
        remote(code, codes_v.at[by], code_s.at[0], code_r.at[0], (bx, (by + k) % NY)) for k in range(1, NY)
    ]
    for c in tell:
        c.start()
    faces.start()
    back_faces = Faces(*face_f)
    for f in (faces, back_faces):
        f.pool[GROUP] = jnp.zeros((5, 32, 128), BF)
        for to in range(2):
            f.side[to, GROUP] = jnp.zeros((32, 128), BF)
    loads[1].wait()
    blank = jnp.zeros((64, 64), F32)

    def build(tap, carry):
        w = [conv_w[tap * 3 + k].astype(F32) for k in range(3)]
        ahead = [blank, *w, blank]
        for z in range(4):
            toep[tap, z * 64 : (z + 1) * 64, :] = jnp.concatenate([ahead[z + 1], ahead[z]], 1).astype(BF)
        rows = ((w[2], w[1], w[0], blank), (blank, w[2], w[1], w[0]))
        for z in range(2):
            for half in range(2):
                pair = jnp.concatenate(rows[z][half * 2 : half * 2 + 2], 1)
                toep_back[tap, z * 64 : (z + 1) * 64, half * 128 : (half + 1) * 128] = pair.astype(BF)
        return carry

    lax.fori_loop(0, 9, build, 0)
    others = codes_v.at[pl.ds(0, NY - 1)]
    told = remote(others, others, code_s.at[0], code_r.at[0], (bx, (by + 1) % NY))
    told.wait_recv()
    to_scalar = pltpu.make_async_copy(codes_v.at[:, 0], codes, code_l.at[0])
    to_scalar.start()
    to_scalar.wait()

    def look(s, carry):
        want = ((s // (TC * 2)) * (TC * NY) + by * TC + (s // 2) % TC) * 2 + s % 2
        found = jnp.int32(GROUP)
        for b in range(GROUP):
            found = jnp.where(codes[b // NB, b % NB] == want, b, found)
        table[s] = found
        return carry

    lax.fori_loop(0, TR * TC * 2, look, 0)
    faces.forward()
    loads[3].wait()
    faces.finish()
    assemble(cur, faces.pool, faces.side, neighbors, shifted, edge)
    for e in range(3):
        wide[:, e * 640 : (e + 1) * 640] = shifted[e].astype(BF)
    for group in range(4):
        total = jnp.concatenate([conv_b[...], conv_b[...]], 1)
        for a in range(3):
            for e in range(3):
                total = total + dot(window(wide, a, e, group), toep[a * 3 + e])
        lanes = slice(group * 128, (group + 1) * 128)
        pre[:, lanes] = total
        act[:, lanes] = (total * jax.nn.sigmoid(total)).astype(BF)
    loads[2].wait()
    for h in range(2):
        fold_both[:, :, :, h * 128 : (h + 1) * 128] = dot(act[...], fold_w[h]).reshape(BS, NB, BS, 128)
    for n in range(NB):
        high = coords[2, n].astype(F32)
        one = fold_both[:, n, :, 0:128] * (1.0 - high) + fold_both[:, n, :, 128:256] * high
        part[n] = one.reshape(64, 128).astype(BF)
    parts = Stream(part, part_pool, 0, *part_sems, straight=True)
    parts.start()
    part_pool[pl.ds(by * NB, NB)] = part[...]
    loads[4].wait()
    parts.take(False)
    parts.take(True)
    parts.finish()

    def fill_slot(r, c):
        total = fold_b[...]
        for h in range(2):
            at = table[(r * TC + c) * 2 + h]
            here = (at < GROUP).astype(F32)
            total = total + part_pool[jnp.minimum(at, GROUP - 1)].astype(F32) * here
        where = (slice(r * BS, (r + 1) * BS), slice(c * BS, (c + 1) * BS))
        fold[where] = total.reshape(BS, BS, 128)
        plane[where] = rounded(total * jax.nn.sigmoid(total)).reshape(BS, BS, 128)

    rims = [
        Rim(row_out.at[p], col_out.at[p], row_in.at[p], col_in.at[p], corner_in.at[p], rim_s.at[p], rim_r.at[p])
        for p in range(2)
    ]
    for r in range(TR):
        for c in range(TC):
            fill_slot(r, c)
    rims[0].start(plane)
    rims[0].finish()
    spread(plane, rims[0], side32, spread_mid)

    def ahead(i, carry):
        start = pl.multiple_of(i * 256, 256)
        total = map_b[...]
        for a in range(3):
            total = total + dot(spread_mid[pl.ds(start + a * COLS, 256), :], map_w[a])
        bev_out[pl.ds(i * BS, BS)] = (total * jax.nn.sigmoid(total)).reshape(BS, COLS, 128).astype(BF)
        g = cot[pl.ds(i * BS, BS)].astype(F32).reshape(256, 128) * slope(total)
        gplane[pl.ds(i * BS, BS)] = rounded(g).reshape(BS, COLS, 128)
        return carry

    lax.fori_loop(0, TR, ahead, 0, unroll=True)
    stores[0].start()
    rims[1].start(gplane)
    turned = gplane[...].reshape(ROWS * COLS, 128).T.astype(BF)
    for a in range(3):
        got = dot(turned, spread_mid[a * COLS : a * COLS + ROWS * COLS, :])
        for e in range(3):
            t = a * 3 + e
            row = t * 128 if t < 8 else 2048
            cat[row : row + 128] = got[:, e * 128 : (e + 1) * 128].T.astype(BF)


    @pl.when(core == 1)
    def _():
        early.to_mate().start()

    rims[1].finish()
    spread(gplane, rims[1], side32, spread_grad)

    def behind(i, carry):
        start = pl.multiple_of(i * 256, 256)
        total = None
        for a in range(3):
            for e in range(3):
                lhs = spread_grad[pl.ds(start + a * COLS, 256), e * 128 : (e + 1) * 128]
                one = dot_t(lhs, map_w[2 - a, (2 - e) * 128 : (3 - e) * 128, :])
                total = one if total is None else total + one
        grad = (total * slope(fold[pl.ds(i * BS, BS)].reshape(256, 128))).reshape(BS, COLS, 128)
        for c in range(TC):
            slots[i * TC + c] = grad[:, c * BS : (c + 1) * BS, :].reshape(64, 128).astype(BF)
        return carry

    lax.fori_loop(0, TR, behind, 0, unroll=True)

    def fill(b, carry):
        number = codes[b // NB, b % NB] // 2
        c = number % (TC * NY) - by * TC
        at = number // (TC * NY) * TC + jnp.clip(c, 0, TC - 1)
        ready[b] = slots[jnp.clip(at, 0, TR * TC - 1)]
        return carry

    lax.fori_loop(0, GROUP, fill, 0, unroll=True)
    give = [
        remote(
            ready.at[pl.ds((by + k) % NY * NB, NB)],
            back.at[by],
            back_s.at[0],
            back_r.at[0],
            (bx, (by + k) % NY),
        )
        for k in (4, 3, 5, 2, 6, 1, 7)
    ]
    for c in give:
        c.start()
    back[by] = ready[pl.ds(by * NB, NB)]
    pl.when(core == 0)(early.combine)
    others = back.at[pl.ds(0, NY - 1)]
    came = remote(others, others, back_s.at[0], back_r.at[0], (bx, (by + 1) % NY))
    came.wait_recv()

    for n in range(NB):
        high = coords[2, n].astype(F32)
        mine = back[jnp.clip(coords[1, n] // TC, 0, NY - 1), n].astype(F32).reshape(BS, BS, 128)
        split[:, n, :, 0:128] = mine * (1.0 - high)
        split[:, n, :, 128:256] = mine * high
    both = split[...].reshape(256, 256)
    act_grad = None
    for h in range(2):
        one = dot_t(both[:, h * 128 : (h + 1) * 128].astype(BF), fold_w[h])
        act_grad = one if act_grad is None else act_grad + one
    grad = rounded(rounded(act_grad) * slope(pre[...]))
    cur[...] = grad.reshape(BS, NB, BS, 512)
    cur_bf[...] = grad.astype(BF)
    pack_faces(cur, back_faces.msg, coords)
    back_faces.start()
    got = dot(both.T.astype(BF), act[...])
    for h in range(2):
        cat[1024 + h * 512 : 1024 + (h + 1) * 512] = got[h * 128 : (h + 1) * 128].T.astype(BF)

    @pl.when(core == 0)
    def _():
        early.to_mate().start()

    turned = [cur_bf[:, g * 128 : (g + 1) * 128].astype(F32).T.astype(BF) for g in range(4)]
    low = lax.broadcasted_iota(jnp.int32, (96, 128), 1) < 64
    for a in range(3):
        for e in range(3):
            total = None
            for g in range(4):
                one = dot(turned[g], window(wide, a, e, g))
                total = one if total is None else total + one
            total = total.T
            summed_z = total[0:192] + pltpu.roll(total[64:256], 64, 1)
            row = 2176 + (a * 3 + e) * 96
            cat[row : row + 96] = jnp.where(
                low, summed_z[0:96], pltpu.roll(summed_z[96:192], 64, 1)
            ).astype(BF)
    cat[3040:3072] = jnp.zeros((32, 128), BF)
    late.to_mate().start()
    pl.when(core == 1)(early.combine)
    late.combine()
    early.sum_x()
    for x in back_faces.streams:
        x.take(False)
    late.sum_x()
    early.sum_ring()
    for x in back_faces.streams:
        x.take(True)
    late.sum_ring()
    back_faces.finish()
    assemble(cur, back_faces.pool, back_faces.side, neighbors, shifted, edge)
    early.relay()
    for e in range(3):
        wide[:, e * 640 : (e + 1) * 640] = shifted[e].astype(BF)
    for g in range(4):
        total = None
        for a in range(3):
            for e in range(3):
                one = dot_t(window(wide, a, e, g), toep_back[(2 - a) * 3 + 2 - e])
                total = one if total is None else total + one
        view = total.reshape(BS, NB, BS, 128)
        for n in range(NB):
            feat_out[n, :, :, g * 128 : (g + 1) * 128] = view[:, n]
    stores[1].start()
    late.relay()
    early.done()
    stores[2].start()
    late.done()
    stores[3].start()

    told.wait_send()
    came.wait_send()
    faces.drain()
    back_faces.drain()
    parts.drain()
    for rim in rims:
        rim.drain()
    early.drain()
    late.drain()
    for c in stores:
        c.wait()


def hand_on(
    bev_in, feat_in, early_in, late_in, bev_far, feat_far, conv_far, fold_far, map_far,
    bev, feat, early, late, conv, fold, grads, sems,
):
    takes = [
        pltpu.make_async_copy(a, b, sems.at[0, i])
        for i, (a, b) in enumerate(((feat_in, feat), (bev_in, bev), (early_in, early), (late_in, late)))
    ]
    for c in takes:
        c.start()
    gives = [
        pltpu.make_async_copy(a, b, sems.at[1, i])
        for i, (a, b) in enumerate(
            ((grads, map_far), (fold, fold_far), (conv, conv_far), (bev, bev_far), (feat, feat_far))
        )
    ]
    takes[0].wait()
    gives[4].start()
    takes[1].wait()
    gives[3].start()
    takes[2].wait()
    for h in range(2):
        fold[h] = early[1024 + h * 512 : 1024 + (h + 1) * 512].astype(F32)
    gives[1].start()
    for t in range(8):
        grads[t] = early[t * 128 : (t + 1) * 128].astype(F32)
    takes[3].wait()
    grads[8] = late[0:128].astype(F32)
    gives[0].start()
    for t in range(9):
        v = late[128 + t * 96 : 128 + (t + 1) * 96].astype(F32)
        conv[t, 0:96] = v[:, 0:64]
        conv[t, 96:192] = v[:, 64:128]
    gives[2].start()
    for c in gives:
        c.wait()


def body(vox_feats, block_coords, neighbors, conv_w, conv_b, fold_w, fold_b, map_w, map_b, cotangent):
    far = pl.BlockSpec(memory_space=pl.ANY)
    outs = [
        jax.ShapeDtypeStruct((ROWS, COLS, 128), BF),
        jax.ShapeDtypeStruct((NB, BS, BS, 512), F32),
        jax.ShapeDtypeStruct((9, 192, 64), F32),
        jax.ShapeDtypeStruct((2, 512, 128), F32),
        jax.ShapeDtypeStruct((9, 128, 128), F32),
    ]
    between = outs[:2] + [jax.ShapeDtypeStruct((2048, 128), BF), jax.ShapeDtypeStruct((1024, 128), BF)]
    made = pl.pallas_call(
        whole,
        in_specs=[far] * 5 + [VMEM] * 3 + [SMEM] * 2,
        out_specs=[far] * 4,
        out_shape=between,
        scratch_shapes=[
            *[pltpu.VMEM(o.shape, o.dtype) for o in outs[:2]],
            DMA((4,)),
            pltpu.VMEM((NB, BS, BS, 512), BF),
            pltpu.VMEM((27, 64, 64), BF),
            pltpu.VMEM((2, 512, 128), BF),
            pltpu.VMEM((3, 384, 128), BF),
            pltpu.VMEM((ROWS, COLS, 128), BF),
            DMA((5,)),
            pltpu.VMEM((BS, NB, BS, 512), F32),
            pltpu.VMEM((3, 320, 640), F32),
            pltpu.VMEM((2, 8, 640), F32),
            pltpu.VMEM((9, 256, 128), BF),
            pltpu.VMEM((9, 128, 256), BF),
            pltpu.VMEM((320, 1920), BF),
            pltpu.VMEM((256, 512), F32),
            pltpu.VMEM((256, 512), BF),
            pltpu.VMEM((BS, NB, BS, 256), F32),
            pltpu.VMEM((NB, 64, 128), BF),
            pltpu.VMEM((GROUP, 64, 128), BF),
            pltpu.VMEM((8, 128), jnp.int32),
            pltpu.VMEM((NY, 8, 128), jnp.int32),
            pltpu.SMEM((NY, 128), jnp.int32),
            pltpu.SMEM((TR * TC * 2,), jnp.int32),
            pltpu.VMEM((ROWS, COLS, 128), F32),
            pltpu.VMEM((ROWS, COLS, 128), F32),
            pltpu.VMEM((ROWS, COLS, 128), F32),
            pltpu.VMEM(((ROWS + 2) * COLS, 384), BF),
            pltpu.VMEM(((ROWS + 2) * COLS, 384), BF),
            pltpu.VMEM((2, ROWS, 128), F32),
            pltpu.VMEM((TR * TC, 64, 128), BF),
            pltpu.VMEM((GROUP, 64, 128), BF),
            pltpu.VMEM((NY, NB, 64, 128), BF),
            pltpu.VMEM((BS, NB, BS, 256), F32),
            pltpu.VMEM((256, 512), BF),
            pltpu.VMEM((CAT, 128), BF),
            total_scratch(1024),
            total_scratch(512),
            FACE_SCRATCH,
            FACE_SCRATCH,
            STREAM_SEMS,
            DMA((1,)),
            DMA((1,)),
            DMA((1,)),
            pltpu.VMEM((2, 2, COLS, 128), BF),
            pltpu.VMEM((2, 2, ROWS, 128), BF),
            pltpu.VMEM((2, 2, COLS, 128), BF),
            pltpu.VMEM((2, 2, ROWS, 128), BF),
            pltpu.VMEM((2, 4, 16, 128), BF),
            DMA((2, 8)),
            DMA((2, 8)),
            DMA((1,)),
            DMA((1,)),
        ],
        compiler_params=pltpu.CompilerParams(
            collective_id=1, has_side_effects=True, vmem_limit_bytes=58 * 2**20
        ),
    )(
        vox_feats,
        conv_w.reshape(27, 64, 64),
        fold_w.reshape(2, 512, 128),
        map_w.reshape(3, 384, 128),
        cotangent,
        conv_b[None],
        fold_b[None],
        map_b[None],
        block_coords,
        neighbors.T,
    )
    bev_map, feat_grad, conv_grads, fold_grads, map_grads = pl.pallas_call(
        hand_on,
        in_specs=[far] * 4,
        out_specs=[far] * 5,
        out_shape=outs,
        scratch_shapes=[*[pltpu.VMEM(o.shape, o.dtype) for o in between + outs[2:]], DMA((2, 5))],
        compiler_params=pltpu.CompilerParams(vmem_limit_bytes=58 * 2**20),
    )(*made)
    return (
        bev_map,
        feat_grad,
        conv_grads.reshape(3, 3, 3, 64, 64),
        fold_grads.reshape(1024, 128),
        map_grads.reshape(3, 3, 128, 128),
    )


def solution(mesh):
    placed = (
        P(("bx", "by"), None, None, None),
        P(None, ("bx", "by")),
        P(None, ("bx", "by")),
        P(),
        P(),
        P(),
        P(),
        P(),
        P(),
        P("bx", "by", None),
    )
    return jax.shard_map(
        body,
        mesh=mesh,
        in_specs=placed,
        out_specs=(P("bx", "by", None), P(("bx", "by"), None, None, None), P(), P(), P()),
        check_vma=False,
    )
```
